32 devices in a mesh: dev: 32 (over z, y, x, core).
Axes of the slice: x: 2, y: 2, z: 4, core: 2. Of those that a mesh axis runs over, the one named last changes fastest.
Arguments:
- hidden_in: bfloat16 [2, 2048, 1280], P(None, 'dev'), may hold values from -6 to 6
- clip_lengths: int32 [2, 3], replicated, may hold values from 1 to 1024, 2048 in all within a row
- ln1_gain: bfloat16 [1280], P('dev'), may hold values from 0.5 to 1.5
- ln1_bias: bfloat16 [1280], P('dev'), may hold values from -1.75 to 1.75
- w_query: bfloat16 [1280, 1280], P('dev'), may hold values from -0.15625 to 0.15625
- b_query: bfloat16 [1280], P('dev'), may hold values from -3 to 3
- w_key: bfloat16 [1280, 1280], P('dev'), may hold values from -0.15625 to 0.15625
- w_value: bfloat16 [1280, 1280], P('dev'), may hold values from -0.15625 to 0.15625
- b_value: bfloat16 [1280], P('dev'), may hold values from -3 to 3
- w_out: bfloat16 [1280, 1280], P('dev'), may hold values from -1 to 1
- b_out: bfloat16 [1280], P('dev'), may hold values from -3 to 3
- ln2_gain: bfloat16 [1280], P('dev'), may hold values from 0.5 to 1.5
- ln2_bias: bfloat16 [1280], P('dev'), may hold values from -1.75 to 1.75
- w_fc1: bfloat16 [1280, 5120], P('dev'), may hold values from -0.15625 to 0.15625
- b_fc1: bfloat16 [5120], P('dev'), may hold values from -3 to 3
- w_fc2: bfloat16 [5120, 1280], P('dev'), may hold values from -0.078125 to 0.078125
- b_fc2: bfloat16 [1280], P('dev'), may hold values from -3 to 3
- cotangent: bfloat16 [2, 2048, 1280], P(None, 'dev'), may hold values from -6 to 6
Outputs:
- layer_out: float32 [2, 2048, 1280], P(None, 'dev')
- input_grad: float32 [2, 2048, 1280], P(None, 'dev')
- grad_ln1_gain: float32 [1280], P('dev')
- grad_ln1_bias: float32 [1280], P('dev')
- grad_w_query: float32 [1280, 1280], P('dev')
- grad_b_query: float32 [1280], P('dev')
- grad_w_key: float32 [1280, 1280], P('dev')
- grad_w_value: float32 [1280, 1280], P('dev')
- grad_b_value: float32 [1280], P('dev')
- grad_w_out: float32 [1280, 1280], P('dev')
- grad_b_out: float32 [1280], P('dev')
- grad_ln2_gain: float32 [1280], P('dev')
- grad_ln2_bias: float32 [1280], P('dev')
- grad_w_fc1: float32 [1280, 5120], P('dev')
- grad_b_fc1: float32 [5120], P('dev')
- grad_w_fc2: float32 [5120, 1280], P('dev')
- grad_b_fc2: float32 [1280], P('dev')
The draws below stay inside these ranges and needn't reach their ends.
Inputs may be any that keep to these rules, and one draw needn't show every extreme that they name: `clip_lengths`: in each micro-batch the 3 lengths sum to 2048, and some clip has exactly 1024 frames.
All inputs are finite; a program needn't handle non-finite values.
Results may differ from the reference program's by a relative error of at most 0.013.
Values may be sent and summed in bfloat16 or wider, within the bound.
No kernel may reach another device: no remote copies, remote signals or barrier semaphores. Data moves between devices by JAX's collectives and lax.ppermute only.
A program may use at most 448 MiB of HBM per device.

```python
import math
import jax
import jax.numpy as jnp
import numpy as np
from jax import lax

D = 1280
HEADS = 16
HD = 80
FF = 5120
TOK_DEV = 64
MB = 2
MAXLEN = 1024
TOKENS = 2048
NCLIP = 3
REACH = 16


def block_scale(key, shape, pieces, smallest, top_value):
    level = 1.0
    for axis_at, blocks in pieces:
        steps = jax.random.uniform(jax.random.fold_in(jax.random.fold_in(key, 6), axis_at), (blocks,), jnp.float32, smallest / len(pieces), top_value / len(pieces))
        level = level * jnp.repeat(jnp.exp(steps), shape[axis_at] // blocks).reshape((-1,) + (1,) * (len(shape) - 1 - axis_at))
    return level


def length_profile(amount, total, bound, slope):
    loads = [(1 << 20) // math.isqrt(standing ** slope) + 1 for standing in range(2, amount + 1)]
    surplus, holding = total - bound - (amount - 1), [1] * (amount - 1)
    while surplus > 0:
        candidates = [i for i in range(amount - 1) if holding[i] < bound]
        whole, remaining = sum([loads[i] for i in candidates]), surplus
        for i in candidates:
            extra = min(bound - holding[i], max(1, remaining * loads[i] // whole), surplus)
            holding[i] = holding[i] + extra
            surplus = surplus - extra
    return np.array([bound] + holding)


def ragged_sizes(stream_key, number_of, total, bound, skew):
    if number_of == 2:
        one = jax.random.randint(stream_key, (), max(1, total - bound), min(bound, total - 1) + 1)
        return jnp.stack([one, total - one])
    tallies = jnp.asarray(length_profile(number_of, total, bound, skew), jnp.int32)
    twos = (number_of - 1) // 2
    donor, receiver = tallies[1:1 + 2 * twos:2], tallies[2:2 + 2 * twos:2]
    margin = jnp.minimum(donor - 1, bound - receiver)
    moved = jax.random.randint(jax.random.fold_in(stream_key, 1), (twos,), 0, 1 << 20) % (margin + 1)
    tallies = tallies.at[1:1 + 2 * twos:2].set(donor - moved).at[2:2 + 2 * twos:2].set(receiver + moved)
    return tallies[jax.random.permutation(jax.random.fold_in(stream_key, 2), number_of)]


def scatter_about(rng, dims, spread, reach, cuts=(), kind=jnp.bfloat16):
    factor_of = block_scale(rng, dims, cuts, -0.22, 0.18) if cuts else 1.0
    values = jax.random.normal(rng, dims, jnp.float32) * spread * factor_of
    return jnp.minimum(jnp.maximum(values, -reach), reach).astype(kind)


def setup_inputs(seed: int = 0) -> dict:
    key_list = jax.random.split(jax.random.key(seed), 19)
    return {
        "hidden_in": scatter_about(key_list[0], (MB, TOKENS, D), 1.0, 6.0, ((1, 32),)),
        "clip_lengths": jax.vmap(lambda own: ragged_sizes(own, NCLIP, TOKENS, MAXLEN, 1))(jax.random.split(key_list[1], MB)).reshape((MB, NCLIP)).astype(jnp.int32),
        "ln1_gain": jnp.clip(1.0 + 0.1 * jax.random.normal(key_list[2], (D,), jnp.float32), 0.5, 1.5).astype(jnp.bfloat16),
        "ln1_bias": scatter_about(key_list[3], (D,), 0.3, 1.75, ((0, 32),)),
        "w_query": scatter_about(key_list[4], (D, D), D ** -0.5, 0.15625, ((0, 32),)),
        "b_query": scatter_about(key_list[5], (D,), 0.5, 3.0, ((0, 32),)),
        "w_key": scatter_about(key_list[6], (D, D), D ** -0.5, 0.15625, ((0, 32),)),
        "w_value": scatter_about(key_list[7], (D, D), D ** -0.5, 0.15625, ((0, 32),)),
        "b_value": scatter_about(key_list[8], (D,), 0.5, 3.0, ((0, 32),)),
        "w_out": scatter_about(key_list[9], (D, D), (D // 32) ** -0.5, 1.0, ((0, 32),)),
        "b_out": scatter_about(key_list[10], (D,), 0.5, 3.0, ((0, 32),)),
        "ln2_gain": jnp.clip(1.0 + 0.1 * jax.random.normal(key_list[11], (D,), jnp.float32), 0.5, 1.5).astype(jnp.bfloat16),
        "ln2_bias": scatter_about(key_list[12], (D,), 0.3, 1.75, ((0, 32),)),
        "w_fc1": scatter_about(key_list[13], (D, FF), D ** -0.5, 0.15625, ((0, 32),)),
        "b_fc1": scatter_about(key_list[14], (FF,), 0.5, 3.0, ((0, 32),)),
        "w_fc2": scatter_about(key_list[15], (FF, D), FF ** -0.5, 0.078125, ((0, 32),)),
        "b_fc2": scatter_about(key_list[16], (D,), 0.5, 3.0, ((0, 32),)),
        "cotangent": scatter_about(key_list[17], (MB, TOKENS, D), 1.0, 6.0, ((1, 32),)),
    }


@jax.custom_vjp
def low(v):
    return lax.optimization_barrier(v.astype(jnp.bfloat16)).astype(jnp.float32)

@jax.custom_vjp
def low_back(v):
    return v

def low_keep(v):
    return (low(v), None)

def low_pass(kept, grad):
    return (grad,)

def back_keep(v):
    return (v, None)

def back_low(kept, grad):
    return (low(grad),)
low.defvjp(low_keep, low_pass)
low_back.defvjp(back_keep, back_low)
eps = 1e-05

def layer_norm(v, gain, shift):
    mean = lax.optimization_barrier(jnp.mean(v, axis=-1, keepdims=True))
    cent = v - mean
    var = lax.optimization_barrier(jnp.mean(cent * cent, axis=-1, keepdims=True))
    return cent * lax.rsqrt(var + eps) * gain + shift

def matmul(a, b):
    return jnp.dot(a, b, precision=lax.Precision.HIGHEST)

def clip_index(lengths):
    ends = jnp.cumsum(lengths).astype(jnp.int32)
    where_at = jnp.arange(TOKENS, dtype=jnp.int32)
    return lax.optimization_barrier(jnp.sum((ends[None, :] <= where_at[:, None]).astype(jnp.int32), axis=1)).astype(jnp.int32)

def forward(x, params, clip):
    g1, b1, wq, bq, wk, wv, bv, wo, bo, g2, b2, w1, c1, w2, c2 = params
    a1 = low(layer_norm(x, g1, b1))
    q = low(low_back(matmul(a1, wq) + bq))
    k = low(low_back(matmul(a1, wk)))
    v = low(low_back(matmul(a1, wv) + bv))
    span = REACH * TOK_DEV
    keys_all = (2 * REACH + 1) * TOK_DEV
    k_pad = jnp.pad(k, ((span, span), (0, 0)))
    v_pad = jnp.pad(v, ((span, span), (0, 0)))
    clip_pad = jnp.concatenate([jnp.full((span,), -1, jnp.int32), clip, jnp.full((span,), -1, jnp.int32)])
    scale = 1.0 / HD ** 0.5

    def block(index):
        start = (index * TOK_DEV).astype(jnp.int32)
        q_rows = lax.dynamic_slice_in_dim(q, start, TOK_DEV, 0).reshape(TOK_DEV, HEADS, HD)
        k_rows = lax.dynamic_slice_in_dim(k_pad, start, keys_all, 0).reshape(keys_all, HEADS, HD)
        v_rows = lax.dynamic_slice_in_dim(v_pad, start, keys_all, 0).reshape(keys_all, HEADS, HD)
        q_clip = lax.dynamic_slice_in_dim(clip, start, TOK_DEV, 0)
        k_clip = lax.dynamic_slice_in_dim(clip_pad, start, keys_all, 0)
        scores = low_back(jnp.einsum('qhd,khd->hqk', q_rows, k_rows, precision=lax.Precision.HIGHEST)) * scale
        same = (q_clip[:, None] == k_clip[None, :])[None]
        scores = jnp.where(same, scores, -1e+30)
        top = lax.optimization_barrier(jnp.max(scores, axis=-1, keepdims=True))
        expo = jnp.exp(scores - top)
        probs = expo / lax.optimization_barrier(jnp.sum(expo, axis=-1, keepdims=True))
        out = jnp.einsum('hqk,khd->qhd', low(probs), v_rows, precision=lax.Precision.HIGHEST)
        return out.reshape(TOK_DEV, D)
    blocks = jnp.arange(TOKENS // TOK_DEV, dtype=jnp.int32)
    att = lax.map(jax.checkpoint(block), blocks).reshape(TOKENS, D)
    att = low(low_back(att))
    rows_blk = 4096 if TOKENS % 4096 == 0 else TOKENS

    def tail(pair):
        x_blk, o_blk = pair
        x2 = x_blk + low_back(matmul(o_blk, wo) + bo)
        a2 = low(layer_norm(x2, g2, b2))
        u = low_back(matmul(a2, w1) + c1)
        hid = low(jax.nn.gelu(u, approximate=False))
        return x2 + low_back(matmul(hid, w2) + c2)
    count = TOKENS // rows_blk
    out = lax.map(jax.checkpoint(tail), (x.reshape(count, rows_blk, D), att.reshape(count, rows_blk, D)))
    return out.reshape(TOKENS, D)

def reference(hidden_in, clip_lengths, ln1_gain, ln1_bias, w_query, b_query, w_key, w_value, b_value, w_out, b_out, ln2_gain, ln2_bias, w_fc1, b_fc1, w_fc2, b_fc2, cotangent):
    params = tuple((p.astype(jnp.float32) for p in (ln1_gain, ln1_bias, w_query, b_query, w_key, w_value, b_value, w_out, b_out, ln2_gain, ln2_bias, w_fc1, b_fc1, w_fc2, b_fc2)))
    outputs = []
    in_grads = []
    totals = None
    for micro in range(MB):
        x = hidden_in[micro].astype(jnp.float32)
        clip = clip_index(clip_lengths[micro])
        value, pull = jax.vjp(lambda xx, pp: forward(xx, pp, clip), x, params)
        grad_x, grad_p = pull(cotangent[micro].astype(jnp.float32))
        outputs.append(value)
        in_grads.append(grad_x)
        totals = grad_p if totals is None else tuple((a + b for a, b in zip(totals, grad_p)))
    return (jnp.stack(outputs), jnp.stack(in_grads), totals[0], totals[1], totals[2], totals[3], totals[4], totals[5], totals[6], totals[7], totals[8], totals[9], totals[10], totals[11], totals[12], totals[13], totals[14])
```

```python
import functools
import math

import jax
import jax.numpy as jnp
from jax import lax
from jax.experimental import pallas as pl
from jax.experimental.pallas import tpu as pltpu
from jax.sharding import PartitionSpec as P

eps = 1e-05
heads = 16
low = jnp.bfloat16
far = -1e30
lanes = 128
exact = jnp.float32


def layer_norm(v, gain, shift):
    mean = jnp.mean(v, axis=-1, keepdims=True)
    cent = v - mean
    var = jnp.mean(cent * cent, axis=-1, keepdims=True)
    return cent * lax.rsqrt(var + eps) * gain + shift


def norm_back(v, gain, shift, grad):
    value, pull = jax.vjp(layer_norm, v, gain, shift)
    return pull(grad)


def exact_gelu(v):
    return jax.nn.gelu(v, approximate=False)


def dot(a, b, ca, cb):
    return lax.dot_general(a, b, (((ca,), (cb,)), ((), ())), preferred_element_type=exact)


class Layout:
    def __init__(self, micro):
        self.count = lax.axis_size("dev")
        self.half = heads
        self.block = micro * heads
        self.blocks = self.count // self.block
        self.me = lax.axis_index("dev")
        self.rank = self.me % self.block
        self.mine = self.rank // self.half
        self.head = self.rank % self.half
        self.odd = self.rank % 2
        self.halves = [list(range(s, s + self.half)) for s in range(0, self.count, self.half)]
        self.whole = [list(range(s, s + self.block)) for s in range(0, self.count, self.block)]
        self.rows = [list(range(s, s + self.blocks)) for s in range(0, self.count, self.blocks)]
        self.even_first = [(d, self.target(d, d % 2)) for d in range(self.count)]
        self.odd_first = [(d, self.target(d, 1 - d % 2)) for d in range(self.count)]

    def target(self, d, half):
        base, rank = d // self.block * self.block, d % self.block
        return base + half * self.half + rank // 2

    def send(self, value, pairs):
        return lax.ppermute(value, "dev", pairs)

    def swapped(self, value, bit):
        return self.send(value, [(d, d ^ bit) for d in range(self.count)])

    def to_block(self, value):
        if self.blocks == 1:
            return value
        value = lax.all_gather(value, "dev", axis=0, tiled=True, axis_index_groups=self.rows)
        return self.send(value, [(d, d % self.blocks * self.block + d // self.blocks) for d in range(self.count)])

    def from_block(self, value):
        if self.blocks == 1:
            return value
        value = self.send(value, [(d % self.blocks * self.block + d // self.blocks, d) for d in range(self.count)])
        return lax.psum_scatter(value, "dev", scatter_dimension=0, tiled=True, axis_index_groups=self.rows)

    def pair_up(self, for_first, for_second):
        a = self.send(for_first, self.even_first)
        b = self.send(for_second, self.odd_first)
        return jnp.where(self.mine == 0, a, b), jnp.where(self.mine == 0, b, a)

    def pair_up_micro(self, value):
        first = lax.dynamic_index_in_dim(value, self.odd, 0, False)
        second = lax.dynamic_index_in_dim(value, 1 - self.odd, 0, False)
        return self.pair_up(first, second)

    def pair_back(self, value):
        first = lax.dynamic_index_in_dim(value, self.mine, 0, False)
        second = lax.dynamic_index_in_dim(value, 1 - self.mine, 0, False)
        a = self.send(first, [(t, s) for s, t in self.even_first])
        b = self.send(second, [(t, s) for s, t in self.odd_first])
        return jnp.where(self.odd == 0, a, b), jnp.where(self.odd == 0, b, a)

    def gather_half(self, value):
        return lax.all_gather(value, "dev", axis=0, axis_index_groups=self.halves)

    def exchange_half(self, value):
        return lax.all_to_all(value, "dev", 0, 0, tiled=True, axis_index_groups=self.halves)

    def exchange_block(self, value):
        return lax.all_to_all(value, "dev", 0, 0, tiled=True, axis_index_groups=self.whole)

    def bit(self, number):
        return (self.me // number) % 2

    def reduce_half(self, make):
        core = self.bit(1)
        got = self.swapped(make(1 - core).astype(low), 1)
        value = make(core) + got.astype(exact)
        tokens, width = value.shape[1:]
        value = value.reshape(2, 2, 2, tokens, width)
        cut = tokens * 3 // 8 // 8 * 8
        parts = [(0, cut, (8, 4, 2)), (cut, 2 * cut, (4, 2, 8)), (2 * cut, tokens, (2, 8, 4))]
        held = [(value[:, :, :, s:e], [8, 4, 2], order) for s, e, order in parts]
        for stage in range(3):
            after = []
            for piece, axes, order in held:
                bit = order[stage]
                at = axes.index(bit)
                side = self.bit(bit)
                away = lax.dynamic_index_in_dim(piece, 1 - side, at, False).astype(low)
                kept = lax.dynamic_index_in_dim(piece, side, at, False)
                after.append((kept.astype(exact) + self.swapped(away, bit).astype(exact), [x for x in axes if x != bit], order))
            held = after
        return jnp.concatenate([piece for piece, _, _ in held], axis=0)


def attend_kernel(hd, coef, q_ref, k_ref, v_ref, o_ref, lse_ref, vt_ref):
    @pl.when(pl.program_id(0) == 0)
    def _():
        vt_ref[...] = v_ref[...].T

    s = dot(k_ref[...], q_ref[...], 1, 1)
    top = jnp.max(s, axis=0, keepdims=True)
    e = jnp.exp2((s - top) * coef)
    total = jnp.sum(e, axis=0, keepdims=True)
    o = dot(vt_ref[...], e.astype(low), 1, 0) / total
    o = o.astype(low)
    for piece in range(o_ref.shape[0]):
        o_ref[piece] = o[:hd, piece * lanes : (piece + 1) * lanes]
    lse_ref[0] = top * coef + jnp.log2(total)


def attend(q, k, v, hd, rows):
    tokens, keys = q.shape[0], k.shape[0]
    coef = math.log2(math.e) / hd**0.5
    steps = tokens // rows
    return pl.pallas_call(
        functools.partial(attend_kernel, hd, coef),
        grid=(steps,),
        in_specs=[
            pl.BlockSpec((rows, lanes), lambda i: (i, 0)),
            pl.BlockSpec((keys, lanes), lambda i: (0, 0)),
            pl.BlockSpec((keys, lanes), lambda i: (0, 0)),
        ],
        out_specs=[
            pl.BlockSpec((rows // lanes, hd, lanes), lambda i: (i, 0, 0)),
            pl.BlockSpec((1, 1, rows), lambda i: (i, 0, 0)),
        ],
        out_shape=[
            jax.ShapeDtypeStruct((tokens // lanes, hd, lanes), low),
            jax.ShapeDtypeStruct((steps, 1, rows), exact),
        ],
        scratch_shapes=[pltpu.VMEM((lanes, keys), low)],
        compiler_params=pltpu.CompilerParams(vmem_limit_bytes=48 << 20),
        cost_estimate=pl.CostEstimate(flops=4 * tokens * keys * lanes, bytes_accessed=6 * keys * lanes, transcendentals=tokens * keys),
        name="attend",
    )(q, k, v)


def attend_back_kernel(hd, coef, scale, q_ref, k_ref, v_ref, do_ref, lse_ref, dq_ref, dk_ref, dv_ref, kt_ref, dk_sum, dv_sum):
    step = pl.program_id(0)

    @pl.when(step == 0)
    def _():
        kt_ref[...] = k_ref[...].T
        dk_sum[...] = jnp.zeros_like(dk_sum)
        dv_sum[...] = jnp.zeros_like(dv_sum)

    pieces = do_ref.shape[0]
    dot_t = jnp.concatenate([do_ref[piece] for piece in range(pieces)], axis=1)
    fill = jnp.zeros((lanes - hd, dot_t.shape[1]), low)
    dot_t = jnp.concatenate([dot_t, fill], axis=0)
    q = q_ref[...]
    s = dot(k_ref[...], q, 1, 1)
    p = jnp.exp2(s * coef - lse_ref[0])
    dp = dot(v_ref[...], dot_t, 1, 0)
    r = jnp.sum(p * dp, axis=0, keepdims=True)
    ds = (p * (dp - r)).astype(low)
    dv_sum[...] += dot(p.astype(low), dot_t.T, 1, 0)
    dk_sum[...] += dot(ds, q, 1, 0)
    dq = dot(kt_ref[...], ds, 1, 0) * scale
    head = lax.broadcasted_iota(jnp.int32, dq.shape, 0) < hd
    dq_ref[...] = jnp.where(head, dq, 0.0).T.astype(low)

    @pl.when(step == pl.num_programs(0) - 1)
    def _():
        head = lax.broadcasted_iota(jnp.int32, dk_sum.shape, 1) < hd
        dk_ref[...] = jnp.where(head, dk_sum[...] * scale, 0.0).astype(dk_ref.dtype)
        dv_ref[...] = dv_sum[...].astype(dv_ref.dtype)


def attend_back(q, k, v, do, lse, hd, rows, kind):
    tokens, keys = q.shape[0], k.shape[0]
    scale = 1.0 / hd**0.5
    coef = math.log2(math.e) * scale
    steps = tokens // rows
    whole = pl.BlockSpec((keys, lanes), lambda i: (0, 0))
    return pl.pallas_call(
        functools.partial(attend_back_kernel, hd, coef, scale),
        grid=(steps,),
        in_specs=[
            pl.BlockSpec((rows, lanes), lambda i: (i, 0)),
            whole,
            whole,
            pl.BlockSpec((rows // lanes, hd, lanes), lambda i: (i, 0, 0)),
            pl.BlockSpec((1, 1, rows), lambda i: (i, 0, 0)),
        ],
        out_specs=[pl.BlockSpec((rows, lanes), lambda i: (i, 0)), whole, whole],
        out_shape=[
            jax.ShapeDtypeStruct((tokens, lanes), low),
            jax.ShapeDtypeStruct((keys, lanes), kind),
            jax.ShapeDtypeStruct((keys, lanes), kind),
        ],
        scratch_shapes=[
            pltpu.VMEM((lanes, keys), low),
            pltpu.VMEM((keys, lanes), exact),
            pltpu.VMEM((keys, lanes), exact),
        ],
        compiler_params=pltpu.CompilerParams(vmem_limit_bytes=48 << 20),
        cost_estimate=pl.CostEstimate(flops=10 * tokens * keys * lanes, bytes_accessed=10 * keys * lanes, transcendentals=tokens * keys),
        name="attend_back",
    )(q, k, v, do, lse)


def body(
    hidden_in,
    clip_lengths,
    ln1_gain,
    ln1_bias,
    w_query,
    b_query,
    w_key,
    w_value,
    b_value,
    w_out,
    b_out,
    ln2_gain,
    ln2_bias,
    w_fc1,
    b_fc1,
    w_fc2,
    b_fc2,
    cotangent,
):
    micro, rows, width = hidden_in.shape
    at = Layout(micro)
    hd = width // heads
    own = 2 * rows
    tokens = at.half * own
    clips = clip_lengths.shape[1]
    chunk = width // at.block

    vectors = [at.to_block(v) for v in (ln1_gain, ln1_bias, b_query, b_value, b_out, ln2_gain, ln2_bias, b_fc2)]
    ff_bias = at.to_block(b_fc1)
    names = len(vectors)
    small = jnp.concatenate(vectors + [ff_bias])
    row = jnp.pad(small, (0, width - small.shape[0]))[None]
    with_row = jnp.concatenate([hidden_in, jnp.broadcast_to(row, (micro, 1, width))], axis=1)
    x_even, x_odd = at.pair_up_micro(with_row)
    x_own = jnp.concatenate([x_even[:rows], x_odd[:rows]], axis=0)
    packed = jnp.concatenate([x_own, x_even[rows:], x_odd[rows:]], axis=0)
    packed = at.gather_half(packed)
    x_all = packed[:, :own].reshape(tokens, width)
    table = packed[:, own:].reshape(at.block, width)[:, : chunk * names].reshape(at.block, names, chunk)
    g1, b1, bq, bv, bo, g2, b2, bf2 = (table[:, i].reshape(width).astype(exact) for i in range(names))
    ff_rows = ff_bias.shape[0]
    start = chunk * names
    c1 = jnp.concatenate([x_even[rows, start : start + ff_rows], x_odd[rows, start : start + ff_rows]]).astype(exact)

    w_in = jnp.stack([at.to_block(w) for w in (w_query, w_key, w_value)], axis=1)
    w_in = w_in.reshape(chunk, 3, heads, hd).transpose(2, 0, 1, 3).reshape(heads, chunk, 3 * hd)
    w_in = at.exchange_block(jnp.concatenate([w_in] * micro, axis=0)).reshape(width, 3, hd)
    w_in = jnp.pad(w_in, ((0, 0), (0, 0), (0, lanes - hd))).reshape(width, 3 * lanes)
    w1 = at.to_block(w_fc1)
    ff = w1.shape[1] // heads
    w1 = w1.reshape(chunk, heads, ff).transpose(1, 0, 2)
    w1 = at.exchange_block(jnp.concatenate([w1] * micro, axis=0)).reshape(width, ff)
    wo_shard = at.to_block(w_out)
    lower = jnp.concatenate([wo_shard, at.to_block(w_fc2)], axis=0)
    low_even, low_odd = at.pair_up(lower, lower)
    wo_head = jnp.concatenate([low_even[:chunk], low_odd[:chunk]], axis=0)
    w2 = jnp.concatenate([low_even[chunk:], low_odd[chunk:]], axis=0)
    wo = at.gather_half(wo_head).reshape(width, width)
    g_even, g_odd = at.pair_up_micro(cotangent)
    g_own = jnp.concatenate([g_even, g_odd], axis=0)
    g_all = at.gather_half(g_own).reshape(tokens, width)

    lengths = lax.dynamic_index_in_dim(clip_lengths, at.mine, 0, False)
    ends = jnp.cumsum(lengths)
    where_at = at.me // at.block * tokens + jnp.arange(tokens, dtype=jnp.int32)
    ids = jnp.sum((ends[None, :] <= where_at[:, None]).astype(jnp.int32), axis=1)
    column = jnp.arange(lanes, dtype=jnp.int32)[None] - hd
    matches = ids[:, None] == column
    marked = (column >= 0) & (column <= clips)
    q_mark = jnp.where(marked & ~matches, far, 0.0)
    k_mark = jnp.where(marked & matches, 1.0, 0.0)
    marks = jnp.concatenate([q_mark, k_mark, jnp.zeros_like(k_mark)], axis=1)

    a1 = layer_norm(x_all.astype(exact), g1, b1).astype(low)
    bias = jnp.stack([bq, jnp.zeros_like(bq), bv]).reshape(3, heads, hd)
    bias = lax.dynamic_index_in_dim(bias, at.head, 1, False)
    bias = jnp.pad(bias, ((0, 0), (0, lanes - hd))).reshape(3 * lanes)
    qkv = (dot(a1, w_in, 1, 0) + bias + marks).astype(low)
    q, k, v = (qkv[:, i * lanes : (i + 1) * lanes] for i in range(3))
    if at.blocks > 1:
        span = tokens // 2
        ahead = [(d, d + at.block) for d in range(at.count - at.block)]
        behind = [(d + at.block, d) for d in range(at.count - at.block)]
        nothing = jnp.where(column == clips, 1.0, 0.0).astype(low)
        kv = jnp.stack([k, v])
        before = at.send(kv[:, tokens - span :], ahead)
        after = at.send(kv[:, :span], behind)
        is_first = at.me < at.block
        is_last = at.me >= at.count - at.block
        k = jnp.concatenate([jnp.where(is_first, nothing, before[0]), k, jnp.where(is_last, nothing, after[0])], axis=0)
        v = jnp.concatenate([before[1], v, after[1]], axis=0)
    step_rows = 256
    o_head, lse = attend(q, k, v, hd, step_rows)
    o_own = at.exchange_half(o_head).reshape(width, own)

    x2 = x_own.astype(exact) + (dot(o_own, wo, 0, 0) + bo)
    a2_own = layer_norm(x2, g2, b2).astype(low)
    a2 = at.gather_half(a2_own).reshape(tokens, width)
    u = dot(a2, w1, 1, 0) + c1
    hid = exact_gelu(u).astype(low)

    d_hid = dot(g_all, w2, 1, 1)
    du = jax.vjp(exact_gelu, u)[1](d_hid)[0].astype(low)

    def half_terms(left, right, contract):
        split = left.reshape(8, 2, own, left.shape[1])

        def make(part):
            piece = lax.dynamic_index_in_dim(split, part, 1, False).reshape(8 * own, left.shape[1])
            return dot(piece, right, 1, contract).reshape(8, own, width)

        return make

    da2 = at.reduce_half(half_terms(du, w1, 1))
    d_x2n, d_g2, d_b2 = norm_back(x2, g2, b2, da2)
    dx2 = g_own.astype(exact) + d_x2n
    ga_own = dx2.astype(low)
    do_own = dot(wo, ga_own, 1, 1).astype(low).reshape(heads, hd, own)
    do_head = at.exchange_half(do_own)
    ga = at.gather_half(ga_own)

    kind = low if at.blocks == 1 else exact
    dq, dk, dv = attend_back(q, k, v, do_head, lse, hd, step_rows, kind)
    if at.blocks > 1:
        span = tokens // 2
        dkv = jnp.stack([dk, dv])
        to_before = at.send(dkv[:, :span].astype(low), behind).astype(exact)
        to_after = at.send(dkv[:, span + tokens :].astype(low), ahead).astype(exact)
        dkv = dkv[:, span : span + tokens] + jnp.concatenate([to_after, to_before], axis=1)
        dk, dv = dkv[0].astype(low), dkv[1].astype(low)
    dqkv = jnp.concatenate([dq, dk, dv], axis=1)
    da1 = at.reduce_half(half_terms(dqkv, w_in, 1))
    d_xn, d_g1, d_b1 = norm_back(x_own.astype(exact), g1, b1, da1)
    dx = dx2 + d_xn

    y = at.reduce_half(half_terms(hid, w2, 0))
    out = x2 + (y + bf2)

    d_w2 = dot(hid, g_all, 0, 0)
    d_w1 = dot(a2, du, 0, 0)
    d_wo = jnp.einsum("ckt,ctn->kn", o_head, ga, preferred_element_type=exact)
    d_in = dot(a1, dqkv, 0, 0).reshape(width, 3, lanes)[:, :, :hd].reshape(width, 3 * hd)

    back = jnp.concatenate([d_w2.reshape(2, -1, width), d_wo.reshape(2, chunk, width)], axis=1).astype(low)
    first, second = at.pair_back(back)
    total = first.astype(exact) + second.astype(exact)
    grad_w2 = at.from_block(total[:-chunk])
    grad_wo = at.from_block(total[-chunk:])

    wide = jnp.concatenate([d_w1, d_in], axis=1).astype(low).reshape(at.block, chunk, ff + 3 * hd)
    wide = at.exchange_block(wide).astype(exact)
    wide = jnp.sum(wide.reshape(micro, heads, chunk, ff + 3 * hd), axis=0)
    grad_w1 = at.from_block(wide[:, :, :ff].transpose(1, 0, 2).reshape(chunk, heads * ff))
    d_in = wide[:, :, ff:].reshape(heads, chunk, 3, hd).transpose(2, 1, 0, 3).reshape(3, chunk, width)
    grad_wq, grad_wk, grad_wv = (at.from_block(d_in[i]) for i in range(3))

    def spread(value, size):
        zeros = jnp.zeros((heads, size), exact)
        return lax.dynamic_update_index_in_dim(zeros, value, at.head, 0).reshape(heads * size)

    d_bq = spread(jnp.sum(dq[:, :hd].astype(exact), axis=0), hd)
    d_bv = spread(jnp.sum(dv[:, :hd].astype(exact), axis=0), hd)
    d_c1 = spread(jnp.sum(du.astype(exact), axis=0), ff)
    d_bo = jnp.sum(ga_own.astype(exact), axis=0)
    d_bf2 = jnp.sum(g_own.astype(exact), axis=0)
    parts = [d_g1, d_b1, d_bq, d_bv, d_bo, d_g2, d_b2, d_bf2]
    vector = jnp.stack(parts).reshape(names, at.block, chunk).transpose(1, 0, 2).reshape(at.block, names * chunk)
    vector = jnp.concatenate([vector, d_c1.reshape(at.block, ff_rows)], axis=1)
    vector = jnp.sum(at.exchange_block(vector), axis=0)
    pieces = [at.from_block(vector[i * chunk : (i + 1) * chunk]) for i in range(names)]
    grad_g1, grad_b1, grad_bq, grad_bv, grad_bo, grad_g2, grad_b2, grad_bf2 = pieces
    grad_c1 = at.from_block(vector[names * chunk :])

    ends_out = jnp.stack([out, dx], axis=0).astype(low).reshape(2, 2, rows, width).transpose(1, 0, 2, 3)
    first, second = at.pair_back(ends_out)
    layer_out = jnp.stack([first[0], second[0]]).astype(exact)
    input_grad = jnp.stack([first[1], second[1]]).astype(exact)
    return (
        layer_out,
        input_grad,
        grad_g1,
        grad_b1,
        grad_wq,
        grad_bq,
        grad_wk,
        grad_wv,
        grad_bv,
        grad_wo,
        grad_bo,
        grad_g2,
        grad_b2,
        grad_w1,
        grad_c1,
        grad_w2,
        grad_bf2,
    )


def solution(mesh):
    tokens, vector, matrix = P(None, "dev", None), P("dev"), P("dev", None)
    grads = (vector, vector, matrix, vector, matrix, matrix, vector, matrix, vector, vector, vector, matrix, vector, matrix, vector)
    return jax.shard_map(
        body,
        mesh=mesh,
        in_specs=(tokens, P()) + grads + (tokens,),
        out_specs=(tokens, tokens) + grads,
        check_vma=False,
    )
```

```python
import functools
import math

import jax
import jax.numpy as jnp
from jax import lax
from jax.experimental import pallas as pl
from jax.experimental.pallas import tpu as pltpu
from jax.sharding import PartitionSpec as P

eps = 1e-05
heads = 16
low = jnp.bfloat16
exact = jnp.float32
far = -1e30
lanes = 128
extra_rows = 8


def dot(a, b, ca, cb):
    return lax.dot_general(a, b, (((ca,), (cb,)), ((), ())), preferred_element_type=exact)


def normalized(v):
    mean = jnp.mean(v, axis=-1, keepdims=True)
    cent = v - mean
    inverse = lax.rsqrt(jnp.mean(cent * cent, axis=-1, keepdims=True) + eps)
    return cent * inverse, inverse


def norm_back(unit, inverse, gain, grad):
    scaled = grad * gain
    along = jnp.mean(scaled * unit, axis=-1, keepdims=True)
    return inverse * (scaled - jnp.mean(scaled, axis=-1, keepdims=True) - unit * along)


def tie(value, *others):
    return lax.optimization_barrier((value,) + others)[0]


def together(*values):
    return lax.optimization_barrier(values)


class Layout:
    def __init__(self, micro):
        self.count = lax.axis_size("dev")
        self.half = heads
        self.block = micro * heads
        self.blocks = self.count // self.block
        self.me = lax.axis_index("dev")
        self.rank = self.me % self.block
        self.mine = self.rank // self.half
        self.head = self.rank % self.half
        self.odd = self.rank % 2
        bits = [(self.me // bit) % 2 for bit in (1, 2, 4, 8)]
        self.place = jnp.stack(bits + [self.mine, self.head, self.odd]).astype(jnp.int32)
        self.halves = [list(range(s, s + self.half)) for s in range(0, self.count, self.half)]
        self.whole = [list(range(s, s + self.block)) for s in range(0, self.count, self.block)]
        self.rows = [list(range(s, s + self.blocks)) for s in range(0, self.count, self.blocks)]
        first = [d // self.half % 2 for d in range(self.count)]
        base = [d // self.block * self.block + 2 * (d % self.half) for d in range(self.count)]
        self.even_first = [(d, base[d] + first[d]) for d in range(self.count)]
        self.odd_first = [(d, base[d] + 1 - first[d]) for d in range(self.count)]

    def send(self, value, pairs):
        return lax.ppermute(value, "dev", pairs)

    def swapped(self, value, bit):
        return self.send(value, [(d, d ^ bit) for d in range(self.count)])

    def to_block(self, value):
        if self.blocks == 1:
            return value
        value = lax.all_gather(value, "dev", axis=0, tiled=True, axis_index_groups=self.rows)
        return self.send(value, [(d, d % self.blocks * self.block + d // self.blocks) for d in range(self.count)])

    def from_block(self, value):
        if self.blocks == 1:
            return value
        value = self.send(value, [(d % self.blocks * self.block + d // self.blocks, d) for d in range(self.count)])
        return lax.psum_scatter(value, "dev", scatter_dimension=0, tiled=True, axis_index_groups=self.rows)

    def partner(self, value):
        return self.swapped(value, self.half)

    def ordered(self, kept, got):
        return jnp.where(self.mine == 0, kept, got), jnp.where(self.mine == 0, got, kept)

    def exchanged(self, value):
        kept = lax.dynamic_index_in_dim(value, self.mine, 0, False)
        return kept, self.partner(lax.dynamic_index_in_dim(value, 1 - self.mine, 0, False))

    def send_rows_back(self, value):
        first = lax.dynamic_index_in_dim(value, self.mine, 0, False)
        second = lax.dynamic_index_in_dim(value, 1 - self.mine, 0, False)
        return self.send(first, self.even_first), self.send(second, self.odd_first)

    def gather_half(self, value):
        return lax.all_gather(value, "dev", axis=0, axis_index_groups=self.halves)

    def exchange_half(self, value):
        return lax.all_to_all(value, "dev", 0, 0, tiled=True, axis_index_groups=self.halves)

    def exchange_block(self, value):
        return lax.all_to_all(value, "dev", 0, 0, tiled=True, axis_index_groups=self.whole)

    def gather_tree(self, parts, marks=None):
        for stage in range(2):
            got = [self.swapped(piece, order[stage]) for piece, order in zip(parts, part_orders)]
            parts = merge(parts, got)
            if marks is not None:
                marks.append(parts[0])
        got = [self.swapped(piece, order[2]) for piece, order in zip(parts, part_orders)]
        other = [self.swapped(piece, 1) for piece in (*parts, *got)]
        return (*parts, *got), other

    def reduce_half(self, away, kept, marks=None, before=None):
        got = [self.swapped(away, 1)]
        kept = [kept]
        for stage in range(3):
            if before and stage in before:
                got = [tie(got[0], *before[stage](marks)), *got[1:]]
            away, kept = split_terms(self.place, stage, kept, got)
            if marks is not None:
                marks.append(away[0])
            got = [self.swapped(piece, order[stage]) for piece, order in zip(away, part_orders)]
        return kept, got


small_cost = pl.CostEstimate(flops=1 << 10, bytes_accessed=1 << 10, transcendentals=0)


def params(megabytes):
    return pltpu.CompilerParams(vmem_limit_bytes=megabytes << 20)


part_orders = ((8, 4, 2), (4, 2, 8), (2, 8, 4))


def part_bounds(tokens):
    cut = tokens * 3 // 8 // 16 * 16
    return ((0, cut), (cut, 2 * cut), (2 * cut, tokens))


def split_kernel(stage, place_ref, *refs):
    place = {bit: place_ref[i] for i, bit in enumerate((1, 2, 4, 8))}
    if stage == 0:
        kept_ref, got_ref = refs[:2]
        outs = refs[2:]
        bounds = part_bounds(kept_ref.shape[1])
    else:
        outs = refs[6:]
    for part, order in enumerate(part_orders):
        left = [bit for bit in (8, 4, 2) if bit not in order[:stage]]
        at = left.index(order[stage])
        below = 1 << (len(left) - 1 - at)
        for half, side in ((0, 1 - place[order[stage]]), (1, place[order[stage]])):
            out_ref = outs[part + 3 * half]
            for j in range(out_ref.shape[0]):
                index = (j // below * 2 + side) * below + j % below
                if stage == 0:
                    start, end = bounds[part]
                    term = kept_ref[index, start:end].astype(exact) + got_ref[index, start:end].astype(exact)
                else:
                    term = refs[part][index].astype(exact) + refs[3 + part][index].astype(exact)
                out_ref[j] = term.astype(out_ref.dtype)


def split_terms(place, stage, kept, got):
    width = kept[0].shape[-1]
    bounds = part_bounds(kept[0].shape[1]) if stage == 0 else [(0, k.shape[1]) for k in kept]
    count = kept[0].shape[0] // 2
    cols = 256 if stage == 0 else 640
    spec = lambda n, t: pl.BlockSpec((n, t, cols), lambda i, p: (0, 0, i))
    outs = [(count, end - start) for start, end in bounds]
    res = pl.pallas_call(
        functools.partial(split_kernel, stage),
        grid_spec=pltpu.PrefetchScalarGridSpec(
            num_scalar_prefetch=1,
            grid=(width // cols,),
            in_specs=[spec(*v.shape[:2]) for v in (*kept, *got)],
            out_specs=[spec(*o) for o in outs] * 2,
        ),
        out_shape=[jax.ShapeDtypeStruct(o + (width,), kind) for kind in (low, exact) for o in outs],
        compiler_params=params(32),
        cost_estimate=small_cost,
        name="split_terms",
    )(place, *kept, *got)
    return res[:3], res[3:]


def last_sum(refs):
    return jnp.concatenate([refs[i][0].astype(exact) + refs[3 + i][0].astype(exact) for i in range(3)], axis=0)


def pack_kernel(place_ref, x_ref, v_ref, c_ref, w_ref, first_ref, second_ref):
    rows, width = x_ref.shape[1:]
    mine = place_ref[4]
    fill = jnp.zeros((v_ref.shape[0], width - v_ref.shape[1]), exact)
    small = jnp.concatenate([v_ref[...].astype(exact), fill], axis=1)
    c = jnp.concatenate([c_ref[...].astype(exact), jnp.zeros((1, width - lanes - c_ref.shape[1]), exact)], axis=1)
    c = jnp.concatenate([jnp.zeros((1, lanes), exact), c], axis=1)
    row = lax.broadcasted_iota(jnp.int32, small.shape, 0)
    small = small + jnp.where(row == 0, c, 0.0)
    tail = jnp.concatenate([small, w_ref[...].astype(exact)], axis=0).astype(low)
    for out_ref, index in ((first_ref, mine), (second_ref, 1 - mine)):
        out_ref[:rows] = x_ref[index]
        out_ref[rows:] = tail


def pack(place, x, vectors, c, w):
    rows, width = x.shape[1:]
    out = jax.ShapeDtypeStruct((rows + extra_rows + w.shape[0], width), low)
    return pl.pallas_call(
        pack_kernel,
        grid_spec=pltpu.PrefetchScalarGridSpec(
            num_scalar_prefetch=1,
            grid=(1,),
            in_specs=[whole_spec(v) for v in (x, vectors, c, w)],
            out_specs=[whole_spec(out)] * 2,
        ),
        out_shape=[out, out],
        compiler_params=params(32),
        name="pack",
    )(place, x, vectors, c, w)


def arrange_kernel(rows, place_ref, first_ref, second_ref, x_ref, small_ref, w_ref, *part_refs):
    mine = place_ref[4]
    for side, refs in enumerate(((first_ref, second_ref), (second_ref, first_ref))):

        @pl.when(mine == side)
        def _():
            x = jnp.concatenate([ref[:rows] for ref in refs], axis=0)
            x_ref[...] = x
            tail = [ref[rows:].astype(exact) for ref in refs]
            small_ref[...] = jnp.concatenate([t[:extra_rows] for t in tail], axis=0).astype(low)
            w_ref[...] = jnp.concatenate([t[extra_rows:] for t in tail], axis=0).astype(low)
            for part_ref, (start, end) in zip(part_refs, part_bounds(2 * rows)):
                part_ref[0] = x[start:end]


def arrange(place, first, second, rows):
    width = first.shape[1]
    shapes = [(2 * rows, width), (2 * extra_rows, width), (2 * (first.shape[0] - rows - extra_rows), width)]
    shapes += [(1, end - start, width) for start, end in part_bounds(2 * rows)]
    outs = [jax.ShapeDtypeStruct(shape, low) for shape in shapes]
    return pl.pallas_call(
        functools.partial(arrange_kernel, rows),
        grid_spec=pltpu.PrefetchScalarGridSpec(
            num_scalar_prefetch=1,
            grid=(1,),
            in_specs=[whole_spec(first), whole_spec(second)],
            out_specs=[whole_spec(out) for out in outs],
        ),
        out_shape=outs,
        compiler_params=params(32),
        name="arrange",
    )(place, first, second)


def merge_kernel(*refs):
    for i in range(3):
        count = refs[i].shape[0]
        refs[6 + i][:count] = refs[i][...]
        refs[6 + i][count:] = refs[3 + i][...]


def merge(parts, got):
    width = parts[0].shape[2]
    cols = 640
    spec = lambda shape: pl.BlockSpec(shape[:2] + (cols,), lambda i: (0, 0, i))
    outs = [(2 * p.shape[0],) + p.shape[1:] for p in parts]
    return pl.pallas_call(
        merge_kernel,
        grid=(width // cols,),
        in_specs=[spec(v.shape) for v in (*parts, *got)],
        out_specs=[spec(o) for o in outs],
        out_shape=[jax.ShapeDtypeStruct(o, low) for o in outs],
        compiler_params=params(32),
        name="merge",
    )(*parts, *got)


def tree_rows(place_ref, chip, refs, fill):
    mine = place_ref[1] + 2 * place_ref[2] + 4 * place_ref[3]
    apart = chip ^ mine
    step = {8: apart // 4, 4: apart // 2 % 2, 2: apart % 2}
    for part, order in enumerate(part_orders):
        index = 2 * step[order[1]] + step[order[0]]
        for late in range(2):

            @pl.when(step[order[2]] == late)
            def _():
                fill(part, refs[part + 3 * late], index)


def fill_rows(place_ref, chip, refs, out_ref, base, own):
    bounds = part_bounds(own)

    def fill(part, ref, index):
        start, end = bounds[part]
        out_ref[pl.ds(base + start, end - start)] = ref[index, : end - start]

    tree_rows(place_ref, chip, refs, fill)


def whole_spec(v):
    return pl.BlockSpec(v.shape, lambda i, p: (0,) * len(v.shape))


def project_kernel(hd, clips, chunk, first, place_ref, *refs):
    pieces, refs = refs[:6], refs[6:]
    ids_ref, w_ref = refs[:2]
    a_ref, qkv_ref, table_ref, x_scr, bias_ref = refs[-5:]
    step, _, own, width = a_ref.shape

    @pl.when(pl.program_id(0) == 0)
    def _():
        if first:
            tail = part_bounds(own)[2]

            def fill(chip, part, ref, index):
                if part != 2:
                    return
                small = ref[index, tail[1] - tail[0] :].astype(exact)
                for far_core in range(2):
                    for slot in range(2):
                        line = (2 * far_core + slot) * extra_rows
                        piece = small[line : line + extra_rows, :chunk]
                        for core in range(2):

                            @pl.when(place_ref[0] == core)
                            def _():
                                at = (heads * slot + 2 * chip + (core ^ far_core)) * chunk
                                table_ref[:, at : at + chunk] = piece

            for chip in range(8):
                tree_rows(place_ref, chip, pieces, functools.partial(fill, chip))
        else:
            table_ref[...] = refs[2][...]
        bias_ref[...] = jnp.zeros_like(bias_ref)
        for h in range(heads):

            @pl.when(place_ref[5] == h)
            def _():
                for line, at in ((2, 0), (3, 2 * lanes)):
                    bias_ref[0:1, at : at + hd] = table_ref[line : line + 1, h * hd : (h + 1) * hd]

    for j in range(step):
        fill_rows(place_ref, pl.program_id(0) * step + j, pieces, x_scr, j * own, own)
    unit, _ = normalized(x_scr[...].astype(exact))
    a = (unit * table_ref[0:1] + table_ref[1:2]).astype(low)
    a_ref[...] = a.reshape(a_ref.shape)
    qkv = dot(a, w_ref[...], 1, 0)
    fill = jnp.zeros((step * own, lanes - hd), exact)
    qkv = [v for i in range(3) for v in (qkv[:, i * hd : (i + 1) * hd], fill)]
    qkv = jnp.concatenate(qkv, axis=1) + bias_ref[0:1]
    column = lax.broadcasted_iota(jnp.int32, (step * own, lanes), 1) - hd
    match = ids_ref[...].reshape(step * own, 1) == column
    marked = (column >= 0) & (column <= clips)
    q = qkv[:, :lanes] + jnp.where(marked & ~match, far, 0.0)
    k = qkv[:, lanes : 2 * lanes] + jnp.where(marked & match, 1.0, 0.0)
    qkv = jnp.concatenate([q, k, qkv[:, 2 * lanes :]], axis=1).astype(low)
    qkv_ref[...] = qkv.reshape(qkv_ref.shape)


def project(place, other, pieces, ids, w, before, hd, clips, own, chunk):
    width = w.shape[0]
    step = 4
    side = (lambda p: 1 - p[0]) if other else (lambda p: p[0])
    pick = lambda size: pl.BlockSpec((step, 1, own, size), lambda i, p: (i, side(p), 0, 0))
    table = jax.ShapeDtypeStruct((extra_rows, width), exact)
    ahead = [before[2], *before[:2]] if before else []
    return pl.pallas_call(
        functools.partial(project_kernel, hd, clips, chunk, not before),
        grid_spec=pltpu.PrefetchScalarGridSpec(
            num_scalar_prefetch=1,
            grid=(8 // step,),
            in_specs=[whole_spec(v) for v in pieces]
            + [pick(1), whole_spec(w)]
            + ([whole_spec(table)] + [pl.BlockSpec(memory_space=pl.ANY)] * 2 if before else []),
            out_specs=[pick(width), pick(3 * lanes), whole_spec(table)],
            scratch_shapes=[pltpu.VMEM((step * own, width), low), pltpu.VMEM((8, 3 * lanes), exact)],
        ),
        out_shape=[
            jax.ShapeDtypeStruct((8, 2, own, width), low),
            jax.ShapeDtypeStruct((8, 2, own, 3 * lanes), low),
            table,
        ],
        input_output_aliases={10: 0, 11: 1} if before else {},
        compiler_params=params(48),
        cost_estimate=small_cost,
        name="project",
    )(place, *pieces, ids, w, *ahead)


def join_kernel(x_ref, o_ref, w_ref, table_ref, x2_ref, *part_refs):
    o = o_ref[...].reshape(w_ref.shape[0], o_ref.shape[2])
    x2 = x_ref[...].astype(exact) + (dot(o, w_ref[...], 0, 0) + table_ref[4:5])
    x2_ref[...] = x2
    unit, _ = normalized(x2)
    a2 = (unit * table_ref[5:6] + table_ref[6:7]).astype(low)
    for part_ref, (start, end) in zip(part_refs, part_bounds(x2.shape[0])):
        part_ref[0] = a2[start:end]


def join(x, o, w, table):
    own, width = x.shape
    parts = [jax.ShapeDtypeStruct((1, end - start, width), low) for start, end in part_bounds(own)]
    return pl.pallas_call(
        join_kernel,
        out_shape=[jax.ShapeDtypeStruct(x.shape, exact)] + parts,
        compiler_params=params(32),
        cost_estimate=small_cost,
        name="join",
    )(x, o, w, table)


def assemble_kernel(place_ref, *refs):
    mine, others, out_ref = refs[:6], refs[6:12], refs[12]
    chips, _, own, _ = out_ref.shape
    for j in range(chips):
        chip = pl.program_id(0) * chips + j
        for core, pieces in ((place_ref[0], mine), (1 - place_ref[0], others)):
            bounds = part_bounds(own)

            def fill(part, ref, index):
                start, end = bounds[part]
                out_ref[j, core, start:end] = ref[index]

            tree_rows(place_ref, chip, pieces, fill)


def assemble(place, mine, others, own):
    width = mine[0].shape[2]
    step = 2
    return pl.pallas_call(
        assemble_kernel,
        grid_spec=pltpu.PrefetchScalarGridSpec(
            num_scalar_prefetch=1,
            grid=(8 // step,),
            in_specs=[whole_spec(v) for v in (*mine, *others)],
            out_specs=pl.BlockSpec((step, 2, own, width), lambda i, p: (i, 0, 0, 0)),
        ),
        out_shape=jax.ShapeDtypeStruct((8, 2, own, width), low),
        compiler_params=params(40),
        cost_estimate=small_cost,
        name="assemble",
    )(place, *mine, *others)


def feed_kernel(place_ref, *refs):
    pieces, (g_ref, w1_ref, w2_ref, c_ref) = refs[:6], refs[6:10]
    hid_ref, du_ref, da_ref, sum_ref, a_scr = refs[-5:]
    step, own, width = da_ref.shape
    rows = step * own
    for j in range(step):
        fill_rows(place_ref, pl.program_id(0) * step + j, pieces, a_scr, j * own, own)
    w1 = w1_ref[...]
    u = dot(a_scr[...], w1, 1, 0) + c_ref[...]
    d_hid = dot(g_ref[...].reshape(rows, width), w2_ref[...], 1, 1)
    below = 0.5 * (1.0 + lax.erf(u * math.sqrt(0.5)))
    hid_ref[...] = (u * below).astype(low).reshape(hid_ref.shape)
    slope = below + u * (jnp.exp(-0.5 * u * u) * (1.0 / math.sqrt(2.0 * math.pi)))
    du = (d_hid * slope).astype(low)
    du_ref[...] = du.reshape(du_ref.shape)
    da_ref[...] = dot(du, w1, 1, 1).reshape(da_ref.shape).astype(da_ref.dtype)

    @pl.when(pl.program_id(0) == 0)
    def _():
        sum_ref[...] = jnp.zeros_like(sum_ref)

    sum_ref[...] += jnp.sum(du.astype(exact), axis=0, keepdims=True)


def feed(place, other, pieces, g, w1, w2, c1, before, own, kind):
    width, ff = w1.shape
    step = 4
    tokens = 8 * own
    side = (lambda p: 1 - p[0]) if other else (lambda p: p[0])
    pick = lambda size: pl.BlockSpec((step, 1, own, size), lambda i, p: (i, side(p), 0, 0))
    pair = jax.ShapeDtypeStruct((8, 2, own, ff), low)
    row = pl.BlockSpec((1, ff), lambda i, p: (0, 0))
    return pl.pallas_call(
        feed_kernel,
        grid_spec=pltpu.PrefetchScalarGridSpec(
            num_scalar_prefetch=1,
            grid=(8 // step,),
            in_specs=[whole_spec(v) for v in pieces]
            + [pick(width), whole_spec(w1), whole_spec(w2), row]
            + [pl.BlockSpec(memory_space=pl.ANY)] * len(before),
            out_specs=[pick(ff), pick(ff), pl.BlockSpec((step, own, width), lambda i, p: (i, 0, 0)), row],
            scratch_shapes=[pltpu.VMEM((step * own, width), low)],
        ),
        out_shape=[
            pair,
            pair,
            jax.ShapeDtypeStruct((8, own, width), kind),
            jax.ShapeDtypeStruct((1, ff), exact),
        ],
        input_output_aliases={11: 0, 12: 1} if before else {},
        compiler_params=params(56),
        cost_estimate=small_cost,
        name="feed",
    )(place, *pieces, g, w1, w2, c1, *before)


def terms_kernel(contract, place_ref, left_ref, right_ref, out_ref):
    rows = out_ref.shape[0] * out_ref.shape[1]
    left = left_ref[...].reshape(rows, left_ref.shape[-1])
    out_ref[...] = dot(left, right_ref[...], 1, contract).reshape(out_ref.shape).astype(out_ref.dtype)


def terms(place, other, left, right, contract, kind):
    eight, two, own, depth = left.shape
    width = right.shape[1 - contract]
    step = 2
    side = (lambda p: 1 - p[0]) if other else (lambda p: p[0])
    return pl.pallas_call(
        functools.partial(terms_kernel, contract),
        grid_spec=pltpu.PrefetchScalarGridSpec(
            num_scalar_prefetch=1,
            grid=(eight // step,),
            in_specs=[
                pl.BlockSpec((step, 1, own, depth), lambda i, p: (i, side(p), 0, 0)),
                pl.BlockSpec(right.shape, lambda i, p: (0, 0)),
            ],
            out_specs=pl.BlockSpec((step, own, width), lambda i, p: (i, 0, 0)),
        ),
        out_shape=jax.ShapeDtypeStruct((eight, own, width), kind),
        compiler_params=params(40),
        cost_estimate=small_cost,
        name="terms",
    )(place, left, right)


def rows_of(values, width):
    fill = jnp.zeros((8 - len(values), width), exact)
    return jnp.concatenate(values + [fill], axis=0)


def second_back_kernel(*refs):
    da2 = last_sum(refs[:6])
    x2_ref, g_ref, table_ref, w_ref, dx2_ref, ga_ref, do_ref, sum_ref = refs[6:]
    unit, inverse = normalized(x2_ref[...])
    g = g_ref[...].astype(exact)
    dx2 = g + norm_back(unit, inverse, table_ref[5:6], da2)
    dx2_ref[...] = dx2
    ga = dx2.astype(low)
    ga_ref[...] = ga
    do_ref[...] = dot(w_ref[...], ga, 1, 1).astype(low).reshape(do_ref.shape)
    total = lambda v: jnp.sum(v, axis=0, keepdims=True)
    sum_ref[...] = rows_of([total(da2 * unit), total(da2), total(ga.astype(exact)), total(g)], ga.shape[1])


def second_back(kept, got, x2, g, table, w, hd):
    own, width = x2.shape
    return pl.pallas_call(
        second_back_kernel,
        out_shape=[
            jax.ShapeDtypeStruct((own, width), exact),
            jax.ShapeDtypeStruct((own, width), low),
            jax.ShapeDtypeStruct((heads, hd, own), low),
            jax.ShapeDtypeStruct((8, width), exact),
        ],
        compiler_params=params(40),
        cost_estimate=small_cost,
        name="second_back",
    )(*kept, *got, x2, g, table, w)


def first_back_kernel(chunk, *refs):
    da1 = last_sum(refs[:6])
    x_ref, dx2_ref, table_ref, dx_ref, vec_ref = refs[6:]
    unit, inverse = normalized(x_ref[...].astype(exact))
    dx = dx2_ref[...] + norm_back(unit, inverse, table_ref[0:1], da1)
    dx_ref[...] = dx.astype(low)
    total = lambda v: jnp.sum(v, axis=0, keepdims=True)
    rows = [total(da1 * unit), total(da1)]
    fill = jnp.zeros((1, lanes // 2 - chunk), exact)
    for device in range(vec_ref.shape[0]):
        part = slice(device * chunk, (device + 1) * chunk)
        vec_ref[device] = jnp.concatenate([rows[0][:, part], fill, rows[1][:, part], fill], axis=1)


def first_back(kept, got, x, dx2, table, chunk, block):
    return pl.pallas_call(
        functools.partial(first_back_kernel, chunk),
        out_shape=[jax.ShapeDtypeStruct(x.shape, low), jax.ShapeDtypeStruct((block, 1, lanes), exact)],
        compiler_params=params(32),
        name="first_back",
    )(*kept, *got, x, dx2, table)


def lay_out_kernel(hd, chunk, place_ref, in_ref, sum2_ref, sum_in_ref, sum_c_ref, sum_c2_ref, out_ref):
    block = out_ref.shape[0]
    head = place_ref[5]
    c = sum_c_ref[...] + sum_c2_ref[...]
    ff_rows = c.shape[1] // 2
    rest = jnp.zeros((8, 3 * hd - chunk), exact)
    zeros = jnp.zeros((2, chunk), exact)
    narrow = jnp.concatenate([in_ref[:, i * lanes : i * lanes + hd] for i in range(3)], axis=1)
    pad = jnp.zeros((1, 3 * hd - chunk - ff_rows), exact)
    row = lax.broadcasted_iota(jnp.int32, (8, 3 * hd), 0)
    for device in range(block):
        part = slice(device * chunk, (device + 1) * chunk)
        small = jnp.concatenate([sum2_ref[0:4, part], zeros, zeros], axis=0)
        small = jnp.concatenate([small, rest], axis=1)
        slot = device % 2
        cols = slice(slot * chunk, (slot + 1) * chunk)
        for line, at in ((4, 0), (5, 2 * lanes)):
            own = jnp.concatenate([sum_in_ref[0:1, at : at + hd][:, cols], rest[0:1]], axis=1)
            small += jnp.where((row == line) & (head == device // 2), own, 0.0)
        slot = device // heads
        own = jnp.concatenate([zeros[0:1], c[:, slot * ff_rows : (slot + 1) * ff_rows], pad], axis=1)
        small += jnp.where((row == 0) & (head == device % heads), own, 0.0)
        out_ref[device] = jnp.concatenate([narrow[part], small], axis=0).astype(low)


def lay_out(place, d_in, sum2, sum_in, sum_c, sum_c2, hd, chunk, block):
    smem = pl.BlockSpec(memory_space=pltpu.SMEM)
    vmem = pl.BlockSpec(memory_space=pltpu.VMEM)
    return pl.pallas_call(
        functools.partial(lay_out_kernel, hd, chunk),
        in_specs=[smem] + [vmem] * 5,
        out_shape=jax.ShapeDtypeStruct((block, chunk + 8, 3 * hd), low),
        compiler_params=params(32),
        name="lay_out",
    )(place, d_in, sum2, sum_in, sum_c, sum_c2)


def collect_kernel(hd, *refs):
    in_ref, *out_refs, small_ref = refs
    chunk = out_refs[0].shape[0]
    block = in_ref.shape[0]
    small = jnp.zeros(small_ref.shape, exact)
    for head in range(block // 2):
        first, second = in_ref[head].astype(exact), in_ref[block // 2 + head].astype(exact)
        total = first + second
        small += total[chunk:]
        for i, out_ref in enumerate(out_refs):
            out_ref[:, head * hd : (head + 1) * hd] = total[:chunk, i * hd : (i + 1) * hd]
    small_ref[...] = small


def collect(terms_in, hd, chunk):
    block = terms_in.shape[0]
    matrix = jax.ShapeDtypeStruct((chunk, block // 2 * hd), exact)
    return pl.pallas_call(
        functools.partial(collect_kernel, hd),
        out_shape=[matrix] * 3 + [jax.ShapeDtypeStruct((8, 3 * hd), exact)],
        compiler_params=params(32),
        name="collect",
    )(terms_in)


def collect_hidden_kernel(in_ref, out_ref):
    block, _, ff = in_ref.shape
    for slice_at in range(block // 2):
        total = in_ref[slice_at].astype(exact) + in_ref[block // 2 + slice_at].astype(exact)
        for slot in range(2):
            at = (slot * (block // 2) + slice_at) * (ff // 2)
            out_ref[:, at : at + ff // 2] = total[:, slot * (ff // 2) : (slot + 1) * (ff // 2)]


def collect_hidden(terms_in):
    block, chunk, ff = terms_in.shape
    return pl.pallas_call(
        collect_hidden_kernel,
        out_shape=jax.ShapeDtypeStruct((chunk, block // 2 * ff), exact),
        compiler_params=params(32),
        name="collect_hidden",
    )(terms_in)


def attend_kernel(hd, coef, q_ref, k_ref, v_ref, o_ref, lse_ref, vt_ref):
    @pl.when(pl.program_id(0) == 0)
    def _():
        vt_ref[...] = v_ref[...].T

    s = dot(k_ref[...], q_ref[...], 1, 1)
    top = jnp.max(s, axis=0, keepdims=True)
    e = jnp.exp2((s - top) * coef)
    total = jnp.sum(e, axis=0, keepdims=True)
    o = dot(vt_ref[...], e.astype(low), 1, 0) / total
    o = o.astype(low)
    for piece in range(o_ref.shape[0]):
        o_ref[piece] = o[:hd, piece * lanes : (piece + 1) * lanes]
    lse_ref[0] = top * coef + jnp.log2(total)


def attend(q, q_at, k, k_at, v, v_at, hd, rows):
    tokens, keys = q.shape[0], k.shape[0]
    coef = math.log2(math.e) / hd**0.5
    steps = tokens // rows
    return pl.pallas_call(
        functools.partial(attend_kernel, hd, coef),
        grid=(steps,),
        in_specs=[
            pl.BlockSpec((rows, lanes), lambda i: (i, q_at)),
            pl.BlockSpec((keys, lanes), lambda i: (0, k_at)),
            pl.BlockSpec((keys, lanes), lambda i: (0, v_at)),
        ],
        out_specs=[
            pl.BlockSpec((rows // lanes, hd, lanes), lambda i: (i, 0, 0)),
            pl.BlockSpec((1, 1, rows), lambda i: (i, 0, 0)),
        ],
        out_shape=[
            jax.ShapeDtypeStruct((tokens // lanes, hd, lanes), low),
            jax.ShapeDtypeStruct((steps, 1, rows), exact),
        ],
        scratch_shapes=[pltpu.VMEM((lanes, keys), low)],
        compiler_params=params(48),
        cost_estimate=small_cost,
        name="attend",
    )(q, k, v)


def attend_back_kernel(hd, coef, scale, span, q_ref, k_ref, v_ref, do_ref, lse_ref, out_ref, sum_ref, kt_ref, dk_sum, dv_sum):
    step = pl.program_id(0)
    rows = q_ref.shape[0]

    @pl.when(step == 0)
    def _():
        kt_ref[...] = k_ref[...].T
        dk_sum[...] = jnp.zeros_like(dk_sum)
        dv_sum[...] = jnp.zeros_like(dv_sum)
        sum_ref[...] = jnp.zeros_like(sum_ref)

    pieces = do_ref.shape[0]
    dot_t = jnp.concatenate([do_ref[piece] for piece in range(pieces)], axis=1)
    fill = jnp.zeros((lanes - hd, dot_t.shape[1]), low)
    dot_t = jnp.concatenate([dot_t, fill], axis=0)
    q = q_ref[...]
    s = dot(k_ref[...], q, 1, 1)
    p = jnp.exp2(s * coef - lse_ref[0])
    dp = dot(v_ref[...], dot_t, 1, 0)
    r = jnp.sum(p * dp, axis=0, keepdims=True)
    ds = (p * (dp - r)).astype(low)
    dv_sum[...] += dot(p.astype(low), dot_t.T, 1, 0)
    dk_sum[...] += dot(ds, q, 1, 0)
    dq = dot(kt_ref[...], ds, 1, 0) * scale
    head = lax.broadcasted_iota(jnp.int32, dq.shape, 0) < hd
    dq = jnp.where(head, dq, 0.0).T.astype(low)
    out_ref[pl.ds(pl.multiple_of(span + step * rows, rows), rows), :lanes] = dq.astype(out_ref.dtype)
    sum_ref[0:1, :lanes] += jnp.sum(dq.astype(exact), axis=0, keepdims=True)

    @pl.when(step == pl.num_programs(0) - 1)
    def _():
        head = lax.broadcasted_iota(jnp.int32, dk_sum.shape, 1) < hd
        dk = jnp.where(head, dk_sum[...] * scale, 0.0)
        dv = dv_sum[...].astype(out_ref.dtype)
        out_ref[:, lanes : 2 * lanes] = dk.astype(out_ref.dtype)
        out_ref[:, 2 * lanes :] = dv
        sum_ref[0:1, 2 * lanes :] = jnp.sum(dv.astype(exact), axis=0, keepdims=True)


def attend_back(q, q_at, k, k_at, v, v_at, do, lse, hd, rows, span, kind):
    tokens, keys = q.shape[0], k.shape[0]
    scale = 1.0 / hd**0.5
    coef = math.log2(math.e) * scale
    steps = tokens // rows
    return pl.pallas_call(
        functools.partial(attend_back_kernel, hd, coef, scale, span),
        grid=(steps,),
        in_specs=[
            pl.BlockSpec((rows, lanes), lambda i: (i, q_at)),
            pl.BlockSpec((keys, lanes), lambda i: (0, k_at)),
            pl.BlockSpec((keys, lanes), lambda i: (0, v_at)),
            pl.BlockSpec((rows // lanes, hd, lanes), lambda i: (i, 0, 0)),
            pl.BlockSpec((1, 1, rows), lambda i: (i, 0, 0)),
        ],
        out_specs=[pl.BlockSpec((keys, 3 * lanes), lambda i: (0, 0)), pl.BlockSpec((8, 3 * lanes), lambda i: (0, 0))],
        out_shape=[jax.ShapeDtypeStruct((keys, 3 * lanes), kind), jax.ShapeDtypeStruct((8, 3 * lanes), exact)],
        scratch_shapes=[
            pltpu.VMEM((lanes, keys), low),
            pltpu.VMEM((keys, lanes), exact),
            pltpu.VMEM((keys, lanes), exact),
        ],
        compiler_params=params(56),
        cost_estimate=small_cost,
        name="attend_back",
    )(q, k, v, do, lse)


def body(
    hidden_in,
    clip_lengths,
    ln1_gain,
    ln1_bias,
    w_query,
    b_query,
    w_key,
    w_value,
    b_value,
    w_out,
    b_out,
    ln2_gain,
    ln2_bias,
    w_fc1,
    b_fc1,
    w_fc2,
    b_fc2,
    cotangent,
):
    micro, rows, width = hidden_in.shape
    at = Layout(micro)
    place = at.place
    hd = width // heads
    own = 2 * rows
    tokens = at.half * own
    clips = clip_lengths.shape[1]
    chunk = width // at.block
    step_rows = 256

    vectors = [at.to_block(v) for v in (ln1_gain, ln1_bias, b_query, b_value, b_out, ln2_gain, ln2_bias, b_fc2)]
    ff_bias = at.to_block(b_fc1)
    ff_rows = ff_bias.shape[0]
    first, second = pack(place, hidden_in, jnp.stack(vectors), ff_bias[None], at.to_block(w_out))
    second = at.partner(second)
    w_in = jnp.stack([at.to_block(w) for w in (w_query, w_key, w_value)], axis=1)
    w_in = w_in.reshape(chunk, 3, heads, hd).transpose(2, 0, 1, 3).reshape(heads, chunk, 3 * hd)
    w1 = at.to_block(w_fc1)
    ff = w1.shape[1] // heads
    w1 = w1.reshape(chunk, 2, heads, ff // 2).transpose(2, 0, 1, 3).reshape(heads, chunk, ff)
    w1 = jnp.concatenate([w1] * micro, axis=0)
    w_in = jnp.concatenate([w_in] * micro, axis=0)
    lower = jnp.concatenate([lax.dynamic_index_in_dim(cotangent, 1 - at.mine, 0, False), at.to_block(w_fc2)], axis=0)

    second, w_in, w1, lower = together(second, w_in, w1, lower)
    x_own, small, wo, *parts = arrange(place, first, second, rows)
    wo = at.gather_half(wo).reshape(heads, 2, chunk, width).transpose(1, 0, 2, 3).reshape(width, width)
    w_in = at.exchange_block(w_in)
    parts[2] = jnp.concatenate([parts[2], small[None], at.swapped(small, 1)[None]], axis=1)
    c1 = small.reshape(2, extra_rows, width)[:, 0, lanes : lanes + ff_rows].reshape(1, 2 * ff_rows).astype(exact)
    marks = []
    mine, others = at.gather_tree(parts, marks)

    lower, w1 = together(lower, w1, w_in, marks[1])[:2]
    lower = at.partner(lower)
    w1 = at.exchange_block(w1)
    w_in = w_in.reshape(width, 3 * hd)

    lengths = lax.dynamic_index_in_dim(clip_lengths, at.mine, 0, False)
    ends = jnp.cumsum(lengths)
    where_at = jnp.arange(tokens, dtype=jnp.int32).reshape(2, heads, rows).transpose(1, 0, 2).reshape(tokens)
    where_at = at.me // at.block * tokens + where_at
    ids = jnp.sum((ends[None, :] <= where_at[:, None]).astype(jnp.int32), axis=1).reshape(8, 2, own, 1)

    before = project(place, False, mine, ids, w_in, (), hd, clips, own, chunk)
    a1, qkv, table = project(place, True, others, ids, w_in, before, hd, clips, own, chunk)
    a1 = a1.reshape(tokens, width)
    qkv = qkv.reshape(tokens, 3 * lanes)
    span = 0
    qkv_at = (qkv, 0, qkv, 1, qkv, 2)
    if at.blocks > 1:
        span = tokens // 2
        ahead = [(d, d + at.block) for d in range(at.count - at.block)]
        behind = [(d + at.block, d) for d in range(at.count - at.block)]
        nothing = jnp.where(jnp.arange(2 * lanes)[None] == hd + clips, 1.0, 0.0).astype(low)
        kv = qkv[:, lanes:]
        slots = kv.reshape(heads, 2, rows, 2 * lanes)
        before = at.send(slots[:, 1].reshape(span, 2 * lanes), ahead)
        after = at.send(slots[:, 0].reshape(span, 2 * lanes), behind)
        before = jnp.where(at.me < at.block, nothing, before)
        after = jnp.where(at.me >= at.count - at.block, nothing, after)
        kv = jnp.concatenate([before, kv, after], axis=0)
        qkv_at = (qkv, 0, kv, 0, kv, 1)
    o_head, lse = attend(*qkv_at, hd, step_rows)
    o_head, lse, lower, w1 = together(o_head, lse, lower, w1)
    w1 = w1.reshape(width, ff)
    g_kept = lax.dynamic_index_in_dim(cotangent, at.mine, 0, False)
    g_own = jnp.concatenate(at.ordered(g_kept, lower[:rows]), axis=0)
    w2 = jnp.concatenate(at.ordered(at.to_block(w_fc2), lower[rows:]), axis=0)
    g_all = at.gather_half(g_own)
    o_own = at.exchange_half(o_head)

    x2, *parts = join(x_own, o_own, wo, table)
    mine, others = at.gather_tree(parts)

    g_split = g_all.reshape(8, 2, own, width)
    *before, kept, sum_c = feed(place, False, mine, g_split, w1, w2, c1, (), own, exact)
    hid, du, away, sum_c2 = feed(place, True, others, g_split, w1, w2, c1, before, own, low)
    marks, terms_w1 = [], []
    low_hid, low_du = hid.reshape(tokens, ff), du.reshape(tokens, ff)

    def output_terms(marks):
        late = tie(low_hid, marks[0])
        terms_w1.append(dot(late, w2, 1, 0).astype(low))
        terms_w1.append(assemble(place, (tie(mine[0], marks[0]), *mine[1:]), others, own))
        return terms_w1

    def hidden_terms(marks):
        terms_w1.append(dot(tie(terms_w1[1], marks[1]).reshape(tokens, width), low_du, 0, 0).astype(low))
        return terms_w1[2:]

    kept, got = at.reduce_half(away, kept, marks, {1: output_terms, 2: hidden_terms})
    y = lax.psum_scatter(terms_w1[0], "dev", scatter_dimension=0, tiled=True, axis_index_groups=at.halves)
    d_w1 = at.exchange_block(terms_w1[2].reshape(at.block, chunk, ff))
    d_w2 = dot(tie(low_hid, marks[2]), g_all.reshape(tokens, width), 0, 0).astype(low)
    *sums, d_w2 = together(*kept, *got, d_w2)
    kept, got = sums[:3], sums[3:]

    dx2, ga_own, do_own, sum2 = second_back(kept, got, x2, g_own, table, wo, hd)
    do_head = at.exchange_half(do_own)
    ga_sent, d_w2 = together(ga_own, d_w2, do_own)[:2]
    ga = at.gather_half(ga_sent).reshape(tokens, width)
    do_head, d_w1, d_w2 = together(do_head, d_w1, d_w2)
    back_w2 = at.exchanged(d_w2.reshape(2, -1, width))

    kind = low if at.blocks == 1 else exact
    dqkv, sum_in = attend_back(*qkv_at, do_head, lse, hd, step_rows, span, kind)
    if at.blocks > 1:
        dkv = dqkv[:, lanes:]
        to_before = at.send(dkv[:span].astype(low), behind).astype(exact)
        to_after = at.send(dkv[span + tokens :].astype(low), ahead).astype(exact)
        halo = jnp.stack([t.reshape(heads, rows, 2 * lanes) for t in (to_after, to_before)], axis=1)
        dkv = dkv[span : span + tokens] + halo.reshape(tokens, 2 * lanes)
        dqkv = jnp.concatenate([dqkv[span : span + tokens, :lanes], dkv], axis=1).astype(low)
        sum_in = jnp.broadcast_to(jnp.sum(dqkv.astype(exact), axis=0, keepdims=True), (8, 3 * lanes))
    dqkv, sum_in, *back_w2 = together(dqkv, sum_in, *back_w2)
    split = dqkv.reshape(8, 2, own, 3 * lanes)
    w_pad = jnp.pad(w_in.reshape(width, 3, hd), ((0, 0), (0, 0), (0, lanes - hd))).reshape(width, 3 * lanes)
    away = terms(place, True, split, w_pad, 1, low)
    marks = []
    store = []

    def projections(marks):
        late = tie(dqkv, away)
        store.append(lay_out(place, dot(a1, late, 0, 0), sum2, sum_in, sum_c, sum_c2, hd, chunk, at.block))
        return store

    kept, got = at.reduce_half(away, terms(place, False, split, w_pad, 1, exact), marks, {0: projections})
    ga, o_late, y = together(ga, o_head, y, marks[1])[:3]

    d_in = at.exchange_block(store[0])
    d_wo = jnp.einsum("ckt,ctn->kn", o_late, ga.reshape(at.half, own, width), preferred_element_type=exact)
    back_wo = at.send_rows_back(d_wo.astype(low).reshape(2, chunk, width))
    layer_out = at.exchanged((x2 + (y.astype(exact) + table[7])).astype(low).reshape(2, rows, width))
    kept_first, d_in, *moved = together(kept[0], d_in, *back_wo, *layer_out)
    kept = (kept_first, *kept[1:])
    back_wo, layer_out = moved[:2], moved[2:]
    grad_w2 = at.from_block(back_w2[0].astype(exact) + back_w2[1].astype(exact))
    grad_w1 = at.from_block(collect_hidden(d_w1))
    grad_wo = at.from_block(back_wo[0].astype(exact) + back_wo[1].astype(exact))
    *grads, vec = collect(d_in, hd, chunk)
    grad_wq, grad_wk, grad_wv = (at.from_block(v) for v in grads)
    pieces = [at.from_block(vec[i, :chunk]) for i in range(6)]
    grad_g2, grad_b2, grad_bo, grad_bf2, grad_bq, grad_bv = pieces
    grad_c1 = at.from_block(vec[0, chunk : chunk + ff_rows])

    dx, vec = first_back(kept, got, x_own, dx2, table, chunk, at.block)
    input_grad = at.exchanged(dx.reshape(2, rows, width))
    layer_out, input_grad = (jnp.stack(at.ordered(*v)).astype(exact) for v in (layer_out, input_grad))
    vec = jnp.sum(at.exchange_block(vec), axis=(0, 1))
    grad_g1 = at.from_block(vec[:chunk])
    grad_b1 = at.from_block(vec[lanes // 2 : lanes // 2 + chunk])
    return (
        layer_out,
        input_grad,
        grad_g1,
        grad_b1,
        grad_wq,
        grad_bq,
        grad_wk,
        grad_wv,
        grad_bv,
        grad_wo,
        grad_bo,
        grad_g2,
        grad_b2,
        grad_w1,
        grad_c1,
        grad_w2,
        grad_bf2,
    )


def solution(mesh):
    tokens, vector, matrix = P(None, "dev", None), P("dev"), P("dev", None)
    grads = (vector, vector, matrix, vector, matrix, matrix, vector, matrix, vector, vector, vector, matrix, vector, matrix, vector)
    return jax.shard_map(
        body,
        mesh=mesh,
        in_specs=(tokens, P()) + grads + (tokens,),
        out_specs=(tokens, tokens) + grads,
        check_vma=False,
    )
```

```python
import functools
import math

import jax
import jax.numpy as jnp
from jax import lax
from jax.experimental import pallas as pl
from jax.experimental.pallas import tpu as pltpu
from jax.sharding import PartitionSpec as P

eps = 1e-05
heads = 16
low = jnp.bfloat16
exact = jnp.float32
far = -1e30
lanes = 128
extra_rows = 8


def dot(a, b, ca, cb):
    return lax.dot_general(a, b, (((ca,), (cb,)), ((), ())), preferred_element_type=exact)


def normalized(v):
    mean = jnp.mean(v, axis=-1, keepdims=True)
    cent = v - mean
    inverse = lax.rsqrt(jnp.mean(cent * cent, axis=-1, keepdims=True) + eps)
    return cent * inverse, inverse


def norm_back(unit, inverse, gain, grad):
    scaled = grad * gain
    along = jnp.mean(scaled * unit, axis=-1, keepdims=True)
    return inverse * (scaled - jnp.mean(scaled, axis=-1, keepdims=True) - unit * along)


def tie(value, *others):
    return lax.optimization_barrier((value,) + others)[0]


def together(*values):
    return lax.optimization_barrier(values)


class Layout:
    def __init__(self, micro):
        self.count = lax.axis_size("dev")
        self.half = heads
        self.block = micro * heads
        self.blocks = self.count // self.block
        self.me = lax.axis_index("dev")
        self.rank = self.me % self.block
        self.mine = self.rank // self.half
        self.head = self.rank % self.half
        self.odd = self.rank % 2
        bits = [(self.me // bit) % 2 for bit in (1, 2, 4, 8)]
        self.place = jnp.stack(bits + [self.mine, self.head, self.odd]).astype(jnp.int32)
        self.halves = [list(range(s, s + self.half)) for s in range(0, self.count, self.half)]
        self.whole = [list(range(s, s + self.block)) for s in range(0, self.count, self.block)]
        self.rows = [list(range(s, s + self.blocks)) for s in range(0, self.count, self.blocks)]
        first = [d // self.half % 2 for d in range(self.count)]
        base = [d // self.block * self.block + 2 * (d % self.half) for d in range(self.count)]
        self.even_first = [(d, base[d] + first[d]) for d in range(self.count)]
        self.odd_first = [(d, base[d] + 1 - first[d]) for d in range(self.count)]

    def send(self, value, pairs):
        return lax.ppermute(value, "dev", pairs)

    def swapped(self, value, bit):
        return self.send(value, [(d, d ^ bit) for d in range(self.count)])

    def to_block(self, value):
        if self.blocks == 1:
            return value
        value = lax.all_gather(value, "dev", axis=0, tiled=True, axis_index_groups=self.rows)
        return self.send(value, [(d, d % self.blocks * self.block + d // self.blocks) for d in range(self.count)])

    def from_block(self, value):
        if self.blocks == 1:
            return value
        value = self.send(value, [(d % self.blocks * self.block + d // self.blocks, d) for d in range(self.count)])
        return lax.psum_scatter(value, "dev", scatter_dimension=0, tiled=True, axis_index_groups=self.rows)

    def partner(self, value):
        return self.swapped(value, self.half)

    def ordered(self, kept, got):
        return jnp.where(self.mine == 0, kept, got), jnp.where(self.mine == 0, got, kept)

    def exchanged(self, value):
        kept = lax.dynamic_index_in_dim(value, self.mine, 0, False)
        return kept, self.partner(lax.dynamic_index_in_dim(value, 1 - self.mine, 0, False))

    def send_rows_back(self, value):
        first = lax.dynamic_index_in_dim(value, self.mine, 0, False)
        second = lax.dynamic_index_in_dim(value, 1 - self.mine, 0, False)
        return self.send(first, self.even_first), self.send(second, self.odd_first)

    def gather_half(self, value):
        return lax.all_gather(value, "dev", axis=0, axis_index_groups=self.halves)

    def exchange_half(self, value):
        return lax.all_to_all(value, "dev", 0, 0, tiled=True, axis_index_groups=self.halves)

    def exchange_block(self, value):
        return lax.all_to_all(value, "dev", 0, 0, tiled=True, axis_index_groups=self.whole)

    def gather_tree(self, parts, marks=None, last=()):
        for stage in range(2):
            got = [self.swapped(piece, order[stage]) for piece, order in zip(parts, part_orders)]
            parts = merge(parts, got)
            if marks is not None:
                marks.append(parts[0])
        if last:
            parts = [tie(parts[0], *last), *parts[1:]]
        got = [self.swapped(piece, order[2]) for piece, order in zip(parts, part_orders)]
        other = [self.swapped(piece, 1) for piece in (*parts, *got)]
        return (*parts, *got), other

    def reduce_half(self, away, kept, marks=None, before=None):
        got = [self.swapped(away, 1)]
        kept = [kept]
        for stage in range(3):
            if before and stage in before:
                got = [tie(got[0], *before[stage](marks)), *got[1:]]
            away, kept = split_terms(self.place, stage, kept, got)
            if marks is not None:
                marks.append(away[0])
            got = [self.swapped(piece, order[stage]) for piece, order in zip(away, part_orders)]
        return kept, got


small_cost = pl.CostEstimate(flops=1 << 10, bytes_accessed=1 << 10, transcendentals=0)


def params(megabytes):
    return pltpu.CompilerParams(vmem_limit_bytes=megabytes << 20)


part_orders = ((8, 4, 2), (4, 2, 8), (2, 8, 4))


def part_bounds(tokens):
    cut = tokens * 3 // 8 // 16 * 16
    return ((0, cut), (cut, 2 * cut), (2 * cut, tokens))


def split_kernel(stage, place_ref, *refs):
    place = {bit: place_ref[i] for i, bit in enumerate((1, 2, 4, 8))}
    if stage == 0:
        kept_ref, got_ref = refs[:2]
        outs = refs[2:]
        bounds = part_bounds(kept_ref.shape[1])
    else:
        outs = refs[6:]
    for part, order in enumerate(part_orders):
        left = [bit for bit in (8, 4, 2) if bit not in order[:stage]]
        at = left.index(order[stage])
        below = 1 << (len(left) - 1 - at)
        for half, side in ((0, 1 - place[order[stage]]), (1, place[order[stage]])):
            out_ref = outs[part + 3 * half]
            for j in range(out_ref.shape[0]):
                index = (j // below * 2 + side) * below + j % below
                if stage == 0:
                    start, end = bounds[part]
                    term = kept_ref[index, start:end].astype(exact) + got_ref[index, start:end].astype(exact)
                else:
                    term = refs[part][index].astype(exact) + refs[3 + part][index].astype(exact)
                out_ref[j] = term.astype(out_ref.dtype)


def split_terms(place, stage, kept, got):
    width = kept[0].shape[-1]
    bounds = part_bounds(kept[0].shape[1]) if stage == 0 else [(0, k.shape[1]) for k in kept]
    count = kept[0].shape[0] // 2
    cols = 256 if stage == 0 else 640
    spec = lambda n, t: pl.BlockSpec((n, t, cols), lambda i, p: (0, 0, i))
    outs = [(count, end - start) for start, end in bounds]
    res = pl.pallas_call(
        functools.partial(split_kernel, stage),
        grid_spec=pltpu.PrefetchScalarGridSpec(
            num_scalar_prefetch=1,
            grid=(width // cols,),
            in_specs=[spec(*v.shape[:2]) for v in (*kept, *got)],
            out_specs=[spec(*o) for o in outs] * 2,
        ),
        out_shape=[jax.ShapeDtypeStruct(o + (width,), kind) for kind in (low, exact) for o in outs],
        compiler_params=params(10),
        cost_estimate=small_cost,
        name="split_terms",
    )(place, *kept, *got)
    return res[:3], res[3:]


def last_sum(refs):
    return jnp.concatenate([refs[i][0].astype(exact) + refs[3 + i][0].astype(exact) for i in range(3)], axis=0)


def pack_kernel(place_ref, x_ref, v_ref, c_ref, w_ref, first_ref, second_ref):
    rows, width = x_ref.shape[1:]
    mine = place_ref[4]
    fill = jnp.zeros((v_ref.shape[0], width - v_ref.shape[1]), exact)
    small = jnp.concatenate([v_ref[...].astype(exact), fill], axis=1)
    c = jnp.concatenate([c_ref[...].astype(exact), jnp.zeros((1, width - lanes - c_ref.shape[1]), exact)], axis=1)
    c = jnp.concatenate([jnp.zeros((1, lanes), exact), c], axis=1)
    row = lax.broadcasted_iota(jnp.int32, small.shape, 0)
    small = small + jnp.where(row == 0, c, 0.0)
    tail = jnp.concatenate([small, w_ref[...].astype(exact)], axis=0).astype(low)
    for out_ref, index in ((first_ref, mine), (second_ref, 1 - mine)):
        out_ref[:rows] = x_ref[index]
        out_ref[rows:] = tail


def pack(place, x, vectors, c, w):
    rows, width = x.shape[1:]
    out = jax.ShapeDtypeStruct((rows + extra_rows + w.shape[0], width), low)
    return pl.pallas_call(
        pack_kernel,
        grid_spec=pltpu.PrefetchScalarGridSpec(
            num_scalar_prefetch=1,
            grid=(1,),
            in_specs=[whole_spec(v) for v in (x, vectors, c, w)],
            out_specs=[whole_spec(out)] * 2,
        ),
        out_shape=[out, out],
        compiler_params=params(6),
        name="pack",
    )(place, x, vectors, c, w)


def arrange_kernel(rows, place_ref, first_ref, second_ref, x_ref, small_ref, w_ref, *part_refs):
    mine = place_ref[4]
    for side, refs in enumerate(((first_ref, second_ref), (second_ref, first_ref))):

        @pl.when(mine == side)
        def _():
            x = jnp.concatenate([ref[:rows] for ref in refs], axis=0)
            x_ref[...] = x
            tail = [ref[rows:].astype(exact) for ref in refs]
            small_ref[...] = jnp.concatenate([t[:extra_rows] for t in tail], axis=0).astype(low)
            w_ref[...] = jnp.concatenate([t[extra_rows:] for t in tail], axis=0).astype(low)
            for part_ref, (start, end) in zip(part_refs, part_bounds(2 * rows)):
                part_ref[0] = x[start:end]


def arrange(place, first, second, rows):
    width = first.shape[1]
    shapes = [(2 * rows, width), (2 * extra_rows, width), (2 * (first.shape[0] - rows - extra_rows), width)]
    shapes += [(1, end - start, width) for start, end in part_bounds(2 * rows)]
    outs = [jax.ShapeDtypeStruct(shape, low) for shape in shapes]
    return pl.pallas_call(
        functools.partial(arrange_kernel, rows),
        grid_spec=pltpu.PrefetchScalarGridSpec(
            num_scalar_prefetch=1,
            grid=(1,),
            in_specs=[whole_spec(first), whole_spec(second)],
            out_specs=[whole_spec(out) for out in outs],
        ),
        out_shape=outs,
        compiler_params=params(6),
        name="arrange",
    )(place, first, second)


def deal_kernel(hd, q_ref, k_ref, v_ref, w_ref, in_ref, hidden_ref):
    ff = w_ref.shape[1] // heads
    side_by_side = lambda pieces: jnp.concatenate([piece.astype(exact) for piece in pieces], axis=1).astype(low)
    for head in range(heads):
        at = [(slot * heads + head) * (ff // 2) for slot in range(2)]
        hidden = side_by_side([w_ref[:, a : a + ff // 2] for a in at])
        columns = side_by_side([ref[:, head * hd : (head + 1) * hd] for ref in (q_ref, k_ref, v_ref)])
        for device in range(head, in_ref.shape[0], heads):
            in_ref[device] = columns
            hidden_ref[device] = hidden


def deal(q, k, v, w, hd, block):
    chunk, ff = q.shape[0], w.shape[1] // heads
    return pl.pallas_call(
        functools.partial(deal_kernel, hd),
        out_shape=[jax.ShapeDtypeStruct((block, chunk, size), low) for size in (3 * hd, ff)],
        compiler_params=params(8),
        name="deal",
    )(q, k, v, w)


def merge_kernel(*refs):
    for i in range(3):
        count = refs[i].shape[0]
        refs[6 + i][:count] = refs[i][...]
        refs[6 + i][count:] = refs[3 + i][...]


def merge(parts, got):
    width = parts[0].shape[2]
    cols = 640
    spec = lambda shape: pl.BlockSpec(shape[:2] + (cols,), lambda i: (0, 0, i))
    outs = [(2 * p.shape[0],) + p.shape[1:] for p in parts]
    return pl.pallas_call(
        merge_kernel,
        grid=(width // cols,),
        in_specs=[spec(v.shape) for v in (*parts, *got)],
        out_specs=[spec(o) for o in outs],
        out_shape=[jax.ShapeDtypeStruct(o, low) for o in outs],
        compiler_params=params(8),
        name="merge",
    )(*parts, *got)


def tree_rows(place_ref, chip, refs, fill):
    mine = place_ref[1] + 2 * place_ref[2] + 4 * place_ref[3]
    apart = chip ^ mine
    step = {8: apart // 4, 4: apart // 2 % 2, 2: apart % 2}
    for part, order in enumerate(part_orders):
        index = 2 * step[order[1]] + step[order[0]]
        for late in range(2):

            @pl.when(step[order[2]] == late)
            def _():
                fill(part, refs[part + 3 * late], index)


def fill_rows(place_ref, chip, refs, out_ref, base, own):
    bounds = part_bounds(own)

    def fill(part, ref, index):
        start, end = bounds[part]
        out_ref[pl.ds(base + start, end - start)] = ref[index, : end - start]

    tree_rows(place_ref, chip, refs, fill)


def whole_spec(v):
    return pl.BlockSpec(v.shape, lambda i, p: (0,) * len(v.shape))


def project_kernel(hd, clips, chunk, first, place_ref, *refs):
    pieces, refs = refs[:6], refs[6:]
    ids_ref, w_ref = refs[:2]
    a_ref, qkv_ref, table_ref, x_scr, bias_ref = refs[-5:]
    step, _, own, width = a_ref.shape

    @pl.when(pl.program_id(0) == 0)
    def _():
        if first:
            tail = part_bounds(own)[2]

            def fill(chip, part, ref, index):
                if part != 2:
                    return
                small = ref[index, tail[1] - tail[0] :].astype(exact)
                for far_core in range(2):
                    for slot in range(2):
                        line = (2 * far_core + slot) * extra_rows
                        piece = small[line : line + extra_rows, :chunk]
                        for core in range(2):

                            @pl.when(place_ref[0] == core)
                            def _():
                                at = (heads * slot + 2 * chip + (core ^ far_core)) * chunk
                                table_ref[:, at : at + chunk] = piece

            for chip in range(8):
                tree_rows(place_ref, chip, pieces, functools.partial(fill, chip))
        else:
            table_ref[...] = refs[2][...]
        bias_ref[...] = jnp.zeros_like(bias_ref)
        for h in range(heads):

            @pl.when(place_ref[5] == h)
            def _():
                for line, at in ((2, 0), (3, 2 * lanes)):
                    bias_ref[0:1, at : at + hd] = table_ref[line : line + 1, h * hd : (h + 1) * hd]

    for j in range(step):
        fill_rows(place_ref, pl.program_id(0) * step + j, pieces, x_scr, j * own, own)
    unit, _ = normalized(x_scr[...].astype(exact))
    a = (unit * table_ref[0:1] + table_ref[1:2]).astype(low)
    a_ref[...] = a.reshape(a_ref.shape)
    qkv = dot(a, w_ref[...], 1, 0)
    fill = jnp.zeros((step * own, lanes - hd), exact)
    qkv = [v for i in range(3) for v in (qkv[:, i * hd : (i + 1) * hd], fill)]
    qkv = jnp.concatenate(qkv, axis=1) + bias_ref[0:1]
    column = lax.broadcasted_iota(jnp.int32, (step * own, lanes), 1) - hd
    match = ids_ref[...].reshape(step * own, 1) == column
    marked = (column >= 0) & (column <= clips)
    q = qkv[:, :lanes] + jnp.where(marked & ~match, far, 0.0)
    k = qkv[:, lanes : 2 * lanes] + jnp.where(marked & match, 1.0, 0.0)
    qkv = jnp.concatenate([q, k, qkv[:, 2 * lanes :]], axis=1).astype(low)
    qkv_ref[...] = qkv.reshape(qkv_ref.shape)


def project(place, other, pieces, ids, w, before, hd, clips, own, chunk):
    width = w.shape[0]
    step = 4
    side = (lambda p: 1 - p[0]) if other else (lambda p: p[0])
    pick = lambda size: pl.BlockSpec((step, 1, own, size), lambda i, p: (i, side(p), 0, 0))
    table = jax.ShapeDtypeStruct((extra_rows, width), exact)
    ahead = [before[2], *before[:2]] if before else []
    return pl.pallas_call(
        functools.partial(project_kernel, hd, clips, chunk, not before),
        grid_spec=pltpu.PrefetchScalarGridSpec(
            num_scalar_prefetch=1,
            grid=(8 // step,),
            in_specs=[whole_spec(v) for v in pieces]
            + [pick(1), whole_spec(w)]
            + ([whole_spec(table)] + [pl.BlockSpec(memory_space=pl.ANY)] * 2 if before else []),
            out_specs=[pick(width), pick(3 * lanes), whole_spec(table)],
            scratch_shapes=[pltpu.VMEM((step * own, width), low), pltpu.VMEM((8, 3 * lanes), exact)],
        ),
        out_shape=[
            jax.ShapeDtypeStruct((8, 2, own, width), low),
            jax.ShapeDtypeStruct((8, 2, own, 3 * lanes), low),
            table,
        ],
        input_output_aliases={10: 0, 11: 1} if before else {},
        compiler_params=params(30),
        cost_estimate=small_cost,
        name="project",
    )(place, *pieces, ids, w, *ahead)


def join_kernel(x_ref, o_ref, w_ref, table_ref, x2_ref, *part_refs):
    o = o_ref[...].reshape(w_ref.shape[0], o_ref.shape[2])
    x2 = x_ref[...].astype(exact) + (dot(o, w_ref[...], 0, 0) + table_ref[4:5])
    x2_ref[...] = x2
    unit, _ = normalized(x2)
    a2 = (unit * table_ref[5:6] + table_ref[6:7]).astype(low)
    for part_ref, (start, end) in zip(part_refs, part_bounds(x2.shape[0])):
        part_ref[0] = a2[start:end]


def join(x, o, w, table):
    own, width = x.shape
    parts = [jax.ShapeDtypeStruct((1, end - start, width), low) for start, end in part_bounds(own)]
    return pl.pallas_call(
        join_kernel,
        out_shape=[jax.ShapeDtypeStruct(x.shape, exact)] + parts,
        compiler_params=params(10),
        cost_estimate=small_cost,
        name="join",
    )(x, o, w, table)


def assemble_kernel(place_ref, *refs):
    mine, others, out_ref = refs[:6], refs[6:12], refs[12]
    chips, _, own, _ = out_ref.shape
    for j in range(chips):
        chip = pl.program_id(0) * chips + j
        for core, pieces in ((place_ref[0], mine), (1 - place_ref[0], others)):
            bounds = part_bounds(own)

            def fill(part, ref, index):
                start, end = bounds[part]
                out_ref[j, core, start:end] = ref[index]

            tree_rows(place_ref, chip, pieces, fill)


def assemble(place, mine, others, own):
    width = mine[0].shape[2]
    step = 2
    return pl.pallas_call(
        assemble_kernel,
        grid_spec=pltpu.PrefetchScalarGridSpec(
            num_scalar_prefetch=1,
            grid=(8 // step,),
            in_specs=[whole_spec(v) for v in (*mine, *others)],
            out_specs=pl.BlockSpec((step, 2, own, width), lambda i, p: (i, 0, 0, 0)),
        ),
        out_shape=jax.ShapeDtypeStruct((8, 2, own, width), low),
        compiler_params=params(18),
        cost_estimate=small_cost,
        name="assemble",
    )(place, *mine, *others)


def feed_kernel(place_ref, *refs):
    pieces, (g_ref, w1_ref, w2_ref, c_ref) = refs[:6], refs[6:10]
    hid_ref, du_ref, y_ref, da_ref, sum_ref, a_scr = refs[-6:]
    step, own, width = da_ref.shape
    rows = step * own
    for j in range(step):
        fill_rows(place_ref, pl.program_id(0) * step + j, pieces, a_scr, j * own, own)
    w1, w2 = w1_ref[...], w2_ref[...]
    u = dot(a_scr[...], w1, 1, 0) + c_ref[...]
    d_hid = dot(g_ref[...].reshape(rows, width), w2, 1, 1)
    below = 0.5 * (1.0 + lax.erf(u * math.sqrt(0.5)))
    hid = (u * below).astype(low)
    hid_ref[...] = hid.reshape(hid_ref.shape)
    y_ref[...] = dot(hid, w2, 1, 0).reshape(y_ref.shape).astype(low)
    slope = below + u * (jnp.exp(-0.5 * u * u) * (1.0 / math.sqrt(2.0 * math.pi)))
    du = (d_hid * slope).astype(low)
    du_ref[...] = du.reshape(du_ref.shape)
    da_ref[...] = dot(du, w1, 1, 1).reshape(da_ref.shape).astype(da_ref.dtype)

    @pl.when(pl.program_id(0) == 0)
    def _():
        sum_ref[...] = jnp.zeros_like(sum_ref)

    sum_ref[...] += jnp.sum(du.astype(exact), axis=0, keepdims=True)


def feed(place, other, pieces, g, w1, w2, c1, before, own, kind):
    ff, width = w2.shape
    step = 4
    tokens = 8 * own
    side = (lambda p: 1 - p[0]) if other else (lambda p: p[0])
    pick = lambda size: pl.BlockSpec((step, 1, own, size), lambda i, p: (i, side(p), 0, 0))
    shape = lambda size: jax.ShapeDtypeStruct((8, 2, own, size), low)
    row = pl.BlockSpec((1, ff), lambda i, p: (0, 0))
    return pl.pallas_call(
        feed_kernel,
        grid_spec=pltpu.PrefetchScalarGridSpec(
            num_scalar_prefetch=1,
            grid=(8 // step,),
            in_specs=[whole_spec(v) for v in pieces]
            + [pick(width), whole_spec(w1), whole_spec(w2), row]
            + [pl.BlockSpec(memory_space=pl.ANY)] * len(before),
            out_specs=[pick(ff), pick(ff), pick(width), pl.BlockSpec((step, own, width), lambda i, p: (i, 0, 0)), row],
            scratch_shapes=[pltpu.VMEM((step * own, width), low)],
        ),
        out_shape=[
            shape(ff),
            shape(ff),
            shape(width),
            jax.ShapeDtypeStruct((8, own, width), kind),
            jax.ShapeDtypeStruct((1, ff), exact),
        ],
        input_output_aliases={11: 0, 12: 1, 13: 2} if before else {},
        compiler_params=params(34),
        cost_estimate=small_cost,
        name="feed",
    )(place, *pieces, g, w1, w2, c1, *before)


def terms_kernel(contract, place_ref, left_ref, right_ref, out_ref):
    rows = out_ref.shape[0] * out_ref.shape[1]
    left = left_ref[...].reshape(rows, left_ref.shape[-1])
    out_ref[...] = dot(left, right_ref[...], 1, contract).reshape(out_ref.shape).astype(out_ref.dtype)


def terms(place, other, left, right, contract, kind):
    eight, two, own, depth = left.shape
    width = right.shape[1 - contract]
    step = 2
    side = (lambda p: 1 - p[0]) if other else (lambda p: p[0])
    return pl.pallas_call(
        functools.partial(terms_kernel, contract),
        grid_spec=pltpu.PrefetchScalarGridSpec(
            num_scalar_prefetch=1,
            grid=(eight // step,),
            in_specs=[
                pl.BlockSpec((step, 1, own, depth), lambda i, p: (i, side(p), 0, 0)),
                pl.BlockSpec(right.shape, lambda i, p: (0, 0)),
            ],
            out_specs=pl.BlockSpec((step, own, width), lambda i, p: (i, 0, 0)),
        ),
        out_shape=jax.ShapeDtypeStruct((eight, own, width), kind),
        compiler_params=params(12),
        cost_estimate=small_cost,
        name="terms",
    )(place, left, right)


def rows_of(values, width):
    fill = jnp.zeros((8 - len(values), width), exact)
    return jnp.concatenate(values + [fill], axis=0)


def second_back_kernel(*refs):
    da2 = last_sum(refs[:6])
    x2_ref, g_ref, table_ref, w_ref, dx2_ref, ga_ref, do_ref, sum_ref = refs[6:]
    unit, inverse = normalized(x2_ref[...])
    g = g_ref[...].astype(exact)
    dx2 = g + norm_back(unit, inverse, table_ref[5:6], da2)
    dx2_ref[...] = dx2
    ga = dx2.astype(low)
    ga_ref[...] = ga
    do_ref[...] = dot(w_ref[...], ga, 1, 1).astype(low).reshape(do_ref.shape)
    total = lambda v: jnp.sum(v, axis=0, keepdims=True)
    sum_ref[...] = rows_of([total(da2 * unit), total(da2), total(ga.astype(exact)), total(g)], ga.shape[1])


def second_back(kept, got, x2, g, table, w, hd):
    own, width = x2.shape
    return pl.pallas_call(
        second_back_kernel,
        out_shape=[
            jax.ShapeDtypeStruct((own, width), exact),
            jax.ShapeDtypeStruct((own, width), low),
            jax.ShapeDtypeStruct((heads, hd, own), low),
            jax.ShapeDtypeStruct((8, width), exact),
        ],
        compiler_params=params(12),
        cost_estimate=small_cost,
        name="second_back",
    )(*kept, *got, x2, g, table, w)


def first_back_kernel(chunk, *refs):
    da1 = last_sum(refs[:6])
    x_ref, dx2_ref, table_ref, dx_ref, vec_ref = refs[6:]
    unit, inverse = normalized(x_ref[...].astype(exact))
    dx = dx2_ref[...] + norm_back(unit, inverse, table_ref[0:1], da1)
    dx_ref[...] = dx.astype(low)
    total = lambda v: jnp.sum(v, axis=0, keepdims=True)
    rows = [total(da1 * unit), total(da1)]
    fill = jnp.zeros((1, lanes // 2 - chunk), exact)
    for device in range(vec_ref.shape[0]):
        part = slice(device * chunk, (device + 1) * chunk)
        vec_ref[device] = jnp.concatenate([rows[0][:, part], fill, rows[1][:, part], fill], axis=1)


def first_back(kept, got, x, dx2, table, chunk, block):
    return pl.pallas_call(
        functools.partial(first_back_kernel, chunk),
        out_shape=[jax.ShapeDtypeStruct(x.shape, low), jax.ShapeDtypeStruct((block, 1, lanes), exact)],
        compiler_params=params(8),
        name="first_back",
    )(*kept, *got, x, dx2, table)


def lay_out_kernel(hd, chunk, place_ref, in_ref, sum2_ref, sum_in_ref, sum_c_ref, sum_c2_ref, out_ref):
    block = out_ref.shape[0]
    head = place_ref[5]
    c = sum_c_ref[...] + sum_c2_ref[...]
    ff_rows = c.shape[1] // 2
    rest = jnp.zeros((8, 3 * hd - chunk), exact)
    zeros = jnp.zeros((2, chunk), exact)
    narrow = jnp.concatenate([in_ref[:, i * lanes : i * lanes + hd] for i in range(3)], axis=1)
    pad = jnp.zeros((1, 3 * hd - chunk - ff_rows), exact)
    row = lax.broadcasted_iota(jnp.int32, (8, 3 * hd), 0)
    for device in range(block):
        part = slice(device * chunk, (device + 1) * chunk)
        small = jnp.concatenate([sum2_ref[0:4, part], zeros, zeros], axis=0)
        small = jnp.concatenate([small, rest], axis=1)
        slot = device % 2
        cols = slice(slot * chunk, (slot + 1) * chunk)
        for line, at in ((4, 0), (5, 2 * lanes)):
            own = jnp.concatenate([sum_in_ref[0:1, at : at + hd][:, cols], rest[0:1]], axis=1)
            small += jnp.where((row == line) & (head == device // 2), own, 0.0)
        slot = device // heads
        own = jnp.concatenate([zeros[0:1], c[:, slot * ff_rows : (slot + 1) * ff_rows], pad], axis=1)
        small += jnp.where((row == 0) & (head == device % heads), own, 0.0)
        out_ref[device] = jnp.concatenate([narrow[part], small], axis=0).astype(low)


def lay_out(place, d_in, sum2, sum_in, sum_c, sum_c2, hd, chunk, block):
    smem = pl.BlockSpec(memory_space=pltpu.SMEM)
    vmem = pl.BlockSpec(memory_space=pltpu.VMEM)
    return pl.pallas_call(
        functools.partial(lay_out_kernel, hd, chunk),
        in_specs=[smem] + [vmem] * 5,
        out_shape=jax.ShapeDtypeStruct((block, chunk + 8, 3 * hd), low),
        compiler_params=params(12),
        name="lay_out",
    )(place, d_in, sum2, sum_in, sum_c, sum_c2)


def collect_kernel(hd, *refs):
    in_ref, *out_refs, small_ref = refs
    chunk = out_refs[0].shape[0]
    block = in_ref.shape[0]
    small = jnp.zeros(small_ref.shape, exact)
    for head in range(block // 2):
        first, second = in_ref[head].astype(exact), in_ref[block // 2 + head].astype(exact)
        total = first + second
        small += total[chunk:]
        for i, out_ref in enumerate(out_refs):
            out_ref[:, head * hd : (head + 1) * hd] = total[:chunk, i * hd : (i + 1) * hd]
    small_ref[...] = small


def collect(terms_in, hd, chunk):
    block = terms_in.shape[0]
    matrix = jax.ShapeDtypeStruct((chunk, block // 2 * hd), exact)
    return pl.pallas_call(
        functools.partial(collect_kernel, hd),
        out_shape=[matrix] * 3 + [jax.ShapeDtypeStruct((8, 3 * hd), exact)],
        compiler_params=params(8),
        name="collect",
    )(terms_in)


def collect_hidden_kernel(in_ref, out_ref):
    block, _, ff = in_ref.shape
    for slice_at in range(block // 2):
        total = in_ref[slice_at].astype(exact) + in_ref[block // 2 + slice_at].astype(exact)
        for slot in range(2):
            at = (slot * (block // 2) + slice_at) * (ff // 2)
            out_ref[:, at : at + ff // 2] = total[:, slot * (ff // 2) : (slot + 1) * (ff // 2)]


def collect_hidden(terms_in):
    block, chunk, ff = terms_in.shape
    return pl.pallas_call(
        collect_hidden_kernel,
        out_shape=jax.ShapeDtypeStruct((chunk, block // 2 * ff), exact),
        compiler_params=params(8),
        name="collect_hidden",
    )(terms_in)


def attend_kernel(hd, coef, q_ref, k_ref, v_ref, o_ref, lse_ref, vt_ref):
    @pl.when(pl.program_id(0) == 0)
    def _():
        vt_ref[...] = v_ref[...].T

    s = dot(k_ref[...], q_ref[...], 1, 1)
    top = jnp.max(s, axis=0, keepdims=True)
    e = jnp.exp2((s - top) * coef)
    total = jnp.sum(e, axis=0, keepdims=True)
    o = dot(vt_ref[...], e.astype(low), 1, 0) / total
    o = o.astype(low)
    for piece in range(o_ref.shape[0]):
        o_ref[piece] = o[:hd, piece * lanes : (piece + 1) * lanes]
    lse_ref[0] = top * coef + jnp.log2(total)


def attend(q, q_at, k, k_at, v, v_at, hd, rows):
    tokens, keys = q.shape[0], k.shape[0]
    coef = math.log2(math.e) / hd**0.5
    steps = tokens // rows
    return pl.pallas_call(
        functools.partial(attend_kernel, hd, coef),
        grid=(steps,),
        in_specs=[
            pl.BlockSpec((rows, lanes), lambda i: (i, q_at)),
            pl.BlockSpec((keys, lanes), lambda i: (0, k_at)),
            pl.BlockSpec((keys, lanes), lambda i: (0, v_at)),
        ],
        out_specs=[
            pl.BlockSpec((rows // lanes, hd, lanes), lambda i: (i, 0, 0)),
            pl.BlockSpec((1, 1, rows), lambda i: (i, 0, 0)),
        ],
        out_shape=[
            jax.ShapeDtypeStruct((tokens // lanes, hd, lanes), low),
            jax.ShapeDtypeStruct((steps, 1, rows), exact),
        ],
        scratch_shapes=[pltpu.VMEM((lanes, keys), low)],
        compiler_params=params(10 * keys // 1024),
        cost_estimate=small_cost,
        name="attend",
    )(q, k, v)


def attend_back_kernel(hd, coef, scale, span, q_ref, k_ref, v_ref, do_ref, lse_ref, out_ref, sum_ref, kt_ref, dk_sum, dv_sum):
    step = pl.program_id(0)
    rows = q_ref.shape[0]

    @pl.when(step == 0)
    def _():
        kt_ref[...] = k_ref[...].T
        dk_sum[...] = jnp.zeros_like(dk_sum)
        dv_sum[...] = jnp.zeros_like(dv_sum)
        sum_ref[...] = jnp.zeros_like(sum_ref)

    pieces = do_ref.shape[0]
    dot_t = jnp.concatenate([do_ref[piece] for piece in range(pieces)], axis=1)
    fill = jnp.zeros((lanes - hd, dot_t.shape[1]), low)
    dot_t = jnp.concatenate([dot_t, fill], axis=0)
    q = q_ref[...]
    s = dot(k_ref[...], q, 1, 1)
    p = jnp.exp2(s * coef - lse_ref[0])
    dp = dot(v_ref[...], dot_t, 1, 0)
    r = jnp.sum(p * dp, axis=0, keepdims=True)
    ds = (p * (dp - r)).astype(low)
    dv_sum[...] += dot(p.astype(low), dot_t.T, 1, 0)
    dk_sum[...] += dot(ds, q, 1, 0)
    dq = dot(kt_ref[...], ds, 1, 0) * scale
    head = lax.broadcasted_iota(jnp.int32, dq.shape, 0) < hd
    dq = jnp.where(head, dq, 0.0).T.astype(low)
    out_ref[pl.ds(pl.multiple_of(span + step * rows, rows), rows), :lanes] = dq.astype(out_ref.dtype)
    sum_ref[0:1, :lanes] += jnp.sum(dq.astype(exact), axis=0, keepdims=True)

    @pl.when(step == pl.num_programs(0) - 1)
    def _():
        head = lax.broadcasted_iota(jnp.int32, dk_sum.shape, 1) < hd
        dk = jnp.where(head, dk_sum[...] * scale, 0.0)
        dv = dv_sum[...].astype(out_ref.dtype)
        out_ref[:, lanes : 2 * lanes] = dk.astype(out_ref.dtype)
        out_ref[:, 2 * lanes :] = dv
        sum_ref[0:1, 2 * lanes :] = jnp.sum(dv.astype(exact), axis=0, keepdims=True)


def attend_back(q, q_at, k, k_at, v, v_at, do, lse, hd, rows, span, kind):
    tokens, keys = q.shape[0], k.shape[0]
    scale = 1.0 / hd**0.5
    coef = math.log2(math.e) * scale
    steps = tokens // rows
    return pl.pallas_call(
        functools.partial(attend_back_kernel, hd, coef, scale, span),
        grid=(steps,),
        in_specs=[
            pl.BlockSpec((rows, lanes), lambda i: (i, q_at)),
            pl.BlockSpec((keys, lanes), lambda i: (0, k_at)),
            pl.BlockSpec((keys, lanes), lambda i: (0, v_at)),
            pl.BlockSpec((rows // lanes, hd, lanes), lambda i: (i, 0, 0)),
            pl.BlockSpec((1, 1, rows), lambda i: (i, 0, 0)),
        ],
        out_specs=[pl.BlockSpec((keys, 3 * lanes), lambda i: (0, 0)), pl.BlockSpec((8, 3 * lanes), lambda i: (0, 0))],
        out_shape=[jax.ShapeDtypeStruct((keys, 3 * lanes), kind), jax.ShapeDtypeStruct((8, 3 * lanes), exact)],
        scratch_shapes=[
            pltpu.VMEM((lanes, keys), low),
            pltpu.VMEM((keys, lanes), exact),
            pltpu.VMEM((keys, lanes), exact),
        ],
        compiler_params=params(14 * keys // 1024),
        cost_estimate=small_cost,
        name="attend_back",
    )(q, k, v, do, lse)


def body(
    hidden_in,
    clip_lengths,
    ln1_gain,
    ln1_bias,
    w_query,
    b_query,
    w_key,
    w_value,
    b_value,
    w_out,
    b_out,
    ln2_gain,
    ln2_bias,
    w_fc1,
    b_fc1,
    w_fc2,
    b_fc2,
    cotangent,
):
    micro, rows, width = hidden_in.shape
    at = Layout(micro)
    place = at.place
    hd = width // heads
    own = 2 * rows
    tokens = at.half * own
    clips = clip_lengths.shape[1]
    chunk = width // at.block
    step_rows = 256

    vectors = [at.to_block(v) for v in (ln1_gain, ln1_bias, b_query, b_value, b_out, ln2_gain, ln2_bias, b_fc2)]
    ff_bias = at.to_block(b_fc1)
    ff_rows = ff_bias.shape[0]
    first, second = pack(place, hidden_in, jnp.stack(vectors), ff_bias[None], at.to_block(w_out))
    blocked = [at.to_block(w) for w in (w_query, w_key, w_value, w_fc1)]
    w_in, w1 = deal(*blocked, hd, at.block)
    ff = blocked[3].shape[1] // heads
    second = at.partner(second)
    g_far = lax.dynamic_index_in_dim(cotangent, 1 - at.mine, 0, False)
    second, w_in, w1, g_far = together(second, w_in, w1, g_far)

    x_own, small, wo, *parts = arrange(place, first, second, rows)
    marks = []
    small_far = at.swapped(small, 1)
    parts[2] = jnp.concatenate([parts[2], small[None], small_far[None]], axis=1)
    c1 = small.reshape(2, extra_rows, width)[:, 0, lanes : lanes + ff_rows].reshape(1, 2 * ff_rows).astype(exact)
    mine, others = at.gather_tree(parts, marks)
    g_far = at.partner(tie(g_far, x_own))
    *mine, w_in, wo, g_far = together(*mine, w_in, wo, g_far)
    w_in = at.exchange_block(w_in)
    wo = at.gather_half(wo).reshape(heads, 2, chunk, width).transpose(1, 0, 2, 3).reshape(width, width)

    w1 = at.exchange_block(tie(w1, w_in))
    w_in = w_in.reshape(width, 3 * hd)
    g_own = jnp.concatenate(at.ordered(lax.dynamic_index_in_dim(cotangent, at.mine, 0, False), g_far), axis=0)
    g_all = at.gather_half(g_own)

    lengths = lax.dynamic_index_in_dim(clip_lengths, at.mine, 0, False)
    ends = jnp.cumsum(lengths)
    where_at = jnp.arange(tokens, dtype=jnp.int32).reshape(2, heads, rows).transpose(1, 0, 2).reshape(tokens)
    where_at = at.me // at.block * tokens + where_at
    ids = jnp.sum((ends[None, :] <= where_at[:, None]).astype(jnp.int32), axis=1).reshape(8, 2, own, 1)

    before = project(place, False, mine, ids, w_in, (), hd, clips, own, chunk)
    a1, qkv, table = project(place, True, others, ids, w_in, before, hd, clips, own, chunk)
    a1 = a1.reshape(tokens, width)
    qkv = qkv.reshape(tokens, 3 * lanes)
    span = 0
    qkv_at = (qkv, 0, qkv, 1, qkv, 2)
    if at.blocks > 1:
        span = tokens // 2
        ahead = [(d, d + at.block) for d in range(at.count - at.block)]
        behind = [(d + at.block, d) for d in range(at.count - at.block)]
        nothing = jnp.where(jnp.arange(2 * lanes)[None] == hd + clips, 1.0, 0.0).astype(low)
        kv = qkv[:, lanes:]
        slots = kv.reshape(heads, 2, rows, 2 * lanes)
        before = at.send(slots[:, 1].reshape(span, 2 * lanes), ahead)
        after = at.send(slots[:, 0].reshape(span, 2 * lanes), behind)
        before = jnp.where(at.me < at.block, nothing, before)
        after = jnp.where(at.me >= at.count - at.block, nothing, after)
        kv = jnp.concatenate([before, kv, after], axis=0)
        qkv_at = (qkv, 0, kv, 0, kv, 1)
    o_head, lse = attend(*qkv_at, hd, step_rows)
    o_head, lse, w1 = together(o_head, lse, w1)
    w1 = w1.reshape(width, ff)
    w2_shard = at.to_block(w_fc2)
    w2_far = at.partner(tie(w2_shard, o_head))
    w2 = jnp.concatenate(at.ordered(w2_shard, w2_far), axis=0)
    o_own = at.exchange_half(o_head)

    x2, *parts = join(x_own, o_own, wo, table)
    mine, others = at.gather_tree(parts)

    g_split = g_all.reshape(8, 2, own, width)
    *before, kept, sum_c = feed(place, False, mine, g_split, w1, w2, c1, (), own, low)
    hid, du, y, away, sum_c2 = feed(place, True, others, g_split, w1, w2, c1, before, own, low)
    y = lax.psum_scatter(y.reshape(tokens, width), "dev", scatter_dimension=0, tiled=True, axis_index_groups=at.halves)
    marks, made = [], []
    hid, du = hid.reshape(tokens, ff), du.reshape(tokens, ff)

    def second_terms(marks):
        made.append(dot(tie(hid, marks[0]), g_all.reshape(tokens, width), 0, 0).astype(low))
        return made

    def gathered(marks):
        made.append(assemble(place, (tie(mine[0], marks[1]), *mine[1:]), others, own))
        return made[1:]

    kept, got = at.reduce_half(away, kept, marks, {1: second_terms, 2: gathered})
    back_w2 = at.exchanged(made[0].reshape(2, -1, width))
    d_w1 = dot(tie(made[1], marks[2]).reshape(tokens, width), du, 0, 0).astype(low)
    *sums, d_w1 = together(*kept, *got, *back_w2, d_w1)
    kept, got, back_w2 = sums[:3], sums[3:6], sums[6:]

    dx2, ga_own, do_own, sum2 = second_back(kept, got, x2, g_own, table, wo, hd)
    do_head = at.exchange_half(do_own)
    ga = at.gather_half(ga_own).reshape(tokens, width)
    d_w1 = at.exchange_block(tie(d_w1, do_head).reshape(at.block, chunk, ff))

    kind = low if at.blocks == 1 else exact
    dqkv, sum_in = attend_back(*qkv_at, do_head, lse, hd, step_rows, span, kind)
    if at.blocks > 1:
        dkv = dqkv[:, lanes:]
        to_before = at.send(dkv[:span].astype(low), behind).astype(exact)
        to_after = at.send(dkv[span + tokens :].astype(low), ahead).astype(exact)
        halo = jnp.stack([t.reshape(heads, rows, 2 * lanes) for t in (to_after, to_before)], axis=1)
        dkv = dkv[span : span + tokens] + halo.reshape(tokens, 2 * lanes)
        dqkv = jnp.concatenate([dqkv[span : span + tokens, :lanes], dkv], axis=1).astype(low)
        sum_in = jnp.broadcast_to(jnp.sum(dqkv.astype(exact), axis=0, keepdims=True), (8, 3 * lanes))
    dqkv, sum_in, d_w1 = together(dqkv, sum_in, d_w1)
    split = dqkv.reshape(8, 2, own, 3 * lanes)
    w_pad = w_in.reshape(width, 3, hd)
    w_pad = jnp.pad(w_pad, ((0, 0), (0, 0), (0, lanes - hd))).reshape(width, 3 * lanes)
    away = terms(place, True, split, w_pad, 1, low)
    marks, made = [], []

    def projections(marks):
        late = tie(dqkv, away)
        made.append(lay_out(place, dot(a1, late, 0, 0), sum2, sum_in, sum_c, sum_c2, hd, chunk, at.block))
        return made

    def outputs(marks):
        out = x2 + (tie(y, marks[0]).astype(exact) + table[7])
        made.extend(at.exchanged(out.astype(low).reshape(2, rows, width)))
        return made[1:]

    kept, got = at.reduce_half(away, terms(place, False, split, w_pad, 1, low), marks, {0: projections, 2: outputs})
    layer_out = made[1:]

    d_in = at.exchange_block(made[0])
    ga, o_late = together(ga, o_head, marks[1])[:2]
    d_wo = jnp.einsum("ckt,ctn->kn", o_late, ga.reshape(at.half, own, width), preferred_element_type=exact)
    back_wo = at.send_rows_back(d_wo.astype(low).reshape(2, chunk, width))
    kept_first, d_in, *back_wo = together(kept[0], d_in, *back_wo)
    kept = (kept_first, *kept[1:])
    grad_w2 = at.from_block(back_w2[0].astype(exact) + back_w2[1].astype(exact))
    grad_w1 = at.from_block(collect_hidden(d_w1))
    grad_wo = at.from_block(back_wo[0].astype(exact) + back_wo[1].astype(exact))
    *grads, vec = collect(d_in, hd, chunk)
    grad_wq, grad_wk, grad_wv = (at.from_block(v) for v in grads)
    pieces = [at.from_block(vec[i, :chunk]) for i in range(6)]
    grad_g2, grad_b2, grad_bo, grad_bf2, grad_bq, grad_bv = pieces
    grad_c1 = at.from_block(vec[0, chunk : chunk + ff_rows])

    dx, vec = first_back(kept, got, x_own, dx2, table, chunk, at.block)
    input_grad = at.exchanged(dx.reshape(2, rows, width))
    layer_out, input_grad = (jnp.stack(at.ordered(*v)).astype(exact) for v in (layer_out, input_grad))
    vec = jnp.sum(at.exchange_block(vec), axis=(0, 1))
    grad_g1 = at.from_block(vec[:chunk])
    grad_b1 = at.from_block(vec[lanes // 2 : lanes // 2 + chunk])
    return (
        layer_out,
        input_grad,
        grad_g1,
        grad_b1,
        grad_wq,
        grad_bq,
        grad_wk,
        grad_wv,
        grad_bv,
        grad_wo,
        grad_bo,
        grad_g2,
        grad_b2,
        grad_w1,
        grad_c1,
        grad_w2,
        grad_bf2,
    )


def solution(mesh):
    tokens, vector, matrix = P(None, "dev", None), P("dev"), P("dev", None)
    grads = (vector, vector, matrix, vector, matrix, matrix, vector, matrix, vector, vector, vector, matrix, vector, matrix, vector)
    return jax.shard_map(
        body,
        mesh=mesh,
        in_specs=(tokens, P()) + grads + (tokens,),
        out_specs=(tokens, tokens) + grads,
        check_vma=False,
    )
```

```python
import functools
import math

import jax
import jax.numpy as jnp
from jax import lax
from jax.experimental import pallas as pl
from jax.experimental.pallas import tpu as pltpu
from jax.sharding import PartitionSpec as P

eps = 1e-05
heads = 16
low = jnp.bfloat16
exact = jnp.float32
far = -1e30
lanes = 128
extra_rows = 8


def dot(a, b, ca, cb):
    return lax.dot_general(a, b, (((ca,), (cb,)), ((), ())), preferred_element_type=exact)


def normalized(v):
    mean = jnp.mean(v, axis=-1, keepdims=True)
    cent = v - mean
    inverse = lax.rsqrt(jnp.mean(cent * cent, axis=-1, keepdims=True) + eps)
    return cent * inverse, inverse


def norm_back(unit, inverse, gain, grad):
    scaled = grad * gain
    along = jnp.mean(scaled * unit, axis=-1, keepdims=True)
    return inverse * (scaled - jnp.mean(scaled, axis=-1, keepdims=True) - unit * along)


def tie(value, *others):
    return lax.optimization_barrier((value,) + others)[0]


def together(*values):
    return lax.optimization_barrier(values)


class Layout:
    def __init__(self, micro):
        self.count = lax.axis_size("dev")
        self.half = heads
        self.block = micro * heads
        self.blocks = self.count // self.block
        self.me = lax.axis_index("dev")
        self.rank = self.me % self.block
        self.mine = self.rank // self.half
        self.head = self.rank % self.half
        self.odd = self.rank % 2
        bits = [(self.me // bit) % 2 for bit in (1, 2, 4, 8)]
        self.place = jnp.stack(bits + [self.mine, self.head, self.odd]).astype(jnp.int32)
        self.halves = [list(range(s, s + self.half)) for s in range(0, self.count, self.half)]
        self.whole = [list(range(s, s + self.block)) for s in range(0, self.count, self.block)]
        self.rows = [list(range(s, s + self.blocks)) for s in range(0, self.count, self.blocks)]
        first = [d // self.half % 2 for d in range(self.count)]
        base = [d // self.block * self.block + 2 * (d % self.half) for d in range(self.count)]
        self.even_first = [(d, base[d] + first[d]) for d in range(self.count)]
        self.odd_first = [(d, base[d] + 1 - first[d]) for d in range(self.count)]

    def send(self, value, pairs):
        return lax.ppermute(value, "dev", pairs)

    def swapped(self, value, bit):
        return self.send(value, [(d, d ^ bit) for d in range(self.count)])

    def to_block(self, value):
        if self.blocks == 1:
            return value
        value = lax.all_gather(value, "dev", axis=0, tiled=True, axis_index_groups=self.rows)
        return self.send(value, [(d, d % self.blocks * self.block + d // self.blocks) for d in range(self.count)])

    def from_block(self, value):
        if self.blocks == 1:
            return value
        value = self.send(value, [(d % self.blocks * self.block + d // self.blocks, d) for d in range(self.count)])
        return lax.psum_scatter(value, "dev", scatter_dimension=0, tiled=True, axis_index_groups=self.rows)

    def partner(self, value):
        return self.swapped(value, self.half)

    def ordered(self, kept, got):
        return jnp.where(self.mine == 0, kept, got), jnp.where(self.mine == 0, got, kept)

    def exchanged(self, value):
        kept = lax.dynamic_index_in_dim(value, self.mine, 0, False)
        return kept, self.partner(lax.dynamic_index_in_dim(value, 1 - self.mine, 0, False))

    def send_rows_back(self, value):
        first = lax.dynamic_index_in_dim(value, self.mine, 0, False)
        second = lax.dynamic_index_in_dim(value, 1 - self.mine, 0, False)
        return self.send(first, self.even_first), self.send(second, self.odd_first)

    def gather_half(self, value):
        return lax.all_gather(value, "dev", axis=0, axis_index_groups=self.halves)

    def exchange_half(self, value):
        return lax.all_to_all(value, "dev", 0, 0, tiled=True, axis_index_groups=self.halves)

    def exchange_block(self, value):
        return lax.all_to_all(value, "dev", 0, 0, tiled=True, axis_index_groups=self.whole)

    def gather_tree(self, parts, beside=()):
        brought = []
        for stage in range(3):
            got = [self.swapped(piece, order[stage]) for piece, order in zip(parts, part_orders)]
            if beside:
                far = self.partner(tie(beside[stage], parts[0]))
                first, far = together(got[0], far)
                got = [first, *got[1:]]
                brought.append(far)
            if stage < 2:
                parts = merge(parts, got)
        other = [self.swapped(piece, 1) for piece in (*parts, *got)]
        return (*parts, *got), other, brought

    def reduce_half(self, away, kept, marks=None, before=None, arrived=None):
        got = [self.swapped(away, 1)]
        kept = [kept]
        for stage in range(3):
            if before and stage in before:
                got = [tie(got[0], *before[stage](marks)), *got[1:]]
            away, kept = split_terms(self.place, stage, kept, got)
            if marks is not None:
                marks.append(away[0])
            got = [self.swapped(piece, order[stage]) for piece, order in zip(away, part_orders)]
            if arrived is not None:
                arrived.append(got[2])
        return kept, got


small_cost = pl.CostEstimate(flops=1 << 10, bytes_accessed=1 << 10, transcendentals=0)


def far_off(v):
    return pltpu.with_memory_space_constraint(v, pltpu.HBM)


def params(megabytes):
    return pltpu.CompilerParams(vmem_limit_bytes=megabytes << 20)


part_orders = ((8, 4, 2), (4, 2, 8), (2, 8, 4))


def part_bounds(tokens):
    cut = tokens * 3 // 8 // 16 * 16
    return ((0, cut), (cut, 2 * cut), (2 * cut, tokens))


def split_kernel(stage, place_ref, *refs):
    place = {bit: place_ref[i] for i, bit in enumerate((1, 2, 4, 8))}
    if stage == 0:
        kept_ref, got_ref = refs[:2]
        outs = refs[2:]
        bounds = part_bounds(kept_ref.shape[1])
    else:
        outs = refs[6:]
    for part, order in enumerate(part_orders):
        left = [bit for bit in (8, 4, 2) if bit not in order[:stage]]
        at = left.index(order[stage])
        below = 1 << (len(left) - 1 - at)
        for half, side in ((0, 1 - place[order[stage]]), (1, place[order[stage]])):
            out_ref = outs[part + 3 * half]
            for j in range(out_ref.shape[0]):
                index = (j // below * 2 + side) * below + j % below
                if stage == 0:
                    start, end = bounds[part]
                    term = kept_ref[index, start:end].astype(exact) + got_ref[index, start:end].astype(exact)
                else:
                    term = refs[part][index].astype(exact) + refs[3 + part][index].astype(exact)
                out_ref[j] = term.astype(out_ref.dtype)


def split_terms(place, stage, kept, got):
    width = kept[0].shape[-1]
    bounds = part_bounds(kept[0].shape[1]) if stage == 0 else [(0, k.shape[1]) for k in kept]
    count = kept[0].shape[0] // 2
    cols = 256 if stage == 0 else 640
    spec = lambda n, t: pl.BlockSpec((n, t, cols), lambda i, p: (0, 0, i))
    outs = [(count, end - start) for start, end in bounds]
    res = pl.pallas_call(
        functools.partial(split_kernel, stage),
        grid_spec=pltpu.PrefetchScalarGridSpec(
            num_scalar_prefetch=1,
            grid=(width // cols,),
            in_specs=[spec(*v.shape[:2]) for v in (*kept, *got)],
            out_specs=[spec(*o) for o in outs] * 2,
        ),
        out_shape=[jax.ShapeDtypeStruct(o + (width,), kind) for kind in (low, exact) for o in outs],
        compiler_params=params(10),
        cost_estimate=small_cost,
        name="split_terms",
    )(place, *kept, *got)
    return res[:3], res[3:]


def last_sum(refs):
    return jnp.concatenate([refs[i][0].astype(exact) + refs[3 + i][0].astype(exact) for i in range(3)], axis=0)


def pack_kernel(place_ref, x_ref, v_ref, c_ref, first_ref, second_ref):
    rows, width = x_ref.shape[1:]
    mine = place_ref[4]
    fill = jnp.zeros((v_ref.shape[0], width - v_ref.shape[1]), exact)
    small = jnp.concatenate([v_ref[...].astype(exact), fill], axis=1)
    c = jnp.concatenate([c_ref[...].astype(exact), jnp.zeros((1, width - lanes - c_ref.shape[1]), exact)], axis=1)
    c = jnp.concatenate([jnp.zeros((1, lanes), exact), c], axis=1)
    row = lax.broadcasted_iota(jnp.int32, small.shape, 0)
    small = small + jnp.where(row == 0, c, 0.0)
    tail = small.astype(low)
    for out_ref, index in ((first_ref, mine), (second_ref, 1 - mine)):
        out_ref[:rows] = x_ref[index]
        out_ref[rows:] = tail


def pack(place, x, vectors, c):
    rows, width = x.shape[1:]
    out = jax.ShapeDtypeStruct((rows + extra_rows, width), low)
    return pl.pallas_call(
        pack_kernel,
        grid_spec=pltpu.PrefetchScalarGridSpec(
            num_scalar_prefetch=1,
            grid=(1,),
            in_specs=[whole_spec(v) for v in (x, vectors, c)],
            out_specs=[out_spec(out)] * 2,
        ),
        out_shape=[out, out],
        compiler_params=params(6),
        name="pack",
    )(place, x, vectors, c)


def arrange_kernel(rows, place_ref, first_ref, second_ref, x_ref, small_ref, *part_refs):
    mine = place_ref[4]
    for side, refs in enumerate(((first_ref, second_ref), (second_ref, first_ref))):

        @pl.when(mine == side)
        def _():
            x = jnp.concatenate([ref[:rows] for ref in refs], axis=0)
            x_ref[...] = x
            tail = [ref[rows:].astype(exact) for ref in refs]
            small_ref[...] = jnp.concatenate(tail, axis=0).astype(low)
            for part_ref, (start, end) in zip(part_refs, part_bounds(2 * rows)):
                part_ref[0] = x[start:end]


def arrange(place, first, second, rows):
    width = first.shape[1]
    shapes = [(2 * rows, width), (2 * extra_rows, width)]
    shapes += [(1, end - start, width) for start, end in part_bounds(2 * rows)]
    outs = [jax.ShapeDtypeStruct(shape, low) for shape in shapes]
    return pl.pallas_call(
        functools.partial(arrange_kernel, rows),
        grid_spec=pltpu.PrefetchScalarGridSpec(
            num_scalar_prefetch=1,
            grid=(1,),
            in_specs=[whole_spec(first), whole_spec(second)],
            out_specs=[out_spec(out) for out in outs],
        ),
        out_shape=outs,
        compiler_params=params(6),
        name="arrange",
    )(place, first, second)


def up_to_lanes(size):
    return -(-size // lanes) * lanes


def fold(v):
    return jnp.concatenate([v[i : i + 8] for i in range(0, v.shape[0], 8)], axis=1)


def unfold(v, size):
    return jnp.concatenate([v[:, i : i + size] for i in range(0, v.shape[1], size)], axis=0)


def unfold_kernel(in_ref, out_ref):
    size = out_ref.shape[1]
    chunk = in_ref.shape[2] // size * 8
    for device in range(0, in_ref.shape[0], 2):
        rows = [unfold(in_ref[device + i].astype(exact), size) for i in range(2)]
        out_ref[device * chunk : (device + 2) * chunk] = jnp.concatenate(rows, axis=0).astype(low)


def unfolded(v, size):
    return pl.pallas_call(
        unfold_kernel,
        out_shape=jax.ShapeDtypeStruct((v.size // size, size), low),
        compiler_params=params(8),
        cost_estimate=small_cost,
        name="unfolded",
    )(v)


def deal_kernel(hd, q_ref, k_ref, v_ref, w_ref, in_ref, hidden_ref):
    ff = w_ref.shape[1] // heads
    side_by_side = lambda pieces: jnp.concatenate([piece.astype(exact) for piece in pieces], axis=1).astype(low)
    for head in range(heads):
        at = [(slot * heads + head) * (ff // 2) for slot in range(2)]
        hidden = jnp.concatenate([w_ref[:, a : a + ff // 2].astype(exact) for a in at], axis=1)
        hidden = fold(hidden).astype(low)
        columns = side_by_side([ref[:, head * hd : (head + 1) * hd] for ref in (q_ref, k_ref, v_ref)])
        for device in range(head, in_ref.shape[0], heads):
            in_ref[device] = columns
            hidden_ref[device] = hidden


def deal(q, k, v, w, hd, block):
    chunk, ff = q.shape[0], w.shape[1] // heads
    return pl.pallas_call(
        functools.partial(deal_kernel, hd),
        out_shape=[jax.ShapeDtypeStruct(shape, low) for shape in ((block, chunk, 3 * hd), (block, 8, chunk * ff // 8))],
        compiler_params=params(8),
        name="deal",
    )(q, k, v, w)


def merge_kernel(*refs):
    for i in range(3):
        count = refs[i].shape[0]
        refs[6 + i][:count] = refs[i][...]
        refs[6 + i][count:] = refs[3 + i][...]


def merge(parts, got):
    width = parts[0].shape[2]
    cols = 640
    spec = lambda shape: pl.BlockSpec(shape[:2] + (cols,), lambda i: (0, 0, i))
    outs = [(2 * p.shape[0],) + p.shape[1:] for p in parts]
    return pl.pallas_call(
        merge_kernel,
        grid=(width // cols,),
        in_specs=[spec(v.shape) for v in (*parts, *got)],
        out_specs=[spec(o) for o in outs],
        out_shape=[jax.ShapeDtypeStruct(o, low) for o in outs],
        compiler_params=params(8),
        name="merge",
    )(*parts, *got)


def out_spec(v):
    return pl.BlockSpec(v.shape, lambda *_: (0,) * len(v.shape))


def tree_rows(place_ref, chip, refs, fill):
    mine = place_ref[1] + 2 * place_ref[2] + 4 * place_ref[3]
    apart = chip ^ mine
    step = {8: apart // 4, 4: apart // 2 % 2, 2: apart % 2}
    for part, order in enumerate(part_orders):
        index = 2 * step[order[1]] + step[order[0]]
        for late in range(2):

            @pl.when(step[order[2]] == late)
            def _():
                fill(part, refs[part + 3 * late], index)


def fill_rows(place_ref, chip, refs, out_ref, base, own):
    bounds = part_bounds(own)

    def fill(part, ref, index):
        start, end = bounds[part]
        out_ref[pl.ds(base + start, end - start)] = ref[index, : end - start]

    tree_rows(place_ref, chip, refs, fill)


def whole_spec(v):
    return pl.BlockSpec(v.shape, lambda *_: (0,) * len(v.shape), pipeline_mode=pl.Buffered(1))


def norm_kernel(hd, chunk, first, place_ref, *refs):
    pieces = refs[:6]
    a_ref, table_ref, x_scr = refs[-3:]
    step, _, own, width = a_ref.shape

    @pl.when(pl.program_id(0) == 0)
    def _():
        if first:
            tail = part_bounds(own)[2]

            def fill(chip, part, ref, index):
                if part != 2:
                    return
                small = ref[index, tail[1] - tail[0] :].astype(exact)
                for far_core in range(2):
                    for slot in range(2):
                        line = (2 * far_core + slot) * extra_rows
                        piece = small[line : line + extra_rows, :chunk]
                        for core in range(2):

                            @pl.when(place_ref[0] == core)
                            def _():
                                at = (heads * slot + 2 * chip + (core ^ far_core)) * chunk
                                table_ref[:, at : at + chunk] = piece

            for chip in range(8):
                tree_rows(place_ref, chip, pieces, functools.partial(fill, chip))
        else:
            table_ref[...] = refs[6][...]

    for j in range(step):
        fill_rows(place_ref, pl.program_id(0) * step + j, pieces, x_scr, j * own, own)
    unit, _ = normalized(x_scr[...].astype(exact))
    a_ref[...] = (unit * table_ref[0:1] + table_ref[1:2]).astype(low).reshape(a_ref.shape)


def norm(place, other, pieces, before, hd, own, chunk):
    width = pieces[0].shape[2]
    step = 4
    side = (lambda p: 1 - p[0]) if other else (lambda p: p[0])
    table = jax.ShapeDtypeStruct((extra_rows, width), exact)
    return pl.pallas_call(
        functools.partial(norm_kernel, hd, chunk, not before),
        grid_spec=pltpu.PrefetchScalarGridSpec(
            num_scalar_prefetch=1,
            grid=(8 // step,),
            in_specs=[whole_spec(v) for v in pieces] + ([whole_spec(table), pl.BlockSpec(memory_space=pl.ANY)] if before else []),
            out_specs=[pl.BlockSpec((step, 1, own, width), lambda i, p: (i, side(p), 0, 0)), out_spec(table)],
            scratch_shapes=[pltpu.VMEM((step * own, width), low)],
        ),
        out_shape=[pltpu.HBM((8, 2, own, width), low), table],
        input_output_aliases={8: 0} if before else {},
        compiler_params=params(30),
        cost_estimate=small_cost,
        name="norm",
    )(place, *pieces, *before[::-1])


def project_kernel(hd, clips, own_rows, place_ref, ends_ref, a_ref, w_ref, table_ref, qkv_ref, pad_ref, bias_ref):
    rows, width = a_ref.shape

    @pl.when(pl.program_id(0) == 0)
    def _():
        w = w_ref[...].astype(exact)
        fill = jnp.zeros((width, lanes - hd), exact)
        w = [v for i in range(3) for v in (w[:, i * hd : (i + 1) * hd], fill)]
        pad_ref[...] = jnp.concatenate(w, axis=1).astype(low)
        bias_ref[...] = jnp.zeros_like(bias_ref)
        for h in range(heads):

            @pl.when(place_ref[5] == h)
            def _():
                for line, at in ((2, 0), (3, 2 * lanes)):
                    bias_ref[0:1, at : at + hd] = table_ref[line : line + 1, h * hd : (h + 1) * hd]

    qkv = dot(a_ref[...], pad_ref[...], 1, 0) + bias_ref[0:1]
    column = lax.broadcasted_iota(jnp.int32, (rows, lanes), 1) - hd
    row = lax.broadcasted_iota(jnp.int32, (rows, lanes), 0) + pl.program_id(0) * rows
    shift = own_rows.bit_length() - 1
    token = (lax.shift_right_logical(row, shift) & 1) * (heads * own_rows)
    token += lax.shift_right_logical(row, shift + 1) * own_rows + (row & (own_rows - 1))
    clip = jnp.zeros_like(token)
    for i in range(clips):
        clip += (ends_ref[i] <= token).astype(jnp.int32)
    match = clip == column
    marked = (column >= 0) & (column <= clips)
    qkv_ref[:, :lanes] = (qkv[:, :lanes] + jnp.where(marked & ~match, far, 0.0)).astype(low)
    qkv_ref[:, lanes : 2 * lanes] = (qkv[:, lanes : 2 * lanes] + jnp.where(marked & match, 1.0, 0.0)).astype(low)
    qkv_ref[:, 2 * lanes :] = qkv[:, 2 * lanes :].astype(low)


def project(place, ends, a, w, table, hd, own_rows):
    tokens, width = a.shape
    rows = 512
    clips = ends.shape[0]
    assert own_rows & (own_rows - 1) == 0
    wide = jax.ShapeDtypeStruct((width, 3 * lanes), low)
    return pl.pallas_call(
        functools.partial(project_kernel, hd, clips, own_rows),
        grid_spec=pltpu.PrefetchScalarGridSpec(
            num_scalar_prefetch=2,
            grid=(tokens // rows,),
            in_specs=[
                pl.BlockSpec((rows, width), lambda i, p, e: (i, 0)),
                whole_spec(w),
                whole_spec(table),
            ],
            out_specs=[pl.BlockSpec((rows, 3 * lanes), lambda i, p, e: (i, 0)), out_spec(wide)],
            scratch_shapes=[pltpu.VMEM((8, 3 * lanes), exact)],
        ),
        out_shape=[jax.ShapeDtypeStruct((tokens, 3 * lanes), low), pltpu.HBM(wide.shape, low)],
        compiler_params=params(20),
        cost_estimate=small_cost,
        name="project",
    )(place, ends, far_off(a), w, table)


def join_kernel(x_ref, o_ref, w_ref, table_ref, x2_ref, *part_refs):
    o = o_ref[...].reshape(w_ref.shape[0], o_ref.shape[2])
    x2 = x_ref[...].astype(exact) + (dot(o, w_ref[...], 0, 0) + table_ref[4:5])
    x2_ref[...] = x2
    unit, _ = normalized(x2)
    a2 = (unit * table_ref[5:6] + table_ref[6:7]).astype(low)
    for part_ref, (start, end) in zip(part_refs, part_bounds(x2.shape[0])):
        part_ref[0] = a2[start:end]


def join(x, o, w, table):
    own, width = x.shape
    parts = [jax.ShapeDtypeStruct((1, end - start, width), low) for start, end in part_bounds(own)]
    return pl.pallas_call(
        join_kernel,
        out_shape=[jax.ShapeDtypeStruct(x.shape, exact)] + parts,
        compiler_params=params(10),
        cost_estimate=small_cost,
        name="join",
    )(x, o, far_off(w), table)


def accumulate(total_ref, term):
    @pl.when(pl.program_id(0) == 0)
    def _():
        total_ref[...] = term

    @pl.when(pl.program_id(0) > 0)
    def _():
        total_ref[...] += term


def at_end(write):
    pl.when(pl.program_id(0) == pl.num_programs(0) - 1)(write)


def fc2_grad_kernel(hid_ref, g_ref, out_ref, total_ref):
    rows = math.prod(g_ref.shape[:3])
    accumulate(total_ref, dot(hid_ref[...].reshape(rows, hid_ref.shape[3]), g_ref[...].reshape(rows, g_ref.shape[3]), 0, 0))

    @at_end
    def _():
        out_ref[...] = total_ref[...].astype(low).reshape(out_ref.shape)


def fc2_grad(hid, g):
    eight, two, own, width = g.shape
    ff = hid.shape[3]
    step = 2
    out = jax.ShapeDtypeStruct((2, ff // 2, width), low)
    return pl.pallas_call(
        fc2_grad_kernel,
        grid=(eight // step,),
        in_specs=[pl.BlockSpec((step, two, own, size), lambda i: (i, 0, 0, 0)) for size in (ff, width)],
        out_specs=out_spec(out),
        out_shape=out,
        scratch_shapes=[pltpu.VMEM((ff, width), exact)],
        compiler_params=params(12),
        cost_estimate=small_cost,
        name="fc2_grad",
    )(far_off(hid), far_off(g))


def fc1_grad_kernel(place_ref, *refs):
    mine, others, (du_ref, out_ref, a_scr, total_ref) = refs[:6], refs[6:12], refs[12:]
    chips, two, own, ff = du_ref.shape
    width = a_scr.shape[3]
    bounds = part_bounds(own)
    for j in range(chips):
        chip = pl.program_id(0) * chips + j
        for core, pieces in ((place_ref[0], mine), (1 - place_ref[0], others)):

            def fill(part, ref, index):
                start, end = bounds[part]
                a_scr[j, core, start:end] = ref[index]

            tree_rows(place_ref, chip, pieces, fill)
    rows = chips * two * own
    accumulate(total_ref, dot(du_ref[...].reshape(rows, ff), a_scr[...].reshape(rows, width), 0, 0))

    @at_end
    def _():
        total = total_ref[...].T
        chunk = width // out_ref.shape[0]
        for device in range(out_ref.shape[0]):
            out_ref[device] = fold(total[device * chunk : (device + 1) * chunk]).astype(low)


def fc1_grad(place, mine, others, du, chunk):
    eight, two, own, ff = du.shape
    width = mine[0].shape[2]
    step = 2
    out = jax.ShapeDtypeStruct((width // chunk, 8, chunk * ff // 8), low)
    return pl.pallas_call(
        fc1_grad_kernel,
        grid_spec=pltpu.PrefetchScalarGridSpec(
            num_scalar_prefetch=1,
            grid=(eight // step,),
            in_specs=[whole_spec(v) for v in (*mine, *others)] + [pl.BlockSpec((step, two, own, ff), lambda i, p: (i, 0, 0, 0))],
            out_specs=out_spec(out),
            scratch_shapes=[pltpu.VMEM((step, two, own, width), low), pltpu.VMEM((ff, width), exact)],
        ),
        out_shape=out,
        compiler_params=params(20),
        cost_estimate=small_cost,
        name="fc1_grad",
    )(place, *mine, *others, far_off(du))


def output_grad_kernel(o_ref, ga_ref, out_ref, total_ref):
    term = dot(o_ref[0], ga_ref[0], 1, 0)
    for piece in range(1, o_ref.shape[0]):
        term += dot(o_ref[piece], ga_ref[piece], 1, 0)
    accumulate(total_ref, term)

    @at_end
    def _():
        rows = out_ref.shape[1]
        for side in range(2):
            out_ref[side] = total_ref[side * rows : (side + 1) * rows].astype(low)


def output_grad(o, ga):
    count, hd, own = o.shape
    width = ga.shape[2]
    step = 4
    out = jax.ShapeDtypeStruct((2, hd // 2, width), low)
    return pl.pallas_call(
        output_grad_kernel,
        grid=(count // step,),
        in_specs=[pl.BlockSpec((step, hd, own), lambda i: (i, 0, 0)), pl.BlockSpec((step, own, width), lambda i: (i, 0, 0))],
        out_specs=out_spec(out),
        out_shape=out,
        scratch_shapes=[pltpu.VMEM((hd, width), exact)],
        compiler_params=params(8),
        cost_estimate=small_cost,
        name="output_grad",
    )(o, far_off(ga))


def feed_kernel(place_ref, *refs):
    pieces, (g_ref, w1_ref, w2_ref, c_ref) = refs[:6], refs[6:10]
    hid_ref, du_ref, y_ref, da_ref, sum_ref, a_scr = refs[-6:]
    step, own, width = da_ref.shape
    rows = step * own
    for j in range(step):
        fill_rows(place_ref, pl.program_id(0) * step + j, pieces, a_scr, j * own, own)
    w1, w2 = w1_ref[...], w2_ref[...]
    u = dot(a_scr[...], w1, 1, 0) + c_ref[...]
    d_hid = dot(g_ref[...].reshape(rows, width), w2, 1, 1)
    below = 0.5 * (1.0 + lax.erf(u * math.sqrt(0.5)))
    hid = (u * below).astype(low)
    hid_ref[...] = hid.reshape(hid_ref.shape)
    y_ref[...] = dot(hid, w2, 1, 0).reshape(y_ref.shape).astype(low)
    slope = below + u * (jnp.exp(-0.5 * u * u) * (1.0 / math.sqrt(2.0 * math.pi)))
    du = (d_hid * slope).astype(low)
    du_ref[...] = du.reshape(du_ref.shape)
    da_ref[...] = dot(du, w1, 1, 1).reshape(da_ref.shape).astype(da_ref.dtype)

    @pl.when(pl.program_id(0) == 0)
    def _():
        sum_ref[...] = jnp.zeros_like(sum_ref)

    sum_ref[...] += jnp.sum(du.astype(exact), axis=0, keepdims=True)


def feed(place, other, pieces, g, w1, w2, c1, before, own, kind):
    ff, width = w2.shape
    step = 4
    tokens = 8 * own
    side = (lambda p: 1 - p[0]) if other else (lambda p: p[0])
    pick = lambda size: pl.BlockSpec((step, 1, own, size), lambda i, p: (i, side(p), 0, 0))
    shape = lambda size: pltpu.HBM((8, 2, own, size), low)
    row = pl.BlockSpec((1, ff), lambda i, p: (0, 0))
    return pl.pallas_call(
        feed_kernel,
        grid_spec=pltpu.PrefetchScalarGridSpec(
            num_scalar_prefetch=1,
            grid=(8 // step,),
            in_specs=[whole_spec(v) for v in pieces]
            + [pick(width), whole_spec(w1), whole_spec(w2), row]
            + [pl.BlockSpec(memory_space=pl.ANY)] * len(before),
            out_specs=[pick(ff), pick(ff), pick(width), pl.BlockSpec((step, own, width), lambda i, p: (i, 0, 0)), row],
            scratch_shapes=[pltpu.VMEM((step * own, width), low)],
        ),
        out_shape=[
            shape(ff),
            shape(ff),
            shape(width),
            pltpu.HBM((8, own, width), kind),
            jax.ShapeDtypeStruct((1, ff), exact),
        ],
        input_output_aliases={11: 0, 12: 1, 13: 2} if before else {},
        compiler_params=params(34),
        cost_estimate=small_cost,
        name="feed",
    )(place, *pieces, far_off(g), w1, w2, c1, *before)


def terms_kernel(contract, place_ref, left_ref, right_ref, out_ref):
    rows = out_ref.shape[0] * out_ref.shape[1]
    left = left_ref[...].reshape(rows, left_ref.shape[-1])
    out_ref[...] = dot(left, right_ref[...], 1, contract).reshape(out_ref.shape).astype(out_ref.dtype)


def terms(place, other, left, right, contract, kind):
    eight, two, own, depth = left.shape
    width = right.shape[1 - contract]
    step = 4
    side = (lambda p: 1 - p[0]) if other else (lambda p: p[0])
    return pl.pallas_call(
        functools.partial(terms_kernel, contract),
        grid_spec=pltpu.PrefetchScalarGridSpec(
            num_scalar_prefetch=1,
            grid=(eight // step,),
            in_specs=[
                pl.BlockSpec((step, 1, own, depth), lambda i, p: (i, side(p), 0, 0)),
                pl.BlockSpec(right.shape, lambda i, p: (0, 0)),
            ],
            out_specs=pl.BlockSpec((step, own, width), lambda i, p: (i, 0, 0)),
        ),
        out_shape=jax.ShapeDtypeStruct((eight, own, width), kind),
        compiler_params=params(16),
        cost_estimate=small_cost,
        name="terms",
    )(place, left, right)


def rows_of(values, width):
    fill = jnp.zeros((8 - len(values), width), exact)
    return jnp.concatenate(values + [fill], axis=0)


def second_back_kernel(*refs):
    da2 = last_sum(refs[:6])
    x2_ref, g_ref, table_ref, w_ref, dx2_ref, ga_ref, do_ref, sum_ref = refs[6:]
    unit, inverse = normalized(x2_ref[...])
    g = g_ref[...].astype(exact)
    dx2 = g + norm_back(unit, inverse, table_ref[5:6], da2)
    dx2_ref[...] = dx2
    ga = dx2.astype(low)
    ga_ref[...] = ga
    do_ref[...] = dot(w_ref[...], ga, 1, 1).astype(low).reshape(do_ref.shape)
    total = lambda v: jnp.sum(v, axis=0, keepdims=True)
    sum_ref[...] = rows_of([total(da2 * unit), total(da2), total(ga.astype(exact)), total(g)], ga.shape[1])


def second_back(kept, got, x2, g, table, w, hd):
    own, width = x2.shape
    return pl.pallas_call(
        second_back_kernel,
        out_shape=[
            jax.ShapeDtypeStruct((own, width), exact),
            jax.ShapeDtypeStruct((own, width), low),
            jax.ShapeDtypeStruct((heads, hd, own), low),
            jax.ShapeDtypeStruct((8, width), exact),
        ],
        compiler_params=params(12),
        cost_estimate=small_cost,
        name="second_back",
    )(*kept, *got, x2, g, table, far_off(w))


def first_back_kernel(chunk, *refs):
    da1 = last_sum(refs[:6])
    x_ref, dx2_ref, table_ref, dx_ref, vec_ref = refs[6:]
    unit, inverse = normalized(x_ref[...].astype(exact))
    dx = dx2_ref[...] + norm_back(unit, inverse, table_ref[0:1], da1)
    dx_ref[...] = dx.astype(low)
    total = lambda v: jnp.sum(v, axis=0, keepdims=True)
    rows = [total(da1 * unit), total(da1)]
    fill = jnp.zeros((1, lanes // 2 - chunk), exact)
    for device in range(vec_ref.shape[0]):
        part = slice(device * chunk, (device + 1) * chunk)
        vec_ref[device] = jnp.concatenate([rows[0][:, part], fill, rows[1][:, part], fill], axis=1)


def first_back(kept, got, x, dx2, table, chunk, block):
    return pl.pallas_call(
        functools.partial(first_back_kernel, chunk),
        out_shape=[jax.ShapeDtypeStruct(x.shape, low), jax.ShapeDtypeStruct((block, 1, lanes), exact)],
        compiler_params=params(8),
        name="first_back",
    )(*kept, *got, x, dx2, table)


def head_grad_kernel(hd, chunk, place_ref, a_ref, d_ref, sum2_ref, sum_in_ref, sum_c_ref, sum_c2_ref, out_ref, total_ref, line_ref):
    accumulate(total_ref, dot(d_ref[...], a_ref[...], 0, 0))

    @at_end
    def _():
        block = out_ref.shape[0]
        head = place_ref[5]
        c = sum_c_ref[...] + sum_c2_ref[...]
        ff_rows = c.shape[1] // 2
        total = jnp.concatenate([total_ref[i * lanes : i * lanes + hd] for i in range(3)], axis=0).T
        line_ref[...] = jnp.zeros_like(line_ref)
        line_ref[0:4] = sum2_ref[0:4]
        for h in range(heads):

            @pl.when(head == h)
            def _():
                for line, at in ((4, 0), (5, 2 * lanes)):
                    line_ref[line : line + 1, h * hd : (h + 1) * hd] = sum_in_ref[0:1, at : at + hd]
                for slot in range(block // heads):
                    for line in range(ff_rows // chunk):
                        at, start = (slot * heads + h) * chunk, slot * ff_rows + line * chunk
                        line_ref[8 + line : 9 + line, at : at + chunk] = c[:, start : start + chunk]

        small = line_ref[...].T
        for device in range(block):
            part = slice(device * chunk, (device + 1) * chunk)
            out_ref[device] = jnp.concatenate([total[part], small[part]], axis=1).astype(low)


def head_grad(place, a, d, sum2, sum_in, sum_c, sum_c2, hd, chunk, block):
    tokens, width = a.shape
    rows = 512
    out = jax.ShapeDtypeStruct((block, chunk, up_to_lanes(3 * hd)), low)
    small = (sum2, sum_in, sum_c, sum_c2)
    return pl.pallas_call(
        functools.partial(head_grad_kernel, hd, chunk),
        grid_spec=pltpu.PrefetchScalarGridSpec(
            num_scalar_prefetch=1,
            grid=(tokens // rows,),
            in_specs=[pl.BlockSpec((rows, size), lambda i, p: (i, 0)) for size in (width, 3 * lanes)] + [whole_spec(v) for v in small],
            out_specs=out_spec(out),
            scratch_shapes=[pltpu.VMEM((3 * lanes, width), exact), pltpu.VMEM((out.shape[2] - 3 * hd, width), exact)],
        ),
        out_shape=out,
        compiler_params=params(16),
        cost_estimate=small_cost,
        name="head_grad",
    )(place, far_off(a), d, *small)


def collect_kernel(hd, in_ref, *refs):
    out_refs, small_ref = refs[:3], refs[3]
    count = in_ref.shape[0] // 2
    small = jnp.zeros((in_ref.shape[1], in_ref.shape[2] - 3 * hd), exact)
    for head in range(count):
        total = in_ref[head].astype(exact) + in_ref[count + head].astype(exact)
        small += total[:, 3 * hd :]
        for i, out_ref in enumerate(out_refs):
            out_ref[:, head * hd : (head + 1) * hd] = total[:, i * hd : (i + 1) * hd]
    small_ref[...] = small.T


def collect(terms_in, hd):
    block, chunk, size = terms_in.shape
    matrix = jax.ShapeDtypeStruct((chunk, block // 2 * hd), exact)
    return pl.pallas_call(
        functools.partial(collect_kernel, hd),
        out_shape=[matrix] * 3 + [jax.ShapeDtypeStruct((size - 3 * hd, chunk), exact)],
        compiler_params=params(8),
        name="collect",
    )(terms_in)


def collect_hidden_kernel(ff, in_ref, out_ref):
    count = in_ref.shape[0] // 2
    for piece in range(count):
        total = unfold(in_ref[piece].astype(exact) + in_ref[count + piece].astype(exact), ff)
        for slot in range(2):
            at = (slot * count + piece) * (ff // 2)
            out_ref[:, at : at + ff // 2] = total[:, slot * (ff // 2) : (slot + 1) * (ff // 2)]


def collect_hidden(terms_in, ff):
    block, _, size = terms_in.shape
    return pl.pallas_call(
        functools.partial(collect_hidden_kernel, ff),
        out_shape=jax.ShapeDtypeStruct((size * 8 // ff, block // 2 * ff), exact),
        compiler_params=params(8),
        name="collect_hidden",
    )(terms_in)


def attend_kernel(hd, coef, q_ref, k_ref, v_ref, o_ref, e_ref, inverse_ref, vt_ref):
    @pl.when(pl.program_id(0) == 0)
    def _():
        vt_ref[...] = v_ref[...].T

    s = dot(k_ref[...], q_ref[...], 1, 1)
    top = jnp.max(s, axis=0, keepdims=True)
    e = jnp.exp2((s - top) * coef)
    total = jnp.sum(e, axis=0, keepdims=True)
    inverse = 1.0 / total
    e = e.astype(low)
    e_ref[0] = e
    inverse_ref[0] = inverse
    o = (dot(vt_ref[...], e, 1, 0) * inverse).astype(low)
    for piece in range(o_ref.shape[0]):
        o_ref[piece] = o[:hd, piece * lanes : (piece + 1) * lanes]


def attend(q, q_at, k, k_at, v, v_at, hd, rows):
    tokens, keys = q.shape[0], k.shape[0]
    coef = math.log2(math.e) / hd**0.5
    steps = tokens // rows
    return pl.pallas_call(
        functools.partial(attend_kernel, hd, coef),
        grid=(steps,),
        in_specs=[
            pl.BlockSpec((rows, lanes), lambda i: (i, q_at)),
            pl.BlockSpec((keys, lanes), lambda i: (0, k_at)),
            pl.BlockSpec((keys, lanes), lambda i: (0, v_at)),
        ],
        out_specs=[
            pl.BlockSpec((rows // lanes, hd, lanes), lambda i: (i, 0, 0)),
            pl.BlockSpec((1, keys, rows), lambda i: (i, 0, 0)),
            pl.BlockSpec((1, 1, rows), lambda i: (i, 0, 0)),
        ],
        out_shape=[
            jax.ShapeDtypeStruct((tokens // lanes, hd, lanes), low),
            pltpu.HBM((steps, keys, rows), low),
            jax.ShapeDtypeStruct((steps, 1, rows), exact),
        ],
        scratch_shapes=[pltpu.VMEM((lanes, keys), low)],
        compiler_params=params(10 * keys // 1024),
        cost_estimate=small_cost,
        name="attend",
    )(q, k, v)


def attend_back_kernel(hd, scale, span, q_ref, k_ref, v_ref, do_ref, e_ref, inverse_ref, out_ref, sum_ref, kt_ref, dk_sum, dv_sum):
    step = pl.program_id(0)
    rows = q_ref.shape[0]

    @pl.when(step == 0)
    def _():
        kt_ref[...] = k_ref[...].T
        dk_sum[...] = jnp.zeros_like(dk_sum)
        dv_sum[...] = jnp.zeros_like(dv_sum)
        sum_ref[...] = jnp.zeros_like(sum_ref)

    pieces = do_ref.shape[0]
    dot_t = jnp.concatenate([do_ref[piece] for piece in range(pieces)], axis=1)
    fill = jnp.zeros((lanes - hd, dot_t.shape[1]), low)
    dot_t = jnp.concatenate([dot_t, fill], axis=0)
    q = q_ref[...]
    p = e_ref[0].astype(exact) * inverse_ref[0]
    dp = dot(v_ref[...], dot_t, 1, 0)
    r = jnp.sum(p * dp, axis=0, keepdims=True)
    ds = (p * (dp - r)).astype(low)
    dv_sum[...] += dot(p.astype(low), dot_t.T, 1, 0)
    dk_sum[...] += dot(ds, q, 1, 0)
    dq = dot(kt_ref[...], ds, 1, 0) * scale
    head = lax.broadcasted_iota(jnp.int32, dq.shape, 0) < hd
    dq = jnp.where(head, dq, 0.0).T.astype(low)
    out_ref[pl.ds(pl.multiple_of(span + step * rows, rows), rows), :lanes] = dq.astype(out_ref.dtype)
    sum_ref[0:1, :lanes] += jnp.sum(dq.astype(exact), axis=0, keepdims=True)

    @pl.when(step == pl.num_programs(0) - 1)
    def _():
        head = lax.broadcasted_iota(jnp.int32, dk_sum.shape, 1) < hd
        dk = jnp.where(head, dk_sum[...] * scale, 0.0)
        dv = dv_sum[...].astype(out_ref.dtype)
        out_ref[:, lanes : 2 * lanes] = dk.astype(out_ref.dtype)
        out_ref[:, 2 * lanes :] = dv
        sum_ref[0:1, 2 * lanes :] = jnp.sum(dv.astype(exact), axis=0, keepdims=True)


def attend_back(q, q_at, k, k_at, v, v_at, do, e, inverse, hd, rows, span, kind):
    tokens, keys = q.shape[0], k.shape[0]
    scale = 1.0 / hd**0.5
    steps = tokens // rows
    return pl.pallas_call(
        functools.partial(attend_back_kernel, hd, scale, span),
        grid=(steps,),
        in_specs=[
            pl.BlockSpec((rows, lanes), lambda i: (i, q_at)),
            pl.BlockSpec((keys, lanes), lambda i: (0, k_at)),
            pl.BlockSpec((keys, lanes), lambda i: (0, v_at)),
            pl.BlockSpec((rows // lanes, hd, lanes), lambda i: (i, 0, 0)),
            pl.BlockSpec((1, keys, rows), lambda i: (i, 0, 0)),
            pl.BlockSpec((1, 1, rows), lambda i: (i, 0, 0)),
        ],
        out_specs=[pl.BlockSpec((keys, 3 * lanes), lambda i: (0, 0)), pl.BlockSpec((8, 3 * lanes), lambda i: (0, 0))],
        out_shape=[pltpu.HBM((keys, 3 * lanes), kind), jax.ShapeDtypeStruct((8, 3 * lanes), exact)],
        scratch_shapes=[
            pltpu.VMEM((lanes, keys), low),
            pltpu.VMEM((keys, lanes), exact),
            pltpu.VMEM((keys, lanes), exact),
        ],
        compiler_params=params(14 * keys // 1024),
        cost_estimate=small_cost,
        name="attend_back",
    )(q, k, v, do, far_off(e), inverse)


def body(
    hidden_in,
    clip_lengths,
    ln1_gain,
    ln1_bias,
    w_query,
    b_query,
    w_key,
    w_value,
    b_value,
    w_out,
    b_out,
    ln2_gain,
    ln2_bias,
    w_fc1,
    b_fc1,
    w_fc2,
    b_fc2,
    cotangent,
):
    micro, rows, width = hidden_in.shape
    at = Layout(micro)
    place = at.place
    hd = width // heads
    own = 2 * rows
    tokens = at.half * own
    clips = clip_lengths.shape[1]
    chunk = width // at.block
    step_rows = 256

    vectors = [at.to_block(v) for v in (ln1_gain, ln1_bias, b_query, b_value, b_out, ln2_gain, ln2_bias, b_fc2)]
    ff_bias = at.to_block(b_fc1)
    ff_rows = ff_bias.shape[0]
    first, second = pack(place, hidden_in, jnp.stack(vectors), ff_bias[None])
    blocked = [at.to_block(w) for w in (w_query, w_key, w_value, w_fc1)]
    w_in, w1 = deal(*blocked, hd, at.block)
    ff = blocked[3].shape[1] // heads
    second = at.partner(second)
    wo_shard = at.to_block(w_out)
    g_far = jnp.concatenate([lax.dynamic_index_in_dim(cotangent, 1 - at.mine, 0, False), wo_shard], axis=0)
    second, w_in, w1, g_far = together(second, w_in, w1, g_far)

    x_own, small, *parts = arrange(place, first, second, rows)
    marks = []
    small_far = at.swapped(small, 1)
    parts[2] = jnp.concatenate([parts[2], small[None], small_far[None]], axis=1)
    c1 = small.reshape(2, extra_rows, width)[:, 0, lanes : lanes + ff_rows].reshape(1, 2 * ff_rows).astype(exact)
    w2_shard = at.to_block(w_fc2)
    mine, others, (g_far, *w2_far) = at.gather_tree(parts, [g_far, w2_shard[: ff_rows // 2], w2_shard[ff_rows // 2 :]])
    w2 = jnp.concatenate(at.ordered(w2_shard, jnp.concatenate(w2_far, axis=0)), axis=0)
    g_far, wo_far = g_far[:rows], g_far[rows:]
    wo = jnp.concatenate(at.ordered(wo_shard, wo_far), axis=0)
    *mine, w_in, wo = together(*mine, w_in, wo)
    w_in = at.exchange_block(w_in)
    wo = at.gather_half(wo).reshape(heads, 2, chunk, width).transpose(1, 0, 2, 3).reshape(width, width)
    before = norm(place, False, mine, (), hd, own, chunk)
    a1, table = norm(place, True, others, before, hd, own, chunk)
    w_in, a1, table = together(w_in, a1, table)

    w1 = at.exchange_block(tie(w1, w_in))
    w_in = w_in.reshape(width, 3 * hd)
    g_own = jnp.concatenate(at.ordered(lax.dynamic_index_in_dim(cotangent, at.mine, 0, False), g_far), axis=0)
    g_all = at.gather_half(g_own)

    lengths = lax.dynamic_index_in_dim(clip_lengths, at.mine, 0, False)
    ends = jnp.cumsum(lengths)
    ends = ends - at.me // at.block * tokens

    a1 = a1.reshape(tokens, width)
    qkv, w_pad = project(place, ends, a1, w_in, table, hd, rows)
    span = 0
    qkv_at = (qkv, 0, qkv, 1, qkv, 2)
    if at.blocks > 1:
        span = tokens // 2
        ahead = [(d, d + at.block) for d in range(at.count - at.block)]
        behind = [(d + at.block, d) for d in range(at.count - at.block)]
        nothing = jnp.where(jnp.arange(2 * lanes)[None] == hd + clips, 1.0, 0.0).astype(low)
        kv = qkv[:, lanes:]
        slots = kv.reshape(heads, 2, rows, 2 * lanes)
        before = at.send(slots[:, 1].reshape(span, 2 * lanes), ahead)
        after = at.send(slots[:, 0].reshape(span, 2 * lanes), behind)
        before = jnp.where(at.me < at.block, nothing, before)
        after = jnp.where(at.me >= at.count - at.block, nothing, after)
        kv = jnp.concatenate([before, kv, after], axis=0)
        qkv_at = (qkv, 0, kv, 0, kv, 1)
    o_head, expo, inverse = attend(*qkv_at, hd, step_rows)
    o_head, w1 = together(o_head, w1)
    w1 = unfolded(w1, ff)
    o_own = at.exchange_half(o_head)

    x2, *parts = join(x_own, o_own, wo, table)
    g_split = g_all.reshape(8, 2, own, width)
    mine, others, _ = at.gather_tree(parts)

    *before, kept, sum_c = feed(place, False, mine, g_split, w1, w2, c1, (), own, low)
    hid, du, y, away, sum_c2 = feed(place, True, others, g_split, w1, w2, c1, before, own, low)
    y = lax.psum_scatter(y.reshape(tokens, width), "dev", scatter_dimension=0, tiled=True, axis_index_groups=at.halves)
    marks, made = [], []

    def second_terms(marks):
        made.append(fc2_grad(tie(hid, marks[0]), g_split))
        return made

    def first_terms(marks):
        made.append(fc1_grad(place, mine, others, tie(du, marks[1]), chunk))
        return made[1:]

    kept, got = at.reduce_half(away, kept, marks, {1: second_terms, 2: first_terms})
    back_w2 = at.exchanged(tie(made[0], marks[1]))
    d_w1 = made[1]
    *sums, d_w1 = together(*kept, *got, *back_w2, d_w1)
    kept, got, back_w2 = sums[:3], sums[3:6], sums[6:]

    dx2, ga_own, do_own, sum2 = second_back(kept, got, x2, g_own, table, wo, hd)
    do_head = at.exchange_half(do_own)
    ga = at.gather_half(ga_own).reshape(tokens, width)
    d_w1 = at.exchange_block(tie(d_w1, do_head))

    kind = low if at.blocks == 1 else exact
    dqkv, sum_in = attend_back(*qkv_at, do_head, expo, inverse, hd, step_rows, span, kind)
    if at.blocks > 1:
        dkv = dqkv[:, lanes:]
        to_before = at.send(dkv[:span].astype(low), behind).astype(exact)
        to_after = at.send(dkv[span + tokens :].astype(low), ahead).astype(exact)
        halo = jnp.stack([t.reshape(heads, rows, 2 * lanes) for t in (to_after, to_before)], axis=1)
        dkv = dkv[span : span + tokens] + halo.reshape(tokens, 2 * lanes)
        dqkv = jnp.concatenate([dqkv[span : span + tokens, :lanes], dkv], axis=1).astype(low)
        sum_in = jnp.broadcast_to(jnp.sum(dqkv.astype(exact), axis=0, keepdims=True), (8, 3 * lanes))
    dqkv, sum_in, y, d_w1 = together(dqkv, sum_in, y, d_w1)
    split = dqkv.reshape(8, 2, own, 3 * lanes)
    away = terms(place, True, split, w_pad, 1, low)
    marks, made = [], []

    def projections(marks):
        made.append(head_grad(place, a1, tie(dqkv, marks[0]), sum2, sum_in, sum_c, sum_c2, hd, chunk, at.block))
        return made

    def output_weight(marks):
        late, o_late = together(ga, o_head, marks[1])[:2]
        made.append(output_grad(o_late, late.reshape(at.half, own, width)))
        return made[1:]

    kept, got = at.reduce_half(away, terms(place, False, split, w_pad, 1, low), marks, {1: projections, 2: output_weight})
    d_in = at.exchange_block(tie(made[0], marks[1]))
    kept_first, d_in = together(kept[0], d_in)
    kept = (kept_first, *kept[1:])

    dx, vec = first_back(kept, got, x_own, dx2, table, chunk, at.block)
    y, d_w1, *back_w2 = together(y, d_w1, *back_w2, dx)[:4]
    out = (x2 + (y.astype(exact) + table[7])).astype(low)

    input_grad = at.exchanged(dx.reshape(2, rows, width))
    layer_out = at.exchanged(out.reshape(2, rows, width))
    layer_out, input_grad = (jnp.stack(at.ordered(*v)).astype(exact) for v in (layer_out, input_grad))
    back_wo = at.send_rows_back(made[1])
    grad_w2 = at.from_block(back_w2[0].astype(exact) + back_w2[1].astype(exact))
    grad_w1 = at.from_block(collect_hidden(d_w1, ff))
    grad_wo = at.from_block(back_wo[0].astype(exact) + back_wo[1].astype(exact))
    vec = jnp.sum(at.exchange_block(vec), axis=(0, 1))
    grad_g1 = at.from_block(vec[:chunk])
    grad_b1 = at.from_block(vec[lanes // 2 : lanes // 2 + chunk])
    *grads, vec = collect(d_in, hd)
    grad_wq, grad_wk, grad_wv = (at.from_block(v) for v in grads)
    pieces = [at.from_block(vec[i]) for i in range(6)]
    grad_g2, grad_b2, grad_bo, grad_bf2, grad_bq, grad_bv = pieces
    grad_c1 = at.from_block(vec[8 : 8 + ff_rows // chunk].reshape(ff_rows))
    return (
        layer_out,
        input_grad,
        grad_g1,
        grad_b1,
        grad_wq,
        grad_bq,
        grad_wk,
        grad_wv,
        grad_bv,
        grad_wo,
        grad_bo,
        grad_g2,
        grad_b2,
        grad_w1,
        grad_c1,
        grad_w2,
        grad_bf2,
    )


def solution(mesh):
    tokens, vector, matrix = P(None, "dev", None), P("dev"), P("dev", None)
    grads = (vector, vector, matrix, vector, matrix, matrix, vector, matrix, vector, vector, vector, matrix, vector, matrix, vector)
    return jax.shard_map(
        body,
        mesh=mesh,
        in_specs=(tokens, P()) + grads + (tokens,),
        out_specs=(tokens, tokens) + grads,
        check_vma=False,
    )
```

```python
import functools
import math

import jax
import jax.numpy as jnp
from jax import lax
from jax.experimental import pallas as pl
from jax.experimental.pallas import tpu as pltpu
from jax.sharding import PartitionSpec as P

eps = 1e-05
heads = 16
low = jnp.bfloat16
exact = jnp.float32
far = -1e30
lanes = 128
extra_rows = 8


def dot(a, b, ca, cb):
    return lax.dot_general(a, b, (((ca,), (cb,)), ((), ())), preferred_element_type=exact)


def normalized(v):
    mean = jnp.mean(v, axis=-1, keepdims=True)
    cent = v - mean
    inverse = lax.rsqrt(jnp.mean(cent * cent, axis=-1, keepdims=True) + eps)
    return cent * inverse, inverse


def norm_back(unit, inverse, gain, grad):
    scaled = grad * gain
    along = jnp.mean(scaled * unit, axis=-1, keepdims=True)
    return inverse * (scaled - jnp.mean(scaled, axis=-1, keepdims=True) - unit * along)


def tie(value, *others):
    return lax.optimization_barrier((value,) + others)[0]


def together(*values):
    return lax.optimization_barrier(values)


class Layout:
    def __init__(self, micro):
        self.count = lax.axis_size("dev")
        self.half = heads
        self.block = micro * heads
        self.blocks = self.count // self.block
        self.me = lax.axis_index("dev")
        self.rank = self.me % self.block
        self.mine = self.rank // self.half
        self.head = self.rank % self.half
        self.odd = self.rank % 2
        bits = [(self.me // bit) % 2 for bit in (1, 2, 4, 8)]
        self.place = jnp.stack(bits + [self.mine, self.head, self.odd]).astype(jnp.int32)
        self.halves = [list(range(s, s + self.half)) for s in range(0, self.count, self.half)]
        self.whole = [list(range(s, s + self.block)) for s in range(0, self.count, self.block)]
        self.rows = [list(range(s, s + self.blocks)) for s in range(0, self.count, self.blocks)]
        first = [d // self.half % 2 for d in range(self.count)]
        base = [d // self.block * self.block + 2 * (d % self.half) for d in range(self.count)]
        self.even_first = [(d, base[d] + first[d]) for d in range(self.count)]
        self.odd_first = [(d, base[d] + 1 - first[d]) for d in range(self.count)]

    def send(self, value, pairs):
        return lax.ppermute(value, "dev", pairs)

    def swapped(self, value, bit):
        return self.send(value, [(d, d ^ bit) for d in range(self.count)])

    def to_block(self, value):
        if self.blocks == 1:
            return value
        value = lax.all_gather(value, "dev", axis=0, tiled=True, axis_index_groups=self.rows)
        return self.send(value, [(d, d % self.blocks * self.block + d // self.blocks) for d in range(self.count)])

    def from_block(self, value):
        if self.blocks == 1:
            return value
        value = self.send(value, [(d % self.blocks * self.block + d // self.blocks, d) for d in range(self.count)])
        return lax.psum_scatter(value, "dev", scatter_dimension=0, tiled=True, axis_index_groups=self.rows)

    def partner(self, value):
        return self.swapped(value, self.half)

    def ordered(self, kept, got):
        return jnp.where(self.mine == 0, kept, got), jnp.where(self.mine == 0, got, kept)

    def exchanged(self, value):
        kept = lax.dynamic_index_in_dim(value, self.mine, 0, False)
        return kept, self.partner(lax.dynamic_index_in_dim(value, 1 - self.mine, 0, False))

    def send_rows_back(self, value):
        first = lax.dynamic_index_in_dim(value, self.mine, 0, False)
        second = lax.dynamic_index_in_dim(value, 1 - self.mine, 0, False)
        return self.send(first, self.even_first), self.send(second, self.odd_first)

    def gather_half(self, value):
        return lax.all_gather(value, "dev", axis=0, axis_index_groups=self.halves)

    def exchange_half(self, value):
        return lax.all_to_all(value, "dev", 0, 0, tiled=True, axis_index_groups=self.halves)

    def exchange_block(self, value):
        return lax.all_to_all(value, "dev", 0, 0, tiled=True, axis_index_groups=self.whole)

    def gather_tree(self, parts, beside=()):
        brought = []
        for stage in range(3):
            got = [self.swapped(piece, order[stage]) for piece, order in zip(parts, part_orders)]
            if beside:
                far = self.partner(tie(beside[stage], parts[0]))
                first, far = together(got[0], far)
                got = [first, *got[1:]]
                brought.append(far)
            if stage < 2:
                parts = merge(parts, got)
        other = [self.swapped(piece, 1) for piece in (*parts, *got)]
        return (*parts, *got), other, brought

    def reduce_half(self, away, kept, marks=None, before=None, arrived=None):
        got = [self.swapped(away, 1)]
        kept = [kept]
        for stage in range(3):
            if before and stage in before:
                got = [tie(got[0], *before[stage](marks)), *got[1:]]
            away, kept = split_terms(self.place, stage, kept, got)
            if marks is not None:
                marks.append(away[0])
            got = [self.swapped(piece, order[stage]) for piece, order in zip(away, part_orders)]
            if arrived is not None:
                arrived.append(got[2])
        return kept, got


small_cost = pl.CostEstimate(flops=1 << 10, bytes_accessed=1 << 10, transcendentals=0)


def far_off(v):
    return pltpu.with_memory_space_constraint(v, pltpu.HBM)


def params(megabytes):
    return pltpu.CompilerParams(vmem_limit_bytes=megabytes << 20)


part_orders = ((8, 4, 2), (4, 2, 8), (2, 8, 4))


def part_bounds(tokens):
    cut = tokens * 3 // 8 // 16 * 16
    return ((0, cut), (cut, 2 * cut), (2 * cut, tokens))


def split_kernel(stage, place_ref, *refs):
    place = {bit: place_ref[i] for i, bit in enumerate((1, 2, 4, 8))}
    if stage == 0:
        kept_ref, got_ref = refs[:2]
        outs = refs[2:]
        bounds = part_bounds(kept_ref.shape[1])
    else:
        outs = refs[6:]
    for part, order in enumerate(part_orders):
        left = [bit for bit in (8, 4, 2) if bit not in order[:stage]]
        at = left.index(order[stage])
        below = 1 << (len(left) - 1 - at)
        for half, side in ((0, 1 - place[order[stage]]), (1, place[order[stage]])):
            out_ref = outs[part + 3 * half]
            for j in range(out_ref.shape[0]):
                index = (j // below * 2 + side) * below + j % below
                if stage == 0:
                    start, end = bounds[part]
                    term = kept_ref[index, start:end].astype(exact) + got_ref[index, start:end].astype(exact)
                else:
                    term = refs[part][index].astype(exact) + refs[3 + part][index].astype(exact)
                out_ref[j] = term.astype(out_ref.dtype)


def split_terms(place, stage, kept, got):
    width = kept[0].shape[-1]
    bounds = part_bounds(kept[0].shape[1]) if stage == 0 else [(0, k.shape[1]) for k in kept]
    count = kept[0].shape[0] // 2
    cols = (256, 640, width)[stage]
    spec = lambda n, t: pl.BlockSpec((n, t, cols), lambda i, p: (0, 0, i))
    outs = [(count, end - start) for start, end in bounds]
    res = pl.pallas_call(
        functools.partial(split_kernel, stage),
        grid_spec=pltpu.PrefetchScalarGridSpec(
            num_scalar_prefetch=1,
            grid=(width // cols,),
            in_specs=[spec(*v.shape[:2]) for v in (*kept, *got)],
            out_specs=[spec(*o) for o in outs] * 2,
        ),
        out_shape=[jax.ShapeDtypeStruct(o + (width,), low) for o in outs]
        + [(pltpu.HBM if stage == 2 else jax.ShapeDtypeStruct)(o + (width,), exact) for o in outs],
        compiler_params=params(10),
        cost_estimate=small_cost,
        name="split_terms",
    )(place, *kept, *got)
    return res[:3], res[3:]


def last_sum(refs):
    return jnp.concatenate([refs[i][0].astype(exact) + refs[3 + i][0].astype(exact) for i in range(3)], axis=0)


def pack_kernel(place_ref, x_ref, v_ref, c_ref, first_ref, second_ref):
    rows, width = x_ref.shape[1:]
    mine = place_ref[4]
    fill = jnp.zeros((v_ref.shape[0], width - v_ref.shape[1]), exact)
    small = jnp.concatenate([v_ref[...].astype(exact), fill], axis=1)
    c = jnp.concatenate([c_ref[...].astype(exact), jnp.zeros((1, width - lanes - c_ref.shape[1]), exact)], axis=1)
    c = jnp.concatenate([jnp.zeros((1, lanes), exact), c], axis=1)
    row = lax.broadcasted_iota(jnp.int32, small.shape, 0)
    small = small + jnp.where(row == 0, c, 0.0)
    tail = small.astype(low)
    for out_ref, index in ((first_ref, mine), (second_ref, 1 - mine)):
        out_ref[:rows] = x_ref[index]
        out_ref[rows:] = tail


def pack(place, x, vectors, c):
    rows, width = x.shape[1:]
    out = jax.ShapeDtypeStruct((rows + extra_rows, width), low)
    return pl.pallas_call(
        pack_kernel,
        grid_spec=pltpu.PrefetchScalarGridSpec(
            num_scalar_prefetch=1,
            grid=(1,),
            in_specs=[whole_spec(v) for v in (x, vectors, c)],
            out_specs=[out_spec(out)] * 2,
        ),
        out_shape=[out, out],
        compiler_params=params(6),
        name="pack",
    )(place, far_off(x), vectors, c)


def arrange_kernel(rows, place_ref, first_ref, second_ref, x_ref, small_ref, *part_refs):
    mine = place_ref[4]
    for side, refs in enumerate(((first_ref, second_ref), (second_ref, first_ref))):

        @pl.when(mine == side)
        def _():
            x = jnp.concatenate([ref[:rows] for ref in refs], axis=0)
            x_ref[...] = x
            tail = [ref[rows:].astype(exact) for ref in refs]
            small_ref[...] = jnp.concatenate(tail, axis=0).astype(low)
            for part_ref, (start, end) in zip(part_refs, part_bounds(2 * rows)):
                part_ref[0] = x[start:end]


def arrange(place, first, second, rows):
    width = first.shape[1]
    shapes = [(2 * rows, width), (2 * extra_rows, width)]
    shapes += [(1, end - start, width) for start, end in part_bounds(2 * rows)]
    outs = [jax.ShapeDtypeStruct(shape, low) for shape in shapes]
    return pl.pallas_call(
        functools.partial(arrange_kernel, rows),
        grid_spec=pltpu.PrefetchScalarGridSpec(
            num_scalar_prefetch=1,
            grid=(1,),
            in_specs=[whole_spec(first), whole_spec(second)],
            out_specs=[out_spec(out) for out in outs],
        ),
        out_shape=outs,
        compiler_params=params(6),
        name="arrange",
    )(place, first, second)


def up_to_lanes(size):
    return -(-size // lanes) * lanes


def fold(v):
    return jnp.concatenate([v[i : i + 8] for i in range(0, v.shape[0], 8)], axis=1)


def unfold(v, size):
    return jnp.concatenate([v[:, i : i + size] for i in range(0, v.shape[1], size)], axis=0)


def unfold_kernel(in_ref, out_ref):
    size = out_ref.shape[1]
    chunk = in_ref.shape[2] // size * 8
    for device in range(0, in_ref.shape[0], 2):
        rows = [unfold(in_ref[device + i].astype(exact), size) for i in range(2)]
        out_ref[device * chunk : (device + 2) * chunk] = jnp.concatenate(rows, axis=0).astype(low)


def unfolded(v, size):
    return pl.pallas_call(
        unfold_kernel,
        out_shape=jax.ShapeDtypeStruct((v.size // size, size), low),
        compiler_params=params(8),
        cost_estimate=small_cost,
        name="unfolded",
    )(v)


def deal_kernel(hd, q_ref, k_ref, v_ref, w_ref, in_ref, hidden_ref):
    ff = w_ref.shape[1] // heads
    side_by_side = lambda pieces: jnp.concatenate([piece.astype(exact) for piece in pieces], axis=1).astype(low)
    for head in range(heads):
        at = [(slot * heads + head) * (ff // 2) for slot in range(2)]
        hidden = jnp.concatenate([w_ref[:, a : a + ff // 2].astype(exact) for a in at], axis=1)
        hidden = fold(hidden).astype(low)
        columns = side_by_side([ref[:, head * hd : (head + 1) * hd] for ref in (q_ref, k_ref, v_ref)])
        for device in range(head, in_ref.shape[0], heads):
            in_ref[device] = columns
            hidden_ref[device] = hidden


def deal(q, k, v, w, hd, block):
    chunk, ff = q.shape[0], w.shape[1] // heads
    return pl.pallas_call(
        functools.partial(deal_kernel, hd),
        out_shape=[jax.ShapeDtypeStruct(shape, low) for shape in ((block, chunk, 3 * hd), (block, 8, chunk * ff // 8))],
        compiler_params=params(8),
        name="deal",
    )(*map(far_off, (q, k, v, w)))


def merge_kernel(*refs):
    for i in range(3):
        count = refs[i].shape[0]
        refs[6 + i][:count] = refs[i][...]
        refs[6 + i][count:] = refs[3 + i][...]


def merge(parts, got):
    width = parts[0].shape[2]
    cols = 640
    spec = lambda shape: pl.BlockSpec(shape[:2] + (cols,), lambda i: (0, 0, i))
    outs = [(2 * p.shape[0],) + p.shape[1:] for p in parts]
    return pl.pallas_call(
        merge_kernel,
        grid=(width // cols,),
        in_specs=[spec(v.shape) for v in (*parts, *got)],
        out_specs=[spec(o) for o in outs],
        out_shape=[jax.ShapeDtypeStruct(o, low) for o in outs],
        compiler_params=params(8),
        name="merge",
    )(*parts, *got)


def out_spec(v):
    return pl.BlockSpec(v.shape, lambda *_: (0,) * len(v.shape))


def tree_rows(place_ref, chip, refs, fill):
    mine = place_ref[1] + 2 * place_ref[2] + 4 * place_ref[3]
    apart = chip ^ mine
    step = {8: apart // 4, 4: apart // 2 % 2, 2: apart % 2}
    for part, order in enumerate(part_orders):
        index = 2 * step[order[1]] + step[order[0]]
        for late in range(2):

            @pl.when(step[order[2]] == late)
            def _():
                fill(part, refs[part + 3 * late], index)


def fill_rows(place_ref, chip, refs, out_ref, base, own):
    bounds = part_bounds(own)

    def fill(part, ref, index):
        start, end = bounds[part]
        out_ref[pl.ds(base + start, end - start)] = ref[index, : end - start]

    tree_rows(place_ref, chip, refs, fill)


def whole_spec(v):
    return pl.BlockSpec(v.shape, lambda *_: (0,) * len(v.shape), pipeline_mode=pl.Buffered(1))


def norm_kernel(hd, chunk, first, place_ref, *refs):
    pieces = refs[:6]
    a_ref, table_ref, x_scr = refs[-3:]
    step, _, own, width = a_ref.shape

    @pl.when(pl.program_id(0) == 0)
    def _():
        if first:
            tail = part_bounds(own)[2]

            def fill(chip, part, ref, index):
                if part != 2:
                    return
                small = ref[index, tail[1] - tail[0] :].astype(exact)
                for far_core in range(2):
                    for slot in range(2):
                        line = (2 * far_core + slot) * extra_rows
                        piece = small[line : line + extra_rows, :chunk]
                        for core in range(2):

                            @pl.when(place_ref[0] == core)
                            def _():
                                at = (heads * slot + 2 * chip + (core ^ far_core)) * chunk
                                table_ref[:, at : at + chunk] = piece

            for chip in range(8):
                tree_rows(place_ref, chip, pieces, functools.partial(fill, chip))
        else:
            table_ref[...] = refs[6][...]

    for j in range(step):
        fill_rows(place_ref, pl.program_id(0) * step + j, pieces, x_scr, j * own, own)
    unit, _ = normalized(x_scr[...].astype(exact))
    a_ref[...] = (unit * table_ref[0:1] + table_ref[1:2]).astype(low).reshape(a_ref.shape)


def norm(place, other, pieces, before, hd, own, chunk):
    width = pieces[0].shape[2]
    step = 4
    side = (lambda p: 1 - p[0]) if other else (lambda p: p[0])
    table = jax.ShapeDtypeStruct((extra_rows, width), exact)
    return pl.pallas_call(
        functools.partial(norm_kernel, hd, chunk, not before),
        grid_spec=pltpu.PrefetchScalarGridSpec(
            num_scalar_prefetch=1,
            grid=(8 // step,),
            in_specs=[whole_spec(v) for v in pieces] + ([whole_spec(table), pl.BlockSpec(memory_space=pl.ANY)] if before else []),
            out_specs=[pl.BlockSpec((step, 1, own, width), lambda i, p: (i, side(p), 0, 0)), out_spec(table)],
            scratch_shapes=[pltpu.VMEM((step * own, width), low)],
        ),
        out_shape=[pltpu.HBM((8, 2, own, width), low), table],
        input_output_aliases={8: 0} if before else {},
        compiler_params=params(30),
        cost_estimate=small_cost,
        name="norm",
    )(place, *pieces, *before[::-1])


def project_kernel(hd, clips, own_rows, place_ref, ends_ref, a_ref, w_ref, table_ref, qkv_ref, pad_ref, bias_ref):
    rows, width = a_ref.shape

    @pl.when(pl.program_id(0) == 0)
    def _():
        w = w_ref[...].astype(exact)
        fill = jnp.zeros((width, lanes - hd), exact)
        w = [v for i in range(3) for v in (w[:, i * hd : (i + 1) * hd], fill)]
        pad_ref[...] = jnp.concatenate(w, axis=1).astype(low)
        bias_ref[...] = jnp.zeros_like(bias_ref)
        for h in range(heads):

            @pl.when(place_ref[5] == h)
            def _():
                for line, at in ((2, 0), (3, 2 * lanes)):
                    bias_ref[0:1, at : at + hd] = table_ref[line : line + 1, h * hd : (h + 1) * hd]

    qkv = dot(a_ref[...], pad_ref[...], 1, 0) + bias_ref[0:1]
    column = lax.broadcasted_iota(jnp.int32, (rows, lanes), 1) - hd
    row = lax.broadcasted_iota(jnp.int32, (rows, lanes), 0) + pl.program_id(0) * rows
    shift = own_rows.bit_length() - 1
    token = (lax.shift_right_logical(row, shift) & 1) * (heads * own_rows)
    token += lax.shift_right_logical(row, shift + 1) * own_rows + (row & (own_rows - 1))
    clip = jnp.zeros_like(token)
    for i in range(clips):
        clip += (ends_ref[i] <= token).astype(jnp.int32)
    match = clip == column
    marked = (column >= 0) & (column <= clips)
    qkv_ref[:, :lanes] = (qkv[:, :lanes] + jnp.where(marked & ~match, far, 0.0)).astype(low)
    qkv_ref[:, lanes : 2 * lanes] = (qkv[:, lanes : 2 * lanes] + jnp.where(marked & match, 1.0, 0.0)).astype(low)
    qkv_ref[:, 2 * lanes :] = qkv[:, 2 * lanes :].astype(low)


def project(place, ends, a, w, table, hd, own_rows):
    tokens, width = a.shape
    rows = 512
    clips = ends.shape[0]
    assert own_rows & (own_rows - 1) == 0
    wide = jax.ShapeDtypeStruct((width, 3 * lanes), low)
    return pl.pallas_call(
        functools.partial(project_kernel, hd, clips, own_rows),
        grid_spec=pltpu.PrefetchScalarGridSpec(
            num_scalar_prefetch=2,
            grid=(tokens // rows,),
            in_specs=[
                pl.BlockSpec((rows, width), lambda i, p, e: (i, 0)),
                whole_spec(w),
                whole_spec(table),
            ],
            out_specs=[pl.BlockSpec((rows, 3 * lanes), lambda i, p, e: (i, 0)), out_spec(wide)],
            scratch_shapes=[pltpu.VMEM((8, 3 * lanes), exact)],
        ),
        out_shape=[jax.ShapeDtypeStruct((tokens, 3 * lanes), low), pltpu.HBM(wide.shape, low)],
        compiler_params=params(20),
        cost_estimate=small_cost,
        name="project",
    )(place, ends, far_off(a), w, table)


def join_kernel(x_ref, o_ref, w_ref, table_ref, x2_ref, *part_refs):
    o = o_ref[...].reshape(w_ref.shape[0], o_ref.shape[2])
    x2 = x_ref[...].astype(exact) + (dot(o, w_ref[...], 0, 0) + table_ref[4:5])
    x2_ref[...] = x2
    unit, _ = normalized(x2)
    a2 = (unit * table_ref[5:6] + table_ref[6:7]).astype(low)
    for part_ref, (start, end) in zip(part_refs, part_bounds(x2.shape[0])):
        part_ref[0] = a2[start:end]


def join(x, o, w, table):
    own, width = x.shape
    parts = [jax.ShapeDtypeStruct((1, end - start, width), low) for start, end in part_bounds(own)]
    return pl.pallas_call(
        join_kernel,
        out_shape=[jax.ShapeDtypeStruct(x.shape, exact)] + parts,
        compiler_params=params(10),
        cost_estimate=small_cost,
        name="join",
    )(x, o, far_off(w), table)


def accumulate(total_ref, term):
    @pl.when(pl.program_id(0) == 0)
    def _():
        total_ref[...] = term

    @pl.when(pl.program_id(0) > 0)
    def _():
        total_ref[...] += term


def at_end(write):
    pl.when(pl.program_id(0) == pl.num_programs(0) - 1)(write)


def fc2_grad_kernel(hid_ref, g_ref, out_ref, total_ref):
    rows = math.prod(g_ref.shape[:3])
    accumulate(total_ref, dot(hid_ref[...].reshape(rows, hid_ref.shape[3]), g_ref[...].reshape(rows, g_ref.shape[3]), 0, 0))

    @at_end
    def _():
        out_ref[...] = total_ref[...].astype(low).reshape(out_ref.shape)


def fc2_grad(hid, g):
    eight, two, own, width = g.shape
    ff = hid.shape[3]
    step = 2
    out = jax.ShapeDtypeStruct((2, ff // 2, width), low)
    return pl.pallas_call(
        fc2_grad_kernel,
        grid=(eight // step,),
        in_specs=[pl.BlockSpec((step, two, own, size), lambda i: (i, 0, 0, 0)) for size in (ff, width)],
        out_specs=out_spec(out),
        out_shape=out,
        scratch_shapes=[pltpu.VMEM((ff, width), exact)],
        compiler_params=params(12),
        cost_estimate=small_cost,
        name="fc2_grad",
    )(far_off(hid), far_off(g))


def fc1_grad_kernel(place_ref, *refs):
    mine, others, (du_ref, out_ref, a_scr, total_ref) = refs[:6], refs[6:12], refs[12:]
    chips, two, own, ff = du_ref.shape
    width = a_scr.shape[3]
    bounds = part_bounds(own)
    for j in range(chips):
        chip = pl.program_id(0) * chips + j
        for core, pieces in ((place_ref[0], mine), (1 - place_ref[0], others)):

            def fill(part, ref, index):
                start, end = bounds[part]
                a_scr[j, core, start:end] = ref[index]

            tree_rows(place_ref, chip, pieces, fill)
    rows = chips * two * own
    accumulate(total_ref, dot(du_ref[...].reshape(rows, ff), a_scr[...].reshape(rows, width), 0, 0))

    @at_end
    def _():
        total = total_ref[...].T
        chunk = width // out_ref.shape[0]
        for device in range(out_ref.shape[0]):
            out_ref[device] = fold(total[device * chunk : (device + 1) * chunk]).astype(low)


def fc1_grad(place, mine, others, du, chunk):
    eight, two, own, ff = du.shape
    width = mine[0].shape[2]
    step = 2
    out = jax.ShapeDtypeStruct((width // chunk, 8, chunk * ff // 8), low)
    return pl.pallas_call(
        fc1_grad_kernel,
        grid_spec=pltpu.PrefetchScalarGridSpec(
            num_scalar_prefetch=1,
            grid=(eight // step,),
            in_specs=[whole_spec(v) for v in (*mine, *others)] + [pl.BlockSpec((step, two, own, ff), lambda i, p: (i, 0, 0, 0))],
            out_specs=out_spec(out),
            scratch_shapes=[pltpu.VMEM((step, two, own, width), low), pltpu.VMEM((ff, width), exact)],
        ),
        out_shape=out,
        compiler_params=params(20),
        cost_estimate=small_cost,
        name="fc1_grad",
    )(place, *mine, *others, far_off(du))


def output_grad_kernel(o_ref, ga_ref, out_ref, total_ref):
    term = dot(o_ref[0], ga_ref[0], 1, 0)
    for piece in range(1, o_ref.shape[0]):
        term += dot(o_ref[piece], ga_ref[piece], 1, 0)
    accumulate(total_ref, term)

    @at_end
    def _():
        rows = out_ref.shape[1]
        for side in range(2):
            out_ref[side] = total_ref[side * rows : (side + 1) * rows].astype(low)


def output_grad(o, ga):
    count, hd, own = o.shape
    width = ga.shape[2]
    step = 4
    out = jax.ShapeDtypeStruct((2, hd // 2, width), low)
    return pl.pallas_call(
        output_grad_kernel,
        grid=(count // step,),
        in_specs=[pl.BlockSpec((step, hd, own), lambda i: (i, 0, 0)), pl.BlockSpec((step, own, width), lambda i: (i, 0, 0))],
        out_specs=out_spec(out),
        out_shape=out,
        scratch_shapes=[pltpu.VMEM((hd, width), exact)],
        compiler_params=params(8),
        cost_estimate=small_cost,
        name="output_grad",
    )(o, far_off(ga))


def feed_kernel(place_ref, *refs):
    pieces, (g_ref, w1_ref, w2_ref, c_ref) = refs[:6], refs[6:10]
    hid_ref, du_ref, y_ref, da_ref, sum_ref, a_scr = refs[-6:]
    step, own, width = da_ref.shape
    rows = step * own
    for j in range(step):
        fill_rows(place_ref, pl.program_id(0) * step + j, pieces, a_scr, j * own, own)
    w1, w2 = w1_ref[...], w2_ref[...]
    u = dot(a_scr[...], w1, 1, 0) + c_ref[...]
    d_hid = dot(g_ref[...].reshape(rows, width), w2, 1, 1)
    below = 0.5 * (1.0 + lax.erf(u * math.sqrt(0.5)))
    hid = (u * below).astype(low)
    hid_ref[...] = hid.reshape(hid_ref.shape)
    y_ref[...] = dot(hid, w2, 1, 0).reshape(y_ref.shape).astype(low)
    slope = below + u * (jnp.exp(-0.5 * u * u) * (1.0 / math.sqrt(2.0 * math.pi)))
    du = (d_hid * slope).astype(low)
    du_ref[...] = du.reshape(du_ref.shape)
    da_ref[...] = dot(du, w1, 1, 1).reshape(da_ref.shape).astype(da_ref.dtype)

    @pl.when(pl.program_id(0) == 0)
    def _():
        sum_ref[...] = jnp.zeros_like(sum_ref)

    sum_ref[...] += jnp.sum(du.astype(exact), axis=0, keepdims=True)


def feed(place, other, pieces, g, w1, w2, c1, before, own, kind):
    ff, width = w2.shape
    step = 4
    tokens = 8 * own
    side = (lambda p: 1 - p[0]) if other else (lambda p: p[0])
    pick = lambda size: pl.BlockSpec((step, 1, own, size), lambda i, p: (i, side(p), 0, 0))
    shape = lambda size: pltpu.HBM((8, 2, own, size), low)
    row = pl.BlockSpec((1, ff), lambda i, p: (0, 0))
    return pl.pallas_call(
        feed_kernel,
        grid_spec=pltpu.PrefetchScalarGridSpec(
            num_scalar_prefetch=1,
            grid=(8 // step,),
            in_specs=[whole_spec(v) for v in pieces]
            + [pick(width), whole_spec(w1), whole_spec(w2), row]
            + [pl.BlockSpec(memory_space=pl.ANY)] * len(before),
            out_specs=[pick(ff), pick(ff), pick(width), pl.BlockSpec((step, own, width), lambda i, p: (i, 0, 0)), row],
            scratch_shapes=[pltpu.VMEM((step * own, width), low)],
        ),
        out_shape=[
            shape(ff),
            shape(ff),
            shape(width),
            pltpu.HBM((8, own, width), kind),
            jax.ShapeDtypeStruct((1, ff), exact),
        ],
        input_output_aliases={11: 0, 12: 1, 13: 2} if before else {},
        compiler_params=params(34),
        cost_estimate=small_cost,
        name="feed",
    )(place, *pieces, far_off(g), w1, w2, c1, *before)


def terms_kernel(contract, place_ref, left_ref, right_ref, out_ref):
    rows = out_ref.shape[0] * out_ref.shape[1]
    left = left_ref[...].reshape(rows, left_ref.shape[-1])
    out_ref[...] = dot(left, right_ref[...], 1, contract).reshape(out_ref.shape).astype(out_ref.dtype)


def terms(place, other, left, right, contract, kind):
    eight, two, own, depth = left.shape
    width = right.shape[1 - contract]
    step = 4
    side = (lambda p: 1 - p[0]) if other else (lambda p: p[0])
    return pl.pallas_call(
        functools.partial(terms_kernel, contract),
        grid_spec=pltpu.PrefetchScalarGridSpec(
            num_scalar_prefetch=1,
            grid=(eight // step,),
            in_specs=[
                pl.BlockSpec((step, 1, own, depth), lambda i, p: (i, side(p), 0, 0)),
                pl.BlockSpec(right.shape, lambda i, p: (0, 0)),
            ],
            out_specs=pl.BlockSpec((step, own, width), lambda i, p: (i, 0, 0)),
        ),
        out_shape=jax.ShapeDtypeStruct((eight, own, width), kind),
        compiler_params=params(16),
        cost_estimate=small_cost,
        name="terms",
    )(place, left, right)


def rows_of(values, width):
    fill = jnp.zeros((8 - len(values), width), exact)
    return jnp.concatenate(values + [fill], axis=0)


def second_back_kernel(*refs):
    da2 = last_sum(refs[:6])
    x2_ref, g_ref, table_ref, w_ref, dx2_ref, ga_ref, do_ref, sum_ref = refs[6:]
    unit, inverse = normalized(x2_ref[...])
    g = g_ref[...].astype(exact)
    dx2 = g + norm_back(unit, inverse, table_ref[5:6], da2)
    dx2_ref[...] = dx2
    ga = dx2.astype(low)
    ga_ref[...] = ga
    do_ref[...] = dot(w_ref[...], ga, 1, 1).astype(low).reshape(do_ref.shape)
    total = lambda v: jnp.sum(v, axis=0, keepdims=True)
    sum_ref[...] = rows_of([total(da2 * unit), total(da2), total(ga.astype(exact)), total(g)], ga.shape[1])


def second_back(kept, got, x2, g, table, w, hd):
    own, width = x2.shape
    return pl.pallas_call(
        second_back_kernel,
        out_shape=[
            jax.ShapeDtypeStruct((own, width), exact),
            jax.ShapeDtypeStruct((own, width), low),
            jax.ShapeDtypeStruct((heads, hd, own), low),
            jax.ShapeDtypeStruct((8, width), exact),
        ],
        compiler_params=params(12),
        cost_estimate=small_cost,
        name="second_back",
    )(*map(far_off, (*kept, *got)), x2, g, table, far_off(w))


def first_back_kernel(*refs):
    da1 = last_sum(refs[:6])
    x_ref, dx2_ref, table_ref, dx_ref = refs[6:]
    unit, inverse = normalized(x_ref[...].astype(exact))
    dx_ref[...] = (dx2_ref[...] + norm_back(unit, inverse, table_ref[0:1], da1)).astype(low)


def first_back(kept, got, x, dx2, table):
    return pl.pallas_call(
        first_back_kernel,
        out_shape=jax.ShapeDtypeStruct(x.shape, low),
        compiler_params=params(8),
        name="first_back",
    )(*map(far_off, (*kept, *got)), x, dx2, table)


def head_grad_kernel(hd, chunk, place_ref, a_ref, d_ref, w_ref, table_ref, sum2_ref, sum_in_ref, sum_c_ref, sum_c2_ref, out_ref, total_ref, line_ref):
    accumulate(total_ref, dot(d_ref[...], a_ref[...], 0, 0))

    @at_end
    def _():
        block = out_ref.shape[0]
        head = place_ref[5]
        c = sum_c_ref[...] + sum_c2_ref[...]
        ff_rows = c.shape[1] // 2
        total = jnp.concatenate([total_ref[i * lanes : i * lanes + hd] for i in range(3)], axis=0).T
        line_ref[...] = jnp.zeros_like(line_ref)
        line_ref[0:4] = sum2_ref[0:4]
        for h in range(heads):

            @pl.when(head == h)
            def _():
                for line, at in ((4, 0), (5, 2 * lanes)):
                    line_ref[line : line + 1, h * hd : (h + 1) * hd] = sum_in_ref[0:1, at : at + hd]
                for slot in range(block // heads):
                    for line in range(ff_rows // chunk):
                        at, start = (slot * heads + h) * chunk, slot * ff_rows + line * chunk
                        line_ref[8 + line : 9 + line, at : at + chunk] = c[:, start : start + chunk]

        line_ref[12:14] = table_ref[0:2]
        small = line_ref[...].T
        gain, shift = small[:, 12:13], small[:, 13:14]
        sums = jnp.concatenate([sum_in_ref[0:1, i * lanes : i * lanes + hd] for i in range(3)], axis=1)
        w = w_ref[...].astype(exact)
        d_shift = jnp.sum(w * sums, axis=1, keepdims=True)
        d_gain = (jnp.sum(w * total, axis=1, keepdims=True) - shift * d_shift) / gain
        small = jnp.concatenate([small[:, :6], d_gain, d_shift, small[:, 8:12], jnp.zeros_like(small[:, 12:])], axis=1)
        for device in range(block):
            part = slice(device * chunk, (device + 1) * chunk)
            out_ref[device] = jnp.concatenate([total[part], small[part]], axis=1).astype(low)


def head_grad(place, a, d, w, table, sum2, sum_in, sum_c, sum_c2, hd, chunk, block):
    tokens, width = a.shape
    rows = 512
    out = jax.ShapeDtypeStruct((block, chunk, up_to_lanes(3 * hd)), low)
    small = (w, table, sum2, sum_in, sum_c, sum_c2)
    return pl.pallas_call(
        functools.partial(head_grad_kernel, hd, chunk),
        grid_spec=pltpu.PrefetchScalarGridSpec(
            num_scalar_prefetch=1,
            grid=(tokens // rows,),
            in_specs=[pl.BlockSpec((rows, size), lambda i, p: (i, 0)) for size in (width, 3 * lanes)] + [whole_spec(v) for v in small],
            out_specs=out_spec(out),
            scratch_shapes=[pltpu.VMEM((3 * lanes, width), exact), pltpu.VMEM((out.shape[2] - 3 * hd, width), exact)],
        ),
        out_shape=out,
        compiler_params=params(20),
        cost_estimate=small_cost,
        name="head_grad",
    )(place, far_off(a), d, *small)


def collect_kernel(hd, in_ref, *refs):
    out_refs, small_ref = refs[:3], refs[3]
    count = in_ref.shape[0] // 2
    small = jnp.zeros((in_ref.shape[1], in_ref.shape[2] - 3 * hd), exact)
    for head in range(count):
        total = in_ref[head].astype(exact) + in_ref[count + head].astype(exact)
        small += total[:, 3 * hd :]
        for i, out_ref in enumerate(out_refs):
            out_ref[:, head * hd : (head + 1) * hd] = total[:, i * hd : (i + 1) * hd]
    small_ref[...] = small.T


def collect(terms_in, hd):
    block, chunk, size = terms_in.shape
    matrix = jax.ShapeDtypeStruct((chunk, block // 2 * hd), exact)
    return pl.pallas_call(
        functools.partial(collect_kernel, hd),
        out_shape=[matrix] * 3 + [jax.ShapeDtypeStruct((size - 3 * hd, chunk), exact)],
        compiler_params=params(8),
        name="collect",
    )(terms_in)


def collect_hidden_kernel(ff, in_ref, out_ref):
    count = in_ref.shape[0] // 2
    for piece in range(count):
        total = unfold(in_ref[piece].astype(exact) + in_ref[count + piece].astype(exact), ff)
        for slot in range(2):
            at = (slot * count + piece) * (ff // 2)
            out_ref[:, at : at + ff // 2] = total[:, slot * (ff // 2) : (slot + 1) * (ff // 2)]


def collect_hidden(terms_in, ff):
    block, _, size = terms_in.shape
    return pl.pallas_call(
        functools.partial(collect_hidden_kernel, ff),
        out_shape=jax.ShapeDtypeStruct((size * 8 // ff, block // 2 * ff), exact),
        compiler_params=params(8),
        name="collect_hidden",
    )(terms_in)


def attend_kernel(hd, coef, q_ref, k_ref, v_ref, o_ref, e_ref, inverse_ref, vt_ref):
    @pl.when(pl.program_id(0) == 0)
    def _():
        vt_ref[...] = v_ref[...].T

    s = dot(k_ref[...], q_ref[...], 1, 1)
    top = jnp.max(s, axis=0, keepdims=True)
    e = jnp.exp2((s - top) * coef)
    total = jnp.sum(e, axis=0, keepdims=True)
    inverse = 1.0 / total
    e = e.astype(low)
    e_ref[0] = e
    inverse_ref[0] = inverse
    o = (dot(vt_ref[...], e, 1, 0) * inverse).astype(low)
    for piece in range(o_ref.shape[0]):
        o_ref[piece] = o[:hd, piece * lanes : (piece + 1) * lanes]


def attend(q, q_at, k, k_at, v, v_at, hd, rows):
    tokens, keys = q.shape[0], k.shape[0]
    coef = math.log2(math.e) / hd**0.5
    steps = tokens // rows
    return pl.pallas_call(
        functools.partial(attend_kernel, hd, coef),
        grid=(steps,),
        in_specs=[
            pl.BlockSpec((rows, lanes), lambda i: (i, q_at)),
            pl.BlockSpec((keys, lanes), lambda i: (0, k_at)),
            pl.BlockSpec((keys, lanes), lambda i: (0, v_at)),
        ],
        out_specs=[
            pl.BlockSpec((rows // lanes, hd, lanes), lambda i: (i, 0, 0)),
            pl.BlockSpec((1, keys, rows), lambda i: (i, 0, 0)),
            pl.BlockSpec((1, 1, rows), lambda i: (i, 0, 0)),
        ],
        out_shape=[
            jax.ShapeDtypeStruct((tokens // lanes, hd, lanes), low),
            pltpu.HBM((steps, keys, rows), low),
            jax.ShapeDtypeStruct((steps, 1, rows), exact),
        ],
        scratch_shapes=[pltpu.VMEM((lanes, keys), low)],
        compiler_params=params(10 * keys // 1024),
        cost_estimate=small_cost,
        name="attend",
    )(q, k, v)


def attend_back_kernel(hd, scale, span, q_ref, k_ref, v_ref, do_ref, e_ref, inverse_ref, out_ref, sum_ref, kt_ref, dk_sum, dv_sum):
    step = pl.program_id(0)
    rows = q_ref.shape[0]

    @pl.when(step == 0)
    def _():
        kt_ref[...] = k_ref[...].T
        dk_sum[...] = jnp.zeros_like(dk_sum)
        dv_sum[...] = jnp.zeros_like(dv_sum)
        sum_ref[...] = jnp.zeros_like(sum_ref)

    pieces = do_ref.shape[0]
    dot_t = jnp.concatenate([do_ref[piece] for piece in range(pieces)], axis=1)
    fill = jnp.zeros((lanes - hd, dot_t.shape[1]), low)
    dot_t = jnp.concatenate([dot_t, fill], axis=0)
    q = q_ref[...]
    p = e_ref[0].astype(exact) * inverse_ref[0]
    dp = dot(v_ref[...], dot_t, 1, 0)
    r = jnp.sum(p * dp, axis=0, keepdims=True)
    ds = (p * (dp - r)).astype(low)
    dv_sum[...] += dot(p.astype(low), dot_t.T, 1, 0)
    dk_sum[...] += dot(ds, q, 1, 0)
    dq = dot(kt_ref[...], ds, 1, 0) * scale
    head = lax.broadcasted_iota(jnp.int32, dq.shape, 0) < hd
    dq = jnp.where(head, dq, 0.0).T.astype(low)
    out_ref[pl.ds(pl.multiple_of(span + step * rows, rows), rows), :lanes] = dq.astype(out_ref.dtype)
    sum_ref[0:1, :lanes] += jnp.sum(dq.astype(exact), axis=0, keepdims=True)

    @pl.when(step == pl.num_programs(0) - 1)
    def _():
        head = lax.broadcasted_iota(jnp.int32, dk_sum.shape, 1) < hd
        dk = jnp.where(head, dk_sum[...] * scale, 0.0)
        dv = dv_sum[...].astype(out_ref.dtype)
        dk = dk.astype(out_ref.dtype)
        out_ref[:, lanes : 2 * lanes] = dk
        sum_ref[0:1, lanes : 2 * lanes] = jnp.sum(dk.astype(exact), axis=0, keepdims=True)
        out_ref[:, 2 * lanes :] = dv
        sum_ref[0:1, 2 * lanes :] = jnp.sum(dv.astype(exact), axis=0, keepdims=True)


def attend_back(q, q_at, k, k_at, v, v_at, do, e, inverse, hd, rows, span, kind):
    tokens, keys = q.shape[0], k.shape[0]
    scale = 1.0 / hd**0.5
    steps = tokens // rows
    return pl.pallas_call(
        functools.partial(attend_back_kernel, hd, scale, span),
        grid=(steps,),
        in_specs=[
            pl.BlockSpec((rows, lanes), lambda i: (i, q_at)),
            pl.BlockSpec((keys, lanes), lambda i: (0, k_at)),
            pl.BlockSpec((keys, lanes), lambda i: (0, v_at)),
            pl.BlockSpec((rows // lanes, hd, lanes), lambda i: (i, 0, 0)),
            pl.BlockSpec((1, keys, rows), lambda i: (i, 0, 0)),
            pl.BlockSpec((1, 1, rows), lambda i: (i, 0, 0)),
        ],
        out_specs=[pl.BlockSpec((keys, 3 * lanes), lambda i: (0, 0)), pl.BlockSpec((8, 3 * lanes), lambda i: (0, 0))],
        out_shape=[pltpu.HBM((keys, 3 * lanes), kind), jax.ShapeDtypeStruct((8, 3 * lanes), exact)],
        scratch_shapes=[
            pltpu.VMEM((lanes, keys), low),
            pltpu.VMEM((keys, lanes), exact),
            pltpu.VMEM((keys, lanes), exact),
        ],
        compiler_params=params(14 * keys // 1024),
        cost_estimate=small_cost,
        name="attend_back",
    )(q, k, v, do, far_off(e), inverse)


def body(
    hidden_in,
    clip_lengths,
    ln1_gain,
    ln1_bias,
    w_query,
    b_query,
    w_key,
    w_value,
    b_value,
    w_out,
    b_out,
    ln2_gain,
    ln2_bias,
    w_fc1,
    b_fc1,
    w_fc2,
    b_fc2,
    cotangent,
):
    micro, rows, width = hidden_in.shape
    at = Layout(micro)
    place = at.place
    hd = width // heads
    own = 2 * rows
    tokens = at.half * own
    clips = clip_lengths.shape[1]
    chunk = width // at.block
    step_rows = 256

    vectors = [at.to_block(v) for v in (ln1_gain, ln1_bias, b_query, b_value, b_out, ln2_gain, ln2_bias, b_fc2)]
    ff_bias = at.to_block(b_fc1)
    ff_rows = ff_bias.shape[0]
    first, second = pack(place, hidden_in, jnp.stack(vectors), ff_bias[None])
    blocked = [at.to_block(w) for w in (w_query, w_key, w_value, w_fc1)]
    w_in, w1 = deal(*blocked, hd, at.block)
    ff = blocked[3].shape[1] // heads
    second = at.partner(second)
    wo_shard = at.to_block(w_out)
    g_far = jnp.concatenate([lax.dynamic_index_in_dim(cotangent, 1 - at.mine, 0, False), wo_shard], axis=0)
    second, w_in, w1, g_far = together(second, w_in, w1, g_far)

    x_own, small, *parts = arrange(place, first, second, rows)
    marks = []
    small_far = at.swapped(small, 1)
    parts[2] = jnp.concatenate([parts[2], small[None], small_far[None]], axis=1)
    c1 = small.reshape(2, extra_rows, width)[:, 0, lanes : lanes + ff_rows].reshape(1, 2 * ff_rows).astype(exact)
    w2_shard = at.to_block(w_fc2)
    mine, others, (g_far, *w2_far) = at.gather_tree(parts, [g_far, w2_shard[: ff_rows // 2], w2_shard[ff_rows // 2 :]])
    w2 = jnp.concatenate(at.ordered(w2_shard, jnp.concatenate(w2_far, axis=0)), axis=0)
    g_far, wo_far = g_far[:rows], g_far[rows:]
    wo = jnp.concatenate(at.ordered(wo_shard, wo_far), axis=0)
    *mine, w_in, wo = together(*mine, w_in, wo)
    w_in = at.exchange_block(w_in)
    wo = at.gather_half(wo).reshape(heads, 2, chunk, width).transpose(1, 0, 2, 3).reshape(width, width)
    before = norm(place, False, mine, (), hd, own, chunk)
    a1, table = norm(place, True, others, before, hd, own, chunk)
    w_in, a1, table = together(w_in, a1, table)

    w1 = at.exchange_block(tie(w1, w_in))
    w_in = w_in.reshape(width, 3 * hd)
    g_own = jnp.concatenate(at.ordered(lax.dynamic_index_in_dim(cotangent, at.mine, 0, False), g_far), axis=0)
    g_all = at.gather_half(g_own)

    lengths = lax.dynamic_index_in_dim(clip_lengths, at.mine, 0, False)
    ends = jnp.cumsum(lengths)
    ends = ends - at.me // at.block * tokens

    a1 = a1.reshape(tokens, width)
    qkv, w_pad = project(place, ends, a1, w_in, table, hd, rows)
    span = 0
    qkv_at = (qkv, 0, qkv, 1, qkv, 2)
    if at.blocks > 1:
        span = tokens // 2
        ahead = [(d, d + at.block) for d in range(at.count - at.block)]
        behind = [(d + at.block, d) for d in range(at.count - at.block)]
        nothing = jnp.where(jnp.arange(2 * lanes)[None] == hd + clips, 1.0, 0.0).astype(low)
        kv = qkv[:, lanes:]
        slots = kv.reshape(heads, 2, rows, 2 * lanes)
        before = at.send(slots[:, 1].reshape(span, 2 * lanes), ahead)
        after = at.send(slots[:, 0].reshape(span, 2 * lanes), behind)
        before = jnp.where(at.me < at.block, nothing, before)
        after = jnp.where(at.me >= at.count - at.block, nothing, after)
        kv = jnp.concatenate([before, kv, after], axis=0)
        qkv_at = (qkv, 0, kv, 0, kv, 1)
    o_head, expo, inverse = attend(*qkv_at, hd, step_rows)
    o_head, w1 = together(o_head, w1)
    w1 = unfolded(w1, ff)
    o_own = at.exchange_half(o_head)

    x2, *parts = join(x_own, o_own, wo, table)
    g_split = g_all.reshape(8, 2, own, width)
    mine, others, _ = at.gather_tree(parts)

    *before, kept, sum_c = feed(place, False, mine, g_split, w1, w2, c1, (), own, low)
    hid, du, y, away, sum_c2 = feed(place, True, others, g_split, w1, w2, c1, before, own, low)
    y = lax.psum_scatter(y.reshape(tokens, width), "dev", scatter_dimension=0, tiled=True, axis_index_groups=at.halves)
    marks, made = [], []

    def second_terms(marks):
        made.append(fc2_grad(tie(hid, marks[0]), g_split))
        return made

    def first_terms(marks):
        made.append(fc1_grad(place, mine, others, tie(du, marks[1]), chunk))
        return made[1:]

    kept, got = at.reduce_half(away, kept, marks, {1: second_terms, 2: first_terms})
    back_w2 = at.exchanged(tie(made[0], marks[1]))
    d_w1 = made[1]
    *sums, d_w1 = together(*kept, *got, *back_w2, d_w1)
    kept, got, back_w2 = sums[:3], sums[3:6], sums[6:]

    dx2, ga_own, do_own, sum2 = second_back(kept, got, x2, g_own, table, wo, hd)
    do_head = at.exchange_half(do_own)
    ga = at.gather_half(ga_own).reshape(tokens, width)
    d_w1 = at.exchange_block(tie(d_w1, do_head))

    kind = low if at.blocks == 1 else exact
    dqkv, sum_in = attend_back(*qkv_at, do_head, expo, inverse, hd, step_rows, span, kind)
    if at.blocks > 1:
        dkv = dqkv[:, lanes:]
        to_before = at.send(dkv[:span].astype(low), behind).astype(exact)
        to_after = at.send(dkv[span + tokens :].astype(low), ahead).astype(exact)
        halo = jnp.stack([t.reshape(heads, rows, 2 * lanes) for t in (to_after, to_before)], axis=1)
        dkv = dkv[span : span + tokens] + halo.reshape(tokens, 2 * lanes)
        dqkv = jnp.concatenate([dqkv[span : span + tokens, :lanes], dkv], axis=1).astype(low)
        sum_in = jnp.broadcast_to(jnp.sum(dqkv.astype(exact), axis=0, keepdims=True), (8, 3 * lanes))
    dqkv, sum_in, y = together(dqkv, sum_in, y)
    split = dqkv.reshape(8, 2, own, 3 * lanes)
    away, kept = (terms(place, other, split, w_pad, 1, low) for other in (True, False))
    away, d_w1 = together(away, d_w1)
    marks, made, moved = [], [], []

    def projections(marks):
        made.append(head_grad(place, a1, tie(dqkv, marks[0]), w_in, table, sum2, sum_in, sum_c, sum_c2, hd, chunk, at.block))
        return made

    def output_weight(marks):
        out = (x2 + (tie(y, marks[0]).astype(exact) + table[7])).astype(low)
        moved.extend(at.exchanged(out.reshape(2, rows, width)))
        late, o_late = together(ga, o_head, marks[1])[:2]
        made.append(output_grad(o_late, late.reshape(at.half, own, width)))
        return made[1:] + moved

    kept, got = at.reduce_half(away, kept, marks, {1: projections, 2: output_weight})
    d_in = at.exchange_block(tie(made[0], marks[1]))
    kept_first, d_in = together(kept[0], d_in)
    kept = (kept_first, *kept[1:])

    dx = first_back(kept, got, x_own, dx2, table)
    d_w1, *back_w2 = together(d_w1, *back_w2, dx)[:3]

    input_grad = at.exchanged(dx.reshape(2, rows, width))
    layer_out = moved
    layer_out, input_grad = (jnp.stack(at.ordered(*v)).astype(exact) for v in (layer_out, input_grad))
    back_wo = at.send_rows_back(made[1])
    grad_w2 = at.from_block(back_w2[0].astype(exact) + back_w2[1].astype(exact))
    grad_w1 = at.from_block(collect_hidden(d_w1, ff))
    grad_wo = at.from_block(back_wo[0].astype(exact) + back_wo[1].astype(exact))
    *grads, vec = collect(d_in, hd)
    grad_wq, grad_wk, grad_wv = (at.from_block(v) for v in grads)
    pieces = [at.from_block(vec[i]) for i in range(8)]
    grad_g2, grad_b2, grad_bo, grad_bf2, grad_bq, grad_bv, grad_g1, grad_b1 = pieces
    grad_c1 = at.from_block(vec[8 : 8 + ff_rows // chunk].reshape(ff_rows))
    return (
        layer_out,
        input_grad,
        grad_g1,
        grad_b1,
        grad_wq,
        grad_bq,
        grad_wk,
        grad_wv,
        grad_bv,
        grad_wo,
        grad_bo,
        grad_g2,
        grad_b2,
        grad_w1,
        grad_c1,
        grad_w2,
        grad_bf2,
    )


def solution(mesh):
    tokens, vector, matrix = P(None, "dev", None), P("dev"), P("dev", None)
    grads = (vector, vector, matrix, vector, matrix, matrix, vector, matrix, vector, vector, vector, matrix, vector, matrix, vector)
    return jax.shard_map(
        body,
        mesh=mesh,
        in_specs=(tokens, P()) + grads + (tokens,),
        out_specs=(tokens, tokens) + grads,
        check_vma=False,
    )
```

```python
import functools
import math

import jax
import jax.numpy as jnp
from jax import lax
from jax.experimental import pallas as pl
from jax.experimental.pallas import tpu as pltpu
from jax.sharding import PartitionSpec as P

eps = 1e-05
heads = 16
low = jnp.bfloat16
exact = jnp.float32
far = -1e30
lanes = 128
extra_rows = 8


def dot(a, b, ca, cb):
    return lax.dot_general(a, b, (((ca,), (cb,)), ((), ())), preferred_element_type=exact)


def normalized(v):
    mean = jnp.mean(v, axis=-1, keepdims=True)
    cent = v - mean
    inverse = lax.rsqrt(jnp.mean(cent * cent, axis=-1, keepdims=True) + eps)
    return cent * inverse, inverse


def norm_back(unit, inverse, gain, grad):
    scaled = grad * gain
    along = jnp.mean(scaled * unit, axis=-1, keepdims=True)
    return inverse * (scaled - jnp.mean(scaled, axis=-1, keepdims=True) - unit * along)


def tie(value, *others):
    return lax.optimization_barrier((value,) + others)[0]


def together(*values):
    return lax.optimization_barrier(values)


class Layout:
    def __init__(self, micro):
        self.count = lax.axis_size("dev")
        self.half = heads
        self.block = micro * heads
        self.blocks = self.count // self.block
        self.me = lax.axis_index("dev")
        self.rank = self.me % self.block
        self.mine = self.rank // self.half
        self.head = self.rank % self.half
        self.odd = self.rank % 2
        bits = [(self.me // bit) % 2 for bit in (1, 2, 4, 8)]
        self.place = jnp.stack(bits + [self.mine, self.head, self.odd]).astype(jnp.int32)
        self.halves = [list(range(s, s + self.half)) for s in range(0, self.count, self.half)]
        self.whole = [list(range(s, s + self.block)) for s in range(0, self.count, self.block)]
        self.rows = [list(range(s, s + self.blocks)) for s in range(0, self.count, self.blocks)]
        first = [d // self.half % 2 for d in range(self.count)]
        base = [d // self.block * self.block + 2 * (d % self.half) for d in range(self.count)]
        self.even_first = [(d, base[d] + first[d]) for d in range(self.count)]
        self.odd_first = [(d, base[d] + 1 - first[d]) for d in range(self.count)]

    def send(self, value, pairs):
        return lax.ppermute(value, "dev", pairs)

    def swapped(self, value, bit):
        return self.send(value, [(d, d ^ bit) for d in range(self.count)])

    def to_block(self, value):
        if self.blocks == 1:
            return value
        value = lax.all_gather(value, "dev", axis=0, tiled=True, axis_index_groups=self.rows)
        return self.send(value, [(d, d % self.blocks * self.block + d // self.blocks) for d in range(self.count)])

    def from_block(self, value):
        if self.blocks == 1:
            return value
        value = self.send(value, [(d % self.blocks * self.block + d // self.blocks, d) for d in range(self.count)])
        return lax.psum_scatter(value, "dev", scatter_dimension=0, tiled=True, axis_index_groups=self.rows)

    def partner(self, value):
        return self.swapped(value, self.half)

    def ordered(self, kept, got):
        return jnp.where(self.mine == 0, kept, got), jnp.where(self.mine == 0, got, kept)

    def exchanged(self, value):
        kept = lax.dynamic_index_in_dim(value, self.mine, 0, False)
        return kept, self.partner(lax.dynamic_index_in_dim(value, 1 - self.mine, 0, False))

    def send_rows_back(self, value):
        first = lax.dynamic_index_in_dim(value, self.mine, 0, False)
        second = lax.dynamic_index_in_dim(value, 1 - self.mine, 0, False)
        return self.send(first, self.even_first), self.send(second, self.odd_first)

    def gather_half(self, value):
        return lax.all_gather(value, "dev", axis=0, axis_index_groups=self.halves)

    def exchange_half(self, value):
        return lax.all_to_all(value, "dev", 0, 0, tiled=True, axis_index_groups=self.halves)

    def exchange_block(self, value):
        return lax.all_to_all(value, "dev", 0, 0, tiled=True, axis_index_groups=self.whole)

    def gather_tree(self, parts, beside=()):
        brought = []
        for stage in range(3):
            got = [self.swapped(piece, order[stage]) for piece, order in zip(parts, part_orders)]
            if beside:
                far = self.partner(tie(beside[stage], parts[0]))
                first, far = together(got[0], far)
                got = [first, *got[1:]]
                brought.append(far)
            if stage < 2:
                parts = merge(parts, got)
        other = [self.swapped(piece, 1) for piece in (*parts, *got)]
        return (*parts, *got), other, brought

    def reduce_half(self, away, kept, marks=None, before=None, arrived=None):
        got = [self.swapped(away, 1)]
        kept = [kept]
        for stage in range(3):
            if before and stage in before:
                got = [tie(got[0], *before[stage](marks)), *got[1:]]
            away, kept = split_terms(self.place, stage, kept, got)
            if marks is not None:
                marks.append(away[0])
            got = [self.swapped(piece, order[stage]) for piece, order in zip(away, part_orders)]
            if arrived is not None:
                arrived.append(got[2])
        return kept, got


small_cost = pl.CostEstimate(flops=1 << 10, bytes_accessed=1 << 10, transcendentals=0)


def far_off(v):
    return pltpu.with_memory_space_constraint(v, pltpu.HBM)


def params(megabytes):
    return pltpu.CompilerParams(vmem_limit_bytes=megabytes << 20)


part_orders = ((8, 4, 2), (4, 2, 8), (2, 8, 4))


def part_bounds(tokens):
    cut = tokens * 3 // 8 // 16 * 16
    return ((0, cut), (cut, 2 * cut), (2 * cut, tokens))


def split_kernel(stage, place_ref, *refs):
    place = {bit: place_ref[i] for i, bit in enumerate((1, 2, 4, 8))}
    if stage == 0:
        kept_ref, got_ref = refs[:2]
        outs = refs[2:]
        bounds = part_bounds(kept_ref.shape[1])
    else:
        outs = refs[6:]
    for part, order in enumerate(part_orders):
        left = [bit for bit in (8, 4, 2) if bit not in order[:stage]]
        at = left.index(order[stage])
        below = 1 << (len(left) - 1 - at)
        for half, side in ((0, 1 - place[order[stage]]), (1, place[order[stage]])):
            out_ref = outs[part + 3 * half]
            for j in range(out_ref.shape[0]):
                index = (j // below * 2 + side) * below + j % below
                if stage == 0:
                    start, end = bounds[part]
                    term = kept_ref[index, start:end].astype(exact) + got_ref[index, start:end].astype(exact)
                else:
                    term = refs[part][index].astype(exact) + refs[3 + part][index].astype(exact)
                out_ref[j] = term.astype(out_ref.dtype)


def split_terms(place, stage, kept, got):
    width = kept[0].shape[-1]
    bounds = part_bounds(kept[0].shape[1]) if stage == 0 else [(0, k.shape[1]) for k in kept]
    count = kept[0].shape[0] // 2
    cols = (256, 640, width)[stage]
    spec = lambda n, t: pl.BlockSpec((n, t, cols), lambda i, p: (0, 0, i))
    outs = [(count, end - start) for start, end in bounds]
    res = pl.pallas_call(
        functools.partial(split_kernel, stage),
        grid_spec=pltpu.PrefetchScalarGridSpec(
            num_scalar_prefetch=1,
            grid=(width // cols,),
            in_specs=[spec(*v.shape[:2]) for v in (*kept, *got)],
            out_specs=[spec(*o) for o in outs] * 2,
        ),
        out_shape=[jax.ShapeDtypeStruct(o + (width,), low) for o in outs]
        + [(pltpu.HBM if stage == 2 else jax.ShapeDtypeStruct)(o + (width,), exact) for o in outs],
        compiler_params=params(10),
        cost_estimate=small_cost,
        name="split_terms",
    )(place, *kept, *got)
    return res[:3], res[3:]


def last_sum(refs):
    return jnp.concatenate([refs[i][0].astype(exact) + refs[3 + i][0].astype(exact) for i in range(3)], axis=0)


def pack_kernel(place_ref, x_ref, v_ref, c_ref, first_ref, second_ref):
    rows, width = x_ref.shape[1:]
    mine = place_ref[4]
    fill = jnp.zeros((v_ref.shape[0], width - v_ref.shape[1]), exact)
    small = jnp.concatenate([v_ref[...].astype(exact), fill], axis=1)
    c = jnp.concatenate([c_ref[...].astype(exact), jnp.zeros((1, width - lanes - c_ref.shape[1]), exact)], axis=1)
    c = jnp.concatenate([jnp.zeros((1, lanes), exact), c], axis=1)
    row = lax.broadcasted_iota(jnp.int32, small.shape, 0)
    small = small + jnp.where(row == 0, c, 0.0)
    tail = small.astype(low)
    for out_ref, index in ((first_ref, mine), (second_ref, 1 - mine)):
        out_ref[:rows] = x_ref[index]
        out_ref[rows:] = tail


def pack(place, x, vectors, c):
    rows, width = x.shape[1:]
    out = jax.ShapeDtypeStruct((rows + extra_rows, width), low)
    return pl.pallas_call(
        pack_kernel,
        grid_spec=pltpu.PrefetchScalarGridSpec(
            num_scalar_prefetch=1,
            grid=(1,),
            in_specs=[whole_spec(v) for v in (x, vectors, c)],
            out_specs=[out_spec(out)] * 2,
        ),
        out_shape=[out, out],
        compiler_params=params(6),
        name="pack",
    )(place, far_off(x), vectors, c)


def arrange_kernel(rows, place_ref, first_ref, second_ref, x_ref, small_ref, *part_refs):
    mine = place_ref[4]
    for side, refs in enumerate(((first_ref, second_ref), (second_ref, first_ref))):

        @pl.when(mine == side)
        def _():
            x = jnp.concatenate([ref[:rows] for ref in refs], axis=0)
            x_ref[...] = x
            tail = [ref[rows:].astype(exact) for ref in refs]
            small_ref[...] = jnp.concatenate(tail, axis=0).astype(low)
            for part_ref, (start, end) in zip(part_refs, part_bounds(2 * rows)):
                part_ref[0] = x[start:end]


def arrange(place, first, second, rows):
    width = first.shape[1]
    shapes = [(2 * rows, width), (2 * extra_rows, width)]
    shapes += [(1, end - start, width) for start, end in part_bounds(2 * rows)]
    outs = [jax.ShapeDtypeStruct(shape, low) for shape in shapes]
    return pl.pallas_call(
        functools.partial(arrange_kernel, rows),
        grid_spec=pltpu.PrefetchScalarGridSpec(
            num_scalar_prefetch=1,
            grid=(1,),
            in_specs=[whole_spec(first), whole_spec(second)],
            out_specs=[out_spec(out) for out in outs],
        ),
        out_shape=outs,
        compiler_params=params(6),
        name="arrange",
    )(place, first, second)


def up_to_lanes(size):
    return -(-size // lanes) * lanes


def fold(v):
    return jnp.concatenate([v[i : i + 8] for i in range(0, v.shape[0], 8)], axis=1)


def unfold(v, size):
    return jnp.concatenate([v[:, i : i + size] for i in range(0, v.shape[1], size)], axis=0)


def unfold_kernel(in_ref, out_ref):
    size = out_ref.shape[1]
    chunk = in_ref.shape[2] // size * 8
    for device in range(0, in_ref.shape[0], 2):
        rows = [unfold(in_ref[device + i].astype(exact), size) for i in range(2)]
        out_ref[device * chunk : (device + 2) * chunk] = jnp.concatenate(rows, axis=0).astype(low)


def unfolded(v, size):
    return pl.pallas_call(
        unfold_kernel,
        out_shape=jax.ShapeDtypeStruct((v.size // size, size), low),
        compiler_params=params(8),
        cost_estimate=small_cost,
        name="unfolded",
    )(v)


def deal_kernel(hd, q_ref, k_ref, v_ref, w_ref, in_ref, hidden_ref):
    ff = w_ref.shape[1] // heads
    side_by_side = lambda pieces: jnp.concatenate([piece.astype(exact) for piece in pieces], axis=1).astype(low)
    for head in range(heads):
        at = [(slot * heads + head) * (ff // 2) for slot in range(2)]
        hidden = jnp.concatenate([w_ref[:, a : a + ff // 2].astype(exact) for a in at], axis=1)
        hidden = fold(hidden).astype(low)
        columns = side_by_side([ref[:, head * hd : (head + 1) * hd] for ref in (q_ref, k_ref, v_ref)])
        for device in range(head, in_ref.shape[0], heads):
            in_ref[device] = columns
            hidden_ref[device] = hidden


def deal(q, k, v, w, hd, block):
    chunk, ff = q.shape[0], w.shape[1] // heads
    return pl.pallas_call(
        functools.partial(deal_kernel, hd),
        out_shape=[jax.ShapeDtypeStruct(shape, low) for shape in ((block, chunk, 3 * hd), (block, 8, chunk * ff // 8))],
        compiler_params=params(8),
        name="deal",
    )(*map(far_off, (q, k, v, w)))


def merge_kernel(*refs):
    for i in range(3):
        count = refs[i].shape[0]
        refs[6 + i][:count] = refs[i][...]
        refs[6 + i][count:] = refs[3 + i][...]


def merge(parts, got):
    width = parts[0].shape[2]
    cols = 640
    spec = lambda shape: pl.BlockSpec(shape[:2] + (cols,), lambda i: (0, 0, i))
    outs = [(2 * p.shape[0],) + p.shape[1:] for p in parts]
    return pl.pallas_call(
        merge_kernel,
        grid=(width // cols,),
        in_specs=[spec(v.shape) for v in (*parts, *got)],
        out_specs=[spec(o) for o in outs],
        out_shape=[jax.ShapeDtypeStruct(o, low) for o in outs],
        compiler_params=params(8),
        name="merge",
    )(*parts, *got)


def out_spec(v):
    return pl.BlockSpec(v.shape, lambda *_: (0,) * len(v.shape))


def tree_rows(place_ref, chip, refs, fill):
    mine = place_ref[1] + 2 * place_ref[2] + 4 * place_ref[3]
    apart = chip ^ mine
    step = {8: apart // 4, 4: apart // 2 % 2, 2: apart % 2}
    for part, order in enumerate(part_orders):
        index = 2 * step[order[1]] + step[order[0]]
        for late in range(2):

            @pl.when(step[order[2]] == late)
            def _():
                fill(part, refs[part + 3 * late], index)


def fill_rows(place_ref, chip, refs, out_ref, base, own):
    bounds = part_bounds(own)

    def fill(part, ref, index):
        start, end = bounds[part]
        out_ref[pl.ds(base + start, end - start)] = ref[index, : end - start]

    tree_rows(place_ref, chip, refs, fill)


def whole_spec(v):
    return pl.BlockSpec(v.shape, lambda *_: (0,) * len(v.shape), pipeline_mode=pl.Buffered(1))


def norm_kernel(hd, chunk, first, place_ref, *refs):
    pieces = refs[:6]
    a_ref, table_ref, x_scr = refs[-3:]
    step, _, own, width = a_ref.shape

    @pl.when(pl.program_id(0) == 0)
    def _():
        if first:
            tail = part_bounds(own)[2]

            def fill(chip, part, ref, index):
                if part != 2:
                    return
                small = ref[index, tail[1] - tail[0] :].astype(exact)
                for far_core in range(2):
                    for slot in range(2):
                        line = (2 * far_core + slot) * extra_rows
                        piece = small[line : line + extra_rows, :chunk]
                        for core in range(2):

                            @pl.when(place_ref[0] == core)
                            def _():
                                at = (heads * slot + 2 * chip + (core ^ far_core)) * chunk
                                table_ref[:, at : at + chunk] = piece

            for chip in range(8):
                tree_rows(place_ref, chip, pieces, functools.partial(fill, chip))
        else:
            table_ref[...] = refs[6][...]

    for j in range(step):
        fill_rows(place_ref, pl.program_id(0) * step + j, pieces, x_scr, j * own, own)
    unit, _ = normalized(x_scr[...].astype(exact))
    a_ref[...] = (unit * table_ref[0:1] + table_ref[1:2]).astype(low).reshape(a_ref.shape)


def norm(place, other, pieces, before, hd, own, chunk):
    width = pieces[0].shape[2]
    step = 4
    side = (lambda p: 1 - p[0]) if other else (lambda p: p[0])
    table = jax.ShapeDtypeStruct((extra_rows, width), exact)
    return pl.pallas_call(
        functools.partial(norm_kernel, hd, chunk, not before),
        grid_spec=pltpu.PrefetchScalarGridSpec(
            num_scalar_prefetch=1,
            grid=(8 // step,),
            in_specs=[whole_spec(v) for v in pieces] + ([whole_spec(table), pl.BlockSpec(memory_space=pl.ANY)] if before else []),
            out_specs=[pl.BlockSpec((step, 1, own, width), lambda i, p: (i, side(p), 0, 0)), out_spec(table)],
            scratch_shapes=[pltpu.VMEM((step * own, width), low)],
        ),
        out_shape=[pltpu.HBM((8, 2, own, width), low), table],
        input_output_aliases={8: 0} if before else {},
        compiler_params=params(30),
        cost_estimate=small_cost,
        name="norm",
    )(place, *pieces, *before[::-1])


def project_kernel(hd, clips, own_rows, place_ref, ends_ref, a_ref, w_ref, table_ref, qkv_ref, pad_ref, bias_ref):
    rows, width = a_ref.shape

    @pl.when(pl.program_id(0) == 0)
    def _():
        w = w_ref[...].astype(exact)
        fill = jnp.zeros((width, lanes - hd), exact)
        w = [v for i in range(3) for v in (w[:, i * hd : (i + 1) * hd], fill)]
        pad_ref[...] = jnp.concatenate(w, axis=1).astype(low)
        bias_ref[...] = jnp.zeros_like(bias_ref)
        for h in range(heads):

            @pl.when(place_ref[5] == h)
            def _():
                for line, at in ((2, 0), (3, 2 * lanes)):
                    bias_ref[0:1, at : at + hd] = table_ref[line : line + 1, h * hd : (h + 1) * hd]

    qkv = dot(a_ref[...], pad_ref[...], 1, 0) + bias_ref[0:1]
    column = lax.broadcasted_iota(jnp.int32, (rows, lanes), 1) - hd
    row = lax.broadcasted_iota(jnp.int32, (rows, lanes), 0) + pl.program_id(0) * rows
    shift = own_rows.bit_length() - 1
    token = (lax.shift_right_logical(row, shift) & 1) * (heads * own_rows)
    token += lax.shift_right_logical(row, shift + 1) * own_rows + (row & (own_rows - 1))
    clip = jnp.zeros_like(token)
    for i in range(clips):
        clip += (ends_ref[i] <= token).astype(jnp.int32)
    match = clip == column
    marked = (column >= 0) & (column <= clips)
    qkv_ref[:, :lanes] = (qkv[:, :lanes] + jnp.where(marked & ~match, far, 0.0)).astype(low)
    qkv_ref[:, lanes : 2 * lanes] = (qkv[:, lanes : 2 * lanes] + jnp.where(marked & match, 1.0, 0.0)).astype(low)
    qkv_ref[:, 2 * lanes :] = qkv[:, 2 * lanes :].astype(low)


def project(place, ends, a, w, table, hd, own_rows):
    tokens, width = a.shape
    rows = 512
    clips = ends.shape[0]
    assert own_rows & (own_rows - 1) == 0
    wide = jax.ShapeDtypeStruct((width, 3 * lanes), low)
    return pl.pallas_call(
        functools.partial(project_kernel, hd, clips, own_rows),
        grid_spec=pltpu.PrefetchScalarGridSpec(
            num_scalar_prefetch=2,
            grid=(tokens // rows,),
            in_specs=[
                pl.BlockSpec((rows, width), lambda i, p, e: (i, 0)),
                whole_spec(w),
                whole_spec(table),
            ],
            out_specs=[pl.BlockSpec((rows, 3 * lanes), lambda i, p, e: (i, 0)), out_spec(wide)],
            scratch_shapes=[pltpu.VMEM((8, 3 * lanes), exact)],
        ),
        out_shape=[jax.ShapeDtypeStruct((tokens, 3 * lanes), low), pltpu.HBM(wide.shape, low)],
        compiler_params=params(20),
        cost_estimate=small_cost,
        name="project",
    )(place, ends, far_off(a), w, table)


def join_kernel(x_ref, o_ref, w_ref, table_ref, x2_ref, *part_refs):
    o = o_ref[...].reshape(w_ref.shape[0], o_ref.shape[2])
    x2 = x_ref[...].astype(exact) + (dot(o, w_ref[...], 0, 0) + table_ref[4:5])
    x2_ref[...] = x2
    unit, _ = normalized(x2)
    a2 = (unit * table_ref[5:6] + table_ref[6:7]).astype(low)
    for part_ref, (start, end) in zip(part_refs, part_bounds(x2.shape[0])):
        part_ref[0] = a2[start:end]


def join(x, o, w, table):
    own, width = x.shape
    parts = [jax.ShapeDtypeStruct((1, end - start, width), low) for start, end in part_bounds(own)]
    return pl.pallas_call(
        join_kernel,
        out_shape=[jax.ShapeDtypeStruct(x.shape, exact)] + parts,
        compiler_params=params(10),
        cost_estimate=small_cost,
        name="join",
    )(x, o, far_off(w), table)


def accumulate(total_ref, term):
    @pl.when(pl.program_id(0) == 0)
    def _():
        total_ref[...] = term

    @pl.when(pl.program_id(0) > 0)
    def _():
        total_ref[...] += term


def at_end(write):
    pl.when(pl.program_id(0) == pl.num_programs(0) - 1)(write)


def fc2_grad_kernel(hid_ref, g_ref, out_ref, total_ref):
    rows = math.prod(g_ref.shape[:3])
    accumulate(total_ref, dot(hid_ref[...].reshape(rows, hid_ref.shape[3]), g_ref[...].reshape(rows, g_ref.shape[3]), 0, 0))

    @at_end
    def _():
        out_ref[...] = total_ref[...].astype(low).reshape(out_ref.shape)


def fc2_grad(hid, g):
    eight, two, own, width = g.shape
    ff = hid.shape[3]
    step = 2
    out = jax.ShapeDtypeStruct((2, ff // 2, width), low)
    return pl.pallas_call(
        fc2_grad_kernel,
        grid=(eight // step,),
        in_specs=[pl.BlockSpec((step, two, own, size), lambda i: (i, 0, 0, 0)) for size in (ff, width)],
        out_specs=out_spec(out),
        out_shape=out,
        scratch_shapes=[pltpu.VMEM((ff, width), exact)],
        compiler_params=params(12),
        cost_estimate=small_cost,
        name="fc2_grad",
    )(far_off(hid), far_off(g))


def fc1_grad_kernel(place_ref, *refs):
    mine, others, (du_ref, out_ref, a_scr, total_ref) = refs[:6], refs[6:12], refs[12:]
    chips, two, own, ff = du_ref.shape
    width = a_scr.shape[3]
    bounds = part_bounds(own)
    for j in range(chips):
        chip = pl.program_id(0) * chips + j
        for core, pieces in ((place_ref[0], mine), (1 - place_ref[0], others)):

            def fill(part, ref, index):
                start, end = bounds[part]
                a_scr[j, core, start:end] = ref[index]

            tree_rows(place_ref, chip, pieces, fill)
    rows = chips * two * own
    accumulate(total_ref, dot(du_ref[...].reshape(rows, ff), a_scr[...].reshape(rows, width), 0, 0))

    @at_end
    def _():
        total = total_ref[...].T
        chunk = width // out_ref.shape[0]
        for device in range(out_ref.shape[0]):
            out_ref[device] = fold(total[device * chunk : (device + 1) * chunk]).astype(low)


def fc1_grad(place, mine, others, du, chunk):
    eight, two, own, ff = du.shape
    width = mine[0].shape[2]
    step = 2
    out = jax.ShapeDtypeStruct((width // chunk, 8, chunk * ff // 8), low)
    return pl.pallas_call(
        fc1_grad_kernel,
        grid_spec=pltpu.PrefetchScalarGridSpec(
            num_scalar_prefetch=1,
            grid=(eight // step,),
            in_specs=[whole_spec(v) for v in (*mine, *others)] + [pl.BlockSpec((step, two, own, ff), lambda i, p: (i, 0, 0, 0))],
            out_specs=out_spec(out),
            scratch_shapes=[pltpu.VMEM((step, two, own, width), low), pltpu.VMEM((ff, width), exact)],
        ),
        out_shape=out,
        compiler_params=params(20),
        cost_estimate=small_cost,
        name="fc1_grad",
    )(place, *mine, *others, far_off(du))


def output_grad_kernel(o_ref, ga_ref, out_ref, total_ref):
    term = dot(o_ref[0], ga_ref[0], 1, 0)
    for piece in range(1, o_ref.shape[0]):
        term += dot(o_ref[piece], ga_ref[piece], 1, 0)
    accumulate(total_ref, term)

    @at_end
    def _():
        rows = out_ref.shape[1]
        for side in range(2):
            out_ref[side] = total_ref[side * rows : (side + 1) * rows].astype(low)


def output_grad(o, ga):
    count, hd, own = o.shape
    width = ga.shape[2]
    step = 4
    out = jax.ShapeDtypeStruct((2, hd // 2, width), low)
    return pl.pallas_call(
        output_grad_kernel,
        grid=(count // step,),
        in_specs=[pl.BlockSpec((step, hd, own), lambda i: (i, 0, 0)), pl.BlockSpec((step, own, width), lambda i: (i, 0, 0))],
        out_specs=out_spec(out),
        out_shape=out,
        scratch_shapes=[pltpu.VMEM((hd, width), exact)],
        compiler_params=params(8),
        cost_estimate=small_cost,
        name="output_grad",
    )(o, far_off(ga))


def feed_kernel(place_ref, *refs):
    pieces, (g_ref, w1_ref, w2_ref, c_ref) = refs[:6], refs[6:10]
    hid_ref, du_ref, y_ref, da_ref, sum_ref, a_scr = refs[-6:]
    step, own, width = da_ref.shape
    rows = step * own
    for j in range(step):
        fill_rows(place_ref, pl.program_id(0) * step + j, pieces, a_scr, j * own, own)
    w1, w2 = w1_ref[...], w2_ref[...]
    u = dot(a_scr[...], w1, 1, 0) + c_ref[...]
    d_hid = dot(g_ref[...].reshape(rows, width), w2, 1, 1)
    below = 0.5 * (1.0 + lax.erf(u * math.sqrt(0.5)))
    hid = (u * below).astype(low)
    hid_ref[...] = hid.reshape(hid_ref.shape)
    y_ref[...] = dot(hid, w2, 1, 0).reshape(y_ref.shape).astype(low)
    slope = below + u * (jnp.exp(-0.5 * u * u) * (1.0 / math.sqrt(2.0 * math.pi)))
    du = (d_hid * slope).astype(low)
    du_ref[...] = du.reshape(du_ref.shape)
    da_ref[...] = dot(du, w1, 1, 1).reshape(da_ref.shape).astype(da_ref.dtype)

    @pl.when(pl.program_id(0) == 0)
    def _():
        sum_ref[...] = jnp.zeros_like(sum_ref)

    sum_ref[...] += jnp.sum(du.astype(exact), axis=0, keepdims=True)


def feed(place, other, pieces, g, w1, w2, c1, before, own, kind):
    ff, width = w2.shape
    step = 4
    tokens = 8 * own
    side = (lambda p: 1 - p[0]) if other else (lambda p: p[0])
    pick = lambda size: pl.BlockSpec((step, 1, own, size), lambda i, p: (i, side(p), 0, 0))
    shape = lambda size: pltpu.HBM((8, 2, own, size), low)
    row = pl.BlockSpec((1, ff), lambda i, p: (0, 0))
    return pl.pallas_call(
        feed_kernel,
        grid_spec=pltpu.PrefetchScalarGridSpec(
            num_scalar_prefetch=1,
            grid=(8 // step,),
            in_specs=[whole_spec(v) for v in pieces]
            + [pick(width), whole_spec(w1), whole_spec(w2), row]
            + [pl.BlockSpec(memory_space=pl.ANY)] * len(before),
            out_specs=[pick(ff), pick(ff), pick(width), pl.BlockSpec((step, own, width), lambda i, p: (i, 0, 0)), row],
            scratch_shapes=[pltpu.VMEM((step * own, width), low)],
        ),
        out_shape=[
            shape(ff),
            shape(ff),
            shape(width),
            pltpu.HBM((8, own, width), kind),
            jax.ShapeDtypeStruct((1, ff), exact),
        ],
        input_output_aliases={11: 0, 12: 1, 13: 2} if before else {},
        compiler_params=params(34),
        cost_estimate=small_cost,
        name="feed",
    )(place, *pieces, far_off(g), w1, w2, c1, *before)


def terms_kernel(contract, place_ref, left_ref, right_ref, out_ref):
    rows = out_ref.shape[0] * out_ref.shape[1]
    left = left_ref[...].reshape(rows, left_ref.shape[-1])
    out_ref[...] = dot(left, right_ref[...], 1, contract).reshape(out_ref.shape).astype(out_ref.dtype)


def terms(place, other, left, right, contract, kind):
    eight, two, own, depth = left.shape
    width = right.shape[1 - contract]
    step = 4
    side = (lambda p: 1 - p[0]) if other else (lambda p: p[0])
    return pl.pallas_call(
        functools.partial(terms_kernel, contract),
        grid_spec=pltpu.PrefetchScalarGridSpec(
            num_scalar_prefetch=1,
            grid=(eight // step,),
            in_specs=[
                pl.BlockSpec((step, 1, own, depth), lambda i, p: (i, side(p), 0, 0)),
                pl.BlockSpec(right.shape, lambda i, p: (0, 0)),
            ],
            out_specs=pl.BlockSpec((step, own, width), lambda i, p: (i, 0, 0)),
        ),
        out_shape=jax.ShapeDtypeStruct((eight, own, width), kind),
        compiler_params=params(16),
        cost_estimate=small_cost,
        name="terms",
    )(place, left, right)


def rows_of(values, width):
    fill = jnp.zeros((8 - len(values), width), exact)
    return jnp.concatenate(values + [fill], axis=0)


def second_back_kernel(*refs):
    da2 = last_sum(refs[:6])
    x2_ref, g_ref, table_ref, w_ref, dx2_ref, ga_ref, do_ref, sum_ref = refs[6:]
    unit, inverse = normalized(x2_ref[...])
    g = g_ref[...].astype(exact)
    dx2 = g + norm_back(unit, inverse, table_ref[5:6], da2)
    dx2_ref[...] = dx2
    ga = dx2.astype(low)
    ga_ref[...] = ga
    do_ref[...] = dot(w_ref[...], ga, 1, 1).astype(low).reshape(do_ref.shape)
    total = lambda v: jnp.sum(v, axis=0, keepdims=True)
    sum_ref[...] = rows_of([total(da2 * unit), total(da2), total(ga.astype(exact)), total(g)], ga.shape[1])


def second_back(kept, got, x2, g, table, w, hd):
    own, width = x2.shape
    return pl.pallas_call(
        second_back_kernel,
        out_shape=[
            jax.ShapeDtypeStruct((own, width), exact),
            jax.ShapeDtypeStruct((own, width), low),
            jax.ShapeDtypeStruct((heads, hd, own), low),
            jax.ShapeDtypeStruct((8, width), exact),
        ],
        compiler_params=params(12),
        cost_estimate=small_cost,
        name="second_back",
    )(*map(far_off, (*kept, *got)), x2, g, table, far_off(w))


def first_back_kernel(*refs):
    da1 = last_sum(refs[:6])
    x_ref, dx2_ref, table_ref, dx_ref = refs[6:]
    unit, inverse = normalized(x_ref[...].astype(exact))
    dx_ref[...] = (dx2_ref[...] + norm_back(unit, inverse, table_ref[0:1], da1)).astype(low)


def first_back(kept, got, x, dx2, table):
    return pl.pallas_call(
        first_back_kernel,
        out_shape=jax.ShapeDtypeStruct(x.shape, low),
        compiler_params=params(8),
        name="first_back",
    )(*map(far_off, (*kept, *got)), x, dx2, table)


def head_grad_kernel(hd, chunk, place_ref, a_ref, d_ref, w_ref, table_ref, sum2_ref, sum_in_ref, sum_c_ref, sum_c2_ref, out_ref, total_ref, line_ref):
    accumulate(total_ref, dot(d_ref[...], a_ref[...], 0, 0))

    @at_end
    def _():
        block = out_ref.shape[0]
        head = place_ref[5]
        c = sum_c_ref[...] + sum_c2_ref[...]
        ff_rows = c.shape[1] // 2
        total = jnp.concatenate([total_ref[i * lanes : i * lanes + hd] for i in range(3)], axis=0).T
        line_ref[...] = jnp.zeros_like(line_ref)
        line_ref[0:4] = sum2_ref[0:4]
        for h in range(heads):

            @pl.when(head == h)
            def _():
                for line, at in ((4, 0), (5, 2 * lanes)):
                    line_ref[line : line + 1, h * hd : (h + 1) * hd] = sum_in_ref[0:1, at : at + hd]
                for slot in range(block // heads):
                    for line in range(ff_rows // chunk):
                        at, start = (slot * heads + h) * chunk, slot * ff_rows + line * chunk
                        line_ref[8 + line : 9 + line, at : at + chunk] = c[:, start : start + chunk]

        line_ref[12:14] = table_ref[0:2]
        small = line_ref[...].T
        gain, shift = small[:, 12:13], small[:, 13:14]
        sums = jnp.concatenate([sum_in_ref[0:1, i * lanes : i * lanes + hd] for i in range(3)], axis=1)
        w = w_ref[...].astype(exact)
        d_shift = jnp.sum(w * sums, axis=1, keepdims=True)
        d_gain = (jnp.sum(w * total, axis=1, keepdims=True) - shift * d_shift) / gain
        small = jnp.concatenate([small[:, :6], d_gain, d_shift, small[:, 8:12], jnp.zeros_like(small[:, 12:])], axis=1)
        for device in range(block):
            part = slice(device * chunk, (device + 1) * chunk)
            out_ref[device] = jnp.concatenate([total[part], small[part]], axis=1).astype(low)


def head_grad(place, a, d, w, table, sum2, sum_in, sum_c, sum_c2, hd, chunk, block):
    tokens, width = a.shape
    rows = 512
    out = jax.ShapeDtypeStruct((block, chunk, up_to_lanes(3 * hd)), low)
    small = (w, table, sum2, sum_in, sum_c, sum_c2)
    return pl.pallas_call(
        functools.partial(head_grad_kernel, hd, chunk),
        grid_spec=pltpu.PrefetchScalarGridSpec(
            num_scalar_prefetch=1,
            grid=(tokens // rows,),
            in_specs=[pl.BlockSpec((rows, size), lambda i, p: (i, 0)) for size in (width, 3 * lanes)] + [whole_spec(v) for v in small],
            out_specs=out_spec(out),
            scratch_shapes=[pltpu.VMEM((3 * lanes, width), exact), pltpu.VMEM((out.shape[2] - 3 * hd, width), exact)],
        ),
        out_shape=out,
        compiler_params=params(20),
        cost_estimate=small_cost,
        name="head_grad",
    )(place, far_off(a), d, *small)


def collect_kernel(hd, in_ref, *refs):
    out_refs, small_ref = refs[:3], refs[3]
    count = in_ref.shape[0] // 2
    small = jnp.zeros((in_ref.shape[1], in_ref.shape[2] - 3 * hd), exact)
    for head in range(count):
        total = in_ref[head].astype(exact) + in_ref[count + head].astype(exact)
        small += total[:, 3 * hd :]
        for i, out_ref in enumerate(out_refs):
            out_ref[:, head * hd : (head + 1) * hd] = total[:, i * hd : (i + 1) * hd]
    small_ref[...] = small.T


def collect(terms_in, hd):
    block, chunk, size = terms_in.shape
    matrix = jax.ShapeDtypeStruct((chunk, block // 2 * hd), exact)
    return pl.pallas_call(
        functools.partial(collect_kernel, hd),
        out_shape=[matrix] * 3 + [jax.ShapeDtypeStruct((size - 3 * hd, chunk), exact)],
        compiler_params=params(8),
        name="collect",
    )(terms_in)


def collect_hidden_kernel(ff, in_ref, out_ref):
    count = in_ref.shape[0] // 2
    for piece in range(count):
        total = unfold(in_ref[piece].astype(exact) + in_ref[count + piece].astype(exact), ff)
        for slot in range(2):
            at = (slot * count + piece) * (ff // 2)
            out_ref[:, at : at + ff // 2] = total[:, slot * (ff // 2) : (slot + 1) * (ff // 2)]


def collect_hidden(terms_in, ff):
    block, _, size = terms_in.shape
    return pl.pallas_call(
        functools.partial(collect_hidden_kernel, ff),
        out_shape=jax.ShapeDtypeStruct((size * 8 // ff, block // 2 * ff), exact),
        compiler_params=params(8),
        name="collect_hidden",
    )(terms_in)


def attend_kernel(hd, coef, q_ref, k_ref, v_ref, o_ref, e_ref, inverse_ref, vt_ref):
    @pl.when(pl.program_id(0) == 0)
    def _():
        vt_ref[...] = v_ref[...].T

    s = dot(k_ref[...], q_ref[...], 1, 1)
    top = jnp.max(s, axis=0, keepdims=True)
    e = jnp.exp2((s - top) * coef)
    total = jnp.sum(e, axis=0, keepdims=True)
    inverse = 1.0 / total
    e = e.astype(low)
    e_ref[0] = e
    inverse_ref[0] = inverse
    o = (dot(vt_ref[...], e, 1, 0) * inverse).astype(low)
    for piece in range(o_ref.shape[0]):
        o_ref[piece] = o[:hd, piece * lanes : (piece + 1) * lanes]


def attend(q, q_at, k, k_at, v, v_at, hd, rows):
    tokens, keys = q.shape[0], k.shape[0]
    coef = math.log2(math.e) / hd**0.5
    steps = tokens // rows
    return pl.pallas_call(
        functools.partial(attend_kernel, hd, coef),
        grid=(steps,),
        in_specs=[
            pl.BlockSpec((rows, lanes), lambda i: (i, q_at)),
            pl.BlockSpec((keys, lanes), lambda i: (0, k_at)),
            pl.BlockSpec((keys, lanes), lambda i: (0, v_at)),
        ],
        out_specs=[
            pl.BlockSpec((rows // lanes, hd, lanes), lambda i: (i, 0, 0)),
            pl.BlockSpec((1, keys, rows), lambda i: (i, 0, 0)),
            pl.BlockSpec((1, 1, rows), lambda i: (i, 0, 0)),
        ],
        out_shape=[
            jax.ShapeDtypeStruct((tokens // lanes, hd, lanes), low),
            pltpu.HBM((steps, keys, rows), low),
            jax.ShapeDtypeStruct((steps, 1, rows), exact),
        ],
        scratch_shapes=[pltpu.VMEM((lanes, keys), low)],
        compiler_params=params((20 * rows * keys >> 20) + (2 * keys >> 10)),
        cost_estimate=small_cost,
        name="attend",
    )(q, k, v)


def attend_back_kernel(hd, scale, span, q_ref, k_ref, v_ref, do_ref, e_ref, inverse_ref, out_ref, sum_ref, kt_ref, dk_sum, dv_sum):
    step = pl.program_id(0)
    rows = q_ref.shape[0]

    @pl.when(step == 0)
    def _():
        kt_ref[...] = k_ref[...].T
        dk_sum[...] = jnp.zeros_like(dk_sum)
        dv_sum[...] = jnp.zeros_like(dv_sum)
        sum_ref[...] = jnp.zeros_like(sum_ref)

    pieces = do_ref.shape[0]
    dot_t = jnp.concatenate([do_ref[piece] for piece in range(pieces)], axis=1)
    fill = jnp.zeros((lanes - hd, dot_t.shape[1]), low)
    dot_t = jnp.concatenate([dot_t, fill], axis=0)
    q = q_ref[...]
    p = e_ref[0].astype(exact) * inverse_ref[0]
    dp = dot(v_ref[...], dot_t, 1, 0)
    r = jnp.sum(p * dp, axis=0, keepdims=True)
    ds = (p * (dp - r)).astype(low)
    dv_sum[...] += dot(p.astype(low), dot_t.T, 1, 0)
    dk_sum[...] += dot(ds, q, 1, 0)
    dq = dot(kt_ref[...], ds, 1, 0) * scale
    head = lax.broadcasted_iota(jnp.int32, dq.shape, 0) < hd
    dq = jnp.where(head, dq, 0.0).T.astype(low)
    out_ref[pl.ds(pl.multiple_of(span + step * rows, rows), rows), :lanes] = dq.astype(out_ref.dtype)
    sum_ref[0:1, :lanes] += jnp.sum(dq.astype(exact), axis=0, keepdims=True)

    @pl.when(step == pl.num_programs(0) - 1)
    def _():
        head = lax.broadcasted_iota(jnp.int32, dk_sum.shape, 1) < hd
        dk = jnp.where(head, dk_sum[...] * scale, 0.0)
        dv = dv_sum[...].astype(out_ref.dtype)
        dk = dk.astype(out_ref.dtype)
        out_ref[:, lanes : 2 * lanes] = dk
        sum_ref[0:1, lanes : 2 * lanes] = jnp.sum(dk.astype(exact), axis=0, keepdims=True)
        out_ref[:, 2 * lanes :] = dv
        sum_ref[0:1, 2 * lanes :] = jnp.sum(dv.astype(exact), axis=0, keepdims=True)


def attend_back(q, q_at, k, k_at, v, v_at, do, e, inverse, hd, rows, span, kind):
    tokens, keys = q.shape[0], k.shape[0]
    scale = 1.0 / hd**0.5
    steps = tokens // rows
    return pl.pallas_call(
        functools.partial(attend_back_kernel, hd, scale, span),
        grid=(steps,),
        in_specs=[
            pl.BlockSpec((rows, lanes), lambda i: (i, q_at)),
            pl.BlockSpec((keys, lanes), lambda i: (0, k_at)),
            pl.BlockSpec((keys, lanes), lambda i: (0, v_at)),
            pl.BlockSpec((rows // lanes, hd, lanes), lambda i: (i, 0, 0)),
            pl.BlockSpec((1, keys, rows), lambda i: (i, 0, 0)),
            pl.BlockSpec((1, 1, rows), lambda i: (i, 0, 0)),
        ],
        out_specs=[pl.BlockSpec((keys, 3 * lanes), lambda i: (0, 0)), pl.BlockSpec((8, 3 * lanes), lambda i: (0, 0))],
        out_shape=[pltpu.HBM((keys, 3 * lanes), kind), jax.ShapeDtypeStruct((8, 3 * lanes), exact)],
        scratch_shapes=[
            pltpu.VMEM((lanes, keys), low),
            pltpu.VMEM((keys, lanes), exact),
            pltpu.VMEM((keys, lanes), exact),
        ],
        compiler_params=params((24 * rows * keys >> 20) + (6 * keys >> 10)),
        cost_estimate=small_cost,
        name="attend_back",
    )(q, k, v, do, far_off(e), inverse)


def body(
    hidden_in,
    clip_lengths,
    ln1_gain,
    ln1_bias,
    w_query,
    b_query,
    w_key,
    w_value,
    b_value,
    w_out,
    b_out,
    ln2_gain,
    ln2_bias,
    w_fc1,
    b_fc1,
    w_fc2,
    b_fc2,
    cotangent,
):
    micro, rows, width = hidden_in.shape
    at = Layout(micro)
    place = at.place
    hd = width // heads
    own = 2 * rows
    tokens = at.half * own
    clips = clip_lengths.shape[1]
    chunk = width // at.block
    step_rows = 512 if at.blocks == 1 else 256

    vectors = [at.to_block(v) for v in (ln1_gain, ln1_bias, b_query, b_value, b_out, ln2_gain, ln2_bias, b_fc2)]
    ff_bias = at.to_block(b_fc1)
    ff_rows = ff_bias.shape[0]
    first, second = pack(place, hidden_in, jnp.stack(vectors), ff_bias[None])
    blocked = [at.to_block(w) for w in (w_query, w_key, w_value, w_fc1)]
    w_in, w1 = deal(*blocked, hd, at.block)
    ff = blocked[3].shape[1] // heads
    second = at.partner(second)
    wo_shard = at.to_block(w_out)
    g_far = jnp.concatenate([lax.dynamic_index_in_dim(cotangent, 1 - at.mine, 0, False), wo_shard], axis=0)
    second, w_in, w1, g_far = together(second, w_in, w1, g_far)

    x_own, small, *parts = arrange(place, first, second, rows)
    marks = []
    small_far = at.swapped(small, 1)
    parts[2] = jnp.concatenate([parts[2], small[None], small_far[None]], axis=1)
    c1 = small.reshape(2, extra_rows, width)[:, 0, lanes : lanes + ff_rows].reshape(1, 2 * ff_rows).astype(exact)
    w2_shard = at.to_block(w_fc2)
    mine, others, (g_far, *w2_far) = at.gather_tree(parts, [g_far, w2_shard[: ff_rows // 2], w2_shard[ff_rows // 2 :]])
    w2 = jnp.concatenate(at.ordered(w2_shard, jnp.concatenate(w2_far, axis=0)), axis=0)
    g_far, wo_far = g_far[:rows], g_far[rows:]
    wo = jnp.concatenate(at.ordered(wo_shard, wo_far), axis=0)
    *mine, w_in, wo = together(*mine, w_in, wo)
    w_in = at.exchange_block(w_in)
    wo = at.gather_half(wo).reshape(heads, 2, chunk, width).transpose(1, 0, 2, 3).reshape(width, width)
    before = norm(place, False, mine, (), hd, own, chunk)
    a1, table = norm(place, True, others, before, hd, own, chunk)
    w_in, a1, table = together(w_in, a1, table)

    w1 = at.exchange_block(tie(w1, w_in))
    w_in = w_in.reshape(width, 3 * hd)
    g_own = jnp.concatenate(at.ordered(lax.dynamic_index_in_dim(cotangent, at.mine, 0, False), g_far), axis=0)
    g_all = at.gather_half(g_own)

    lengths = lax.dynamic_index_in_dim(clip_lengths, at.mine, 0, False)
    ends = jnp.cumsum(lengths)
    ends = ends - at.me // at.block * tokens

    a1 = a1.reshape(tokens, width)
    qkv, w_pad = project(place, ends, a1, w_in, table, hd, rows)
    span = 0
    qkv_at = (qkv, 0, qkv, 1, qkv, 2)
    if at.blocks > 1:
        span = tokens // 2
        ahead = [(d, d + at.block) for d in range(at.count - at.block)]
        behind = [(d + at.block, d) for d in range(at.count - at.block)]
        nothing = jnp.where(jnp.arange(2 * lanes)[None] == hd + clips, 1.0, 0.0).astype(low)
        kv = qkv[:, lanes:]
        slots = kv.reshape(heads, 2, rows, 2 * lanes)
        before = at.send(slots[:, 1].reshape(span, 2 * lanes), ahead)
        after = at.send(slots[:, 0].reshape(span, 2 * lanes), behind)
        before = jnp.where(at.me < at.block, nothing, before)
        after = jnp.where(at.me >= at.count - at.block, nothing, after)
        kv = jnp.concatenate([before, kv, after], axis=0)
        qkv_at = (qkv, 0, kv, 0, kv, 1)
    o_head, expo, inverse = attend(*qkv_at, hd, step_rows)
    o_head, w1 = together(o_head, w1)
    w1 = unfolded(w1, ff)
    o_own = at.exchange_half(o_head)

    x2, *parts = join(x_own, o_own, wo, table)
    g_split = g_all.reshape(8, 2, own, width)
    mine, others, _ = at.gather_tree(parts)

    *before, kept, sum_c = feed(place, False, mine, g_split, w1, w2, c1, (), own, low)
    hid, du, y, away, sum_c2 = feed(place, True, others, g_split, w1, w2, c1, before, own, low)
    y = lax.psum_scatter(y.reshape(tokens, width), "dev", scatter_dimension=0, tiled=True, axis_index_groups=at.halves)
    marks, made = [], []

    def second_terms(marks):
        made.append(fc2_grad(tie(hid, marks[0]), g_split))
        return made

    def first_terms(marks):
        made.append(fc1_grad(place, mine, others, tie(du, marks[1]), chunk))
        return made[1:]

    kept, got = at.reduce_half(away, kept, marks, {1: second_terms, 2: first_terms})
    back_w2 = at.exchanged(tie(made[0], marks[1]))
    d_w1 = made[1]
    *sums, d_w1 = together(*kept, *got, *back_w2, d_w1)
    kept, got, back_w2 = sums[:3], sums[3:6], sums[6:]

    dx2, ga_own, do_own, sum2 = second_back(kept, got, x2, g_own, table, wo, hd)
    do_head = at.exchange_half(do_own)
    ga = at.gather_half(ga_own).reshape(tokens, width)
    d_w1 = at.exchange_block(tie(d_w1, do_head))

    kind = low if at.blocks == 1 else exact
    dqkv, sum_in = attend_back(*qkv_at, do_head, expo, inverse, hd, step_rows, span, kind)
    if at.blocks > 1:
        dkv = dqkv[:, lanes:]
        to_before = at.send(dkv[:span].astype(low), behind).astype(exact)
        to_after = at.send(dkv[span + tokens :].astype(low), ahead).astype(exact)
        halo = jnp.stack([t.reshape(heads, rows, 2 * lanes) for t in (to_after, to_before)], axis=1)
        dkv = dkv[span : span + tokens] + halo.reshape(tokens, 2 * lanes)
        dqkv = jnp.concatenate([dqkv[span : span + tokens, :lanes], dkv], axis=1).astype(low)
        sum_in = jnp.broadcast_to(jnp.sum(dqkv.astype(exact), axis=0, keepdims=True), (8, 3 * lanes))
    dqkv, sum_in, y = together(dqkv, sum_in, y)
    split = dqkv.reshape(8, 2, own, 3 * lanes)
    away, kept = (terms(place, other, split, w_pad, 1, low) for other in (True, False))
    away, d_w1 = together(away, d_w1)
    marks, made, moved = [], [], []

    def projections(marks):
        made.append(head_grad(place, a1, tie(dqkv, marks[0]), w_in, table, sum2, sum_in, sum_c, sum_c2, hd, chunk, at.block))
        return made

    def output_weight(marks):
        out = (x2 + (tie(y, marks[0]).astype(exact) + table[7])).astype(low)
        moved.extend(at.exchanged(out.reshape(2, rows, width)))
        late, o_late = together(ga, o_head, marks[1])[:2]
        made.append(output_grad(o_late, late.reshape(at.half, own, width)))
        return made[1:] + moved

    kept, got = at.reduce_half(away, kept, marks, {1: projections, 2: output_weight})
    d_in = at.exchange_block(tie(made[0], marks[1]))
    kept_first, d_in = together(kept[0], d_in)
    kept = (kept_first, *kept[1:])

    dx = first_back(kept, got, x_own, dx2, table)
    d_w1, *back_w2 = together(d_w1, *back_w2, dx)[:3]

    input_grad = at.exchanged(dx.reshape(2, rows, width))
    layer_out = moved
    layer_out, input_grad = (jnp.stack(at.ordered(*v)).astype(exact) for v in (layer_out, input_grad))
    back_wo = at.send_rows_back(made[1])
    grad_w2 = at.from_block(back_w2[0].astype(exact) + back_w2[1].astype(exact))
    grad_w1 = at.from_block(collect_hidden(d_w1, ff))
    grad_wo = at.from_block(back_wo[0].astype(exact) + back_wo[1].astype(exact))
    *grads, vec = collect(d_in, hd)
    grad_wq, grad_wk, grad_wv = (at.from_block(v) for v in grads)
    pieces = [at.from_block(vec[i]) for i in range(8)]
    grad_g2, grad_b2, grad_bo, grad_bf2, grad_bq, grad_bv, grad_g1, grad_b1 = pieces
    grad_c1 = at.from_block(vec[8 : 8 + ff_rows // chunk].reshape(ff_rows))
    return (
        layer_out,
        input_grad,
        grad_g1,
        grad_b1,
        grad_wq,
        grad_bq,
        grad_wk,
        grad_wv,
        grad_bv,
        grad_wo,
        grad_bo,
        grad_g2,
        grad_b2,
        grad_w1,
        grad_c1,
        grad_w2,
        grad_bf2,
    )


def solution(mesh):
    tokens, vector, matrix = P(None, "dev", None), P("dev"), P("dev", None)
    grads = (vector, vector, matrix, vector, matrix, matrix, vector, matrix, vector, vector, vector, matrix, vector, matrix, vector)
    return jax.shard_map(
        body,
        mesh=mesh,
        in_specs=(tokens, P()) + grads + (tokens,),
        out_specs=(tokens, tokens) + grads,
        check_vma=False,
    )
```
